32 devices in a mesh: organ: 4 (over x, core), sub: 8 (over z, y).
Axes of the slice: x: 2, y: 2, z: 4, core: 2. Of those that a mesh axis runs over, the one named last changes fastest.
Arguments:
- dual_rhs: float32 [16, 4, 8, 5, 640], P(None, 'organ', 'sub')
- warm_start: float32 [16, 4, 8, 5, 640], P(None, 'organ', 'sub'), may hold values from -4 to 4
- inverse_blocks: float32 [4, 8, 5, 640, 640], P('organ', 'sub'), as said below
- coarse_basis: float32 [6, 4, 8, 5, 640], P(None, 'organ', 'sub')
- mortar_rows: float32 [4, 8, 128, 640], P('organ', 'sub'), may hold values from -0.25 to 0.25
- match_rounds: int32 [4, 8, 5], P('organ', 'sub'), may hold values from 0 to 4, each once within a row
- slave_owner: int32 [4, 8, 128, 1], P('organ', 'sub'), may hold values from 0 to 31; in each aligned block of 128 rows (0 to 127, 128 to 255, ..., all dimensions but the last counted through in order) at most 8 rows name the same one
- slave_dofs: int32 [4, 8, 128], P('organ', 'sub'), may hold values from 0 to 639
- active_set: int32 [4, 8, 128], P('organ', 'sub'), may hold values 0 or 1
- row_counts: int32 [4, 8, 1], P('organ', 'sub'), may hold values from 96 to 128, as said below
Outputs:
- solution: float32 [16, 4, 8, 5, 640], P(None, 'organ', 'sub')
The draws below stay inside these ranges and needn't reach their ends.
Inputs may be any that keep to these rules, and one draw needn't show every extreme that they name: `match_rounds`: each device's row lists every round's face once. `slave_owner`: in the rows of one device no owner is named more than 8 times; in some device one owner is named exactly 8 times. `row_counts`: some device has all 128 rows live. `inverse_blocks`: each face block is symmetric positive definite.
All inputs are finite; a program needn't handle non-finite values. No bound on the sum of `active_set` on one device may be relied on, other than what follows from the above.
Results may differ from the reference program's by a relative error of at most 0.0001.
Values sent between devices are 32-bit elements; how exact they have to be, the bound alone decides.
No kernel may reach another device: no remote copies, remote signals or barrier semaphores. Data moves between devices by JAX's collectives and lax.ppermute only.
A program may use at most 128 MiB of HBM per device.

```python
import math
import jax
import jax.numpy as jnp
import numpy as np
from jax import lax

NB = 640
DIRS = 16
ROUNDS = 5
MODES = 6
ITERS = 3
CAP = 8
BLOCKS = 5
ORGANS = 4
SUBS = 8
MROWS = 128


def draw_inverse_blocks(key, part):
    block_shape = (ORGANS, SUBS, BLOCKS, NB, NB)
    upper_part = jax.random.uniform(jax.random.fold_in(key, 1), block_shape, jnp.float32, -0.04, 0.04)
    positions = jnp.arange(NB)
    above = positions[:, None] < positions[None, :]
    mirrored = jnp.where(above, upper_part, jnp.swapaxes(upper_part, -1, -2))
    diag_vals = jax.random.uniform(jax.random.fold_in(key, 2), (ORGANS, SUBS, BLOCKS, NB), jnp.float32, 2.0, 3.0)
    diagonal_mask = positions[:, None] == positions[None, :]
    matrix = jnp.where(diagonal_mask, diag_vals[..., None], mirrored)
    return matrix


def coarse_and_load(key):
    mode_basis = jax.random.normal(jax.random.fold_in(key, 11), (MODES, ORGANS, SUBS, BLOCKS, NB), jnp.float32)
    weights = jax.random.normal(jax.random.fold_in(key, 12), (DIRS, ORGANS, MODES), jnp.float32) * 0.7
    rough_part = jax.random.normal(jax.random.fold_in(key, 13), (DIRS, ORGANS, SUBS, BLOCKS, NB), jnp.float32)
    loaded = rough_part
    for mode in range(MODES):
        loaded = loaded + weights[:, :, mode][:, :, None, None, None] * mode_basis[mode][None]
    position = jnp.arange(ORGANS * SUBS).reshape(ORGANS, SUBS).astype(jnp.float32)
    spread = 1.0 + 2.0 * position / max(ORGANS * SUBS - 1, 1)
    return (mode_basis, loaded * spread[None, :, :, None, None])


def draw_coarse_basis(key, part):
    return coarse_and_load(key)[0]


def draw_dual_rhs(key, part):
    return coarse_and_load(key)[1]


def draw_row_counts(key, part):
    device_total = ORGANS * SUBS
    counts = jax.random.randint(jax.random.fold_in(key, 21), (device_total,), 3 * MROWS // 4, MROWS + 1)
    full_device = jax.random.randint(jax.random.fold_in(key, 22), (), 0, device_total)
    counts = jnp.where(jnp.arange(device_total) == full_device, MROWS, counts)
    return counts.reshape(ORGANS, SUBS, 1).astype(jnp.int32)


def place_ends(drawn, rng, least, largest):
    longest = drawn.shape.index(max(drawn.shape))
    spots = []
    for shift in (0, 1):
        where = [jax.random.randint(jax.random.fold_in(rng, axis), (), 0, length) for axis, length in enumerate(drawn.shape)]
        where[longest] = (where[longest] + shift) % drawn.shape[longest]
        spots.append(tuple(where))
    return drawn.at[spots[0]].set(least).at[spots[1]].set(largest)


def level_of(key, shape, split, smallest, top_value):
    loudness, own = 1.0, jax.random.fold_in(key, 6)
    for dim, parts in split:
        heights = jnp.exp(jax.random.uniform(jax.random.fold_in(own, dim), (parts,), jnp.float32, smallest / len(split), top_value / len(split)))
        loudness = loudness * jnp.repeat(heights, shape[dim] // parts).reshape([-1 if axis == dim else 1 for axis in range(len(shape))])
    return loudness


def shared_out(rng, own, number, rows, count, top, bound, skew):
    order = jax.random.permutation(rng, count)
    packed, common = load_shares(count, rows * top, bound, skew, True), load_shares(count, rows * top, bound, skew, False)
    places = jnp.arange(count)

    def named(tallies, turn):
        used = int((tallies > 0).sum())
        fixed = max(1, used // 4)
        moved = fixed + (places - fixed + turn * (used - fixed)) % max(1, count - fixed)
        return jnp.zeros((count,), jnp.int32).at[order[jnp.where(places < fixed, places, moved)]].set(jnp.asarray(tallies, jnp.int32))

    tallies = jnp.where(number % 4 == 0, named(packed, number // 4), named(common, number - number // 4 - 1))
    mixed = jax.random.permutation(jax.random.fold_in(own, 3), count)
    donor, taker = mixed[0:count // 2 * 2:2], mixed[1:count // 2 * 2:2]
    margin = jnp.minimum(tallies[donor] - 1, bound - tallies[taker]) // 2
    margin = jnp.where((donor == order[0]) | (taker == order[0]) | (tallies[taker] == 0), 0, jnp.maximum(margin, 0))
    moved = jax.random.randint(jax.random.fold_in(own, 4), (count // 2,), 0, 1 << 20) % (margin + 1)
    tallies = tallies.at[donor].add(-moved).at[taker].add(moved)
    members = jnp.searchsorted(jnp.cumsum(tallies), jnp.arange(rows * top), side="right").astype(jnp.int32)
    grid = members.reshape(top, rows).T
    grid = grid[jax.random.permutation(jax.random.fold_in(own, 1), rows)]
    turn = jax.random.randint(jax.random.fold_in(own, 2), (rows, 1), 0, top)
    return jnp.take_along_axis(grid, (jnp.arange(top)[None, :] + turn) % top, axis=1)


def load_shares(count, total, limit, slope, full):
    loads = [(1 << 20) // math.isqrt(standing ** slope) + 1 for standing in range(1, count + 1)]
    largest = limit if full else min(limit, max(-(-total // count), total * loads[0] // sum(loads)))
    least = 1 if total - largest >= count - 1 else 0
    holding, spare = [largest] + [least] * (count - 1), total - largest - least * (count - 1)
    while spare > 0:
        free = [i for i in range(1, count) if holding[i] < largest] or [i for i in range(1, count) if holding[i] < limit]
        whole, budget = sum([loads[i] for i in free]), spare
        for i in free:
            addition = min(limit - holding[i], max(1, budget * loads[i] // whole), spare)
            holding[i] = holding[i] + addition
            spare = spare - addition
    return np.array(holding)


def centred(rng, dims, width, bound, shards=(), kind=jnp.bfloat16):
    values = width * jax.random.normal(rng, dims, jnp.float32)
    if shards:
        values = values * level_of(rng, dims, shards, -0.22, 0.18)
    return jnp.clip(values, -bound, bound).astype(kind)


def setup_inputs(seed: int = 0) -> dict:
    key_list = jax.random.split(jax.random.key(seed), 11)
    dual_rhs = draw_dual_rhs(jax.random.fold_in(key_list[10], 71), 0)
    warm_start = centred(key_list[1], (DIRS, ORGANS, SUBS, BLOCKS, NB), 0.3, 4.0, ((1, 4), (2, 8)), jnp.float32)
    inverse_blocks = draw_inverse_blocks(jax.random.fold_in(key_list[10], 71), 0)
    coarse_basis = draw_coarse_basis(jax.random.fold_in(key_list[10], 71), 0)
    mortar_rows = centred(key_list[4], (ORGANS, SUBS, MROWS, NB), NB ** -0.5, 0.25, ((0, 4), (1, 8)), jnp.float32)
    match_rounds = jax.vmap(lambda own: jax.random.permutation(own, ROUNDS))(jax.random.split(key_list[5], ORGANS * SUBS)).reshape((ORGANS, SUBS, ROUNDS)).astype(jnp.int32)
    slave_owner_keys = jax.random.split(jax.random.fold_in(key_list[6], 1), ORGANS * SUBS * MROWS // MROWS)
    slave_owner_turns = jax.random.permutation(jax.random.fold_in(key_list[6], 3), ORGANS * SUBS * MROWS // MROWS)
    slave_owner = jax.vmap(lambda own, number: shared_out(jax.random.fold_in(key_list[6], 2), own, number, MROWS, ORGANS * SUBS, 1, CAP, 2))(slave_owner_keys, slave_owner_turns).reshape((ORGANS, SUBS, MROWS, 1))
    slave_dofs = place_ends(jax.random.randint(key_list[7], (ORGANS, SUBS, MROWS), 0, NB), jax.random.fold_in(key_list[7], 1), 0, NB - 1).astype(jnp.int32)
    active_set = place_ends((jax.random.randint(key_list[8], (ORGANS, SUBS, MROWS), 0, 8) < 7).astype(jnp.int32), jax.random.fold_in(key_list[8], 1), 0, 1)
    row_counts = draw_row_counts(jax.random.fold_in(key_list[10], 71), 0)
    return {"dual_rhs": dual_rhs, "warm_start": warm_start, "inverse_blocks": inverse_blocks, "coarse_basis": coarse_basis, "mortar_rows": mortar_rows, "match_rounds": match_rounds, "slave_owner": slave_owner, "slave_dofs": slave_dofs, "active_set": active_set, "row_counts": row_counts}


def apply_jump(field, match_rounds, mortar_rows, flat_index, live_rows):
    result = field
    block_ids = jnp.arange(BLOCKS, dtype=jnp.int32)
    for round_index in range(ROUNDS):
        selector = (match_rounds[:, :, round_index][:, :, None] == block_ids[None, None, :]).astype(jnp.float32)
        face_vals = jnp.sum(selector[None, :, :, :, None] * field, axis=3)
        if round_index < 3:
            partner = jnp.bitwise_xor(jnp.arange(SUBS, dtype=jnp.int32), 1 << round_index)
            remote = face_vals[:, :, partner, :]
        else:
            partner = jnp.bitwise_xor(jnp.arange(ORGANS, dtype=jnp.int32), 1 << round_index - 3)
            remote = face_vals[:, partner, :, :]
        result = result - selector[None, :, :, :, None] * remote[:, :, :, None, :]
    surface = field[:, :, :, 0, :]
    row_vals = jnp.einsum('kosn,osrn->kosr', surface, mortar_rows, precision=lax.Precision.HIGHEST)
    flat_surface = surface.reshape(DIRS, ORGANS * SUBS * NB)
    slave_vals = flat_surface[:, flat_index]
    gap_vals = live_rows[None] * (row_vals - slave_vals)
    master_part = jnp.einsum('kosr,osrn->kosn', gap_vals, mortar_rows, precision=lax.Precision.HIGHEST)
    slave_part = jnp.zeros((DIRS, ORGANS * SUBS * NB), jnp.float32).at[:, flat_index.reshape(-1)].add(gap_vals.reshape(DIRS, -1))
    slave_part = slave_part.reshape(DIRS, ORGANS, SUBS, NB)
    return result.at[:, :, :, 0, :].add(master_part - slave_part)

def reference(dual_rhs, warm_start, inverse_blocks, coarse_basis, mortar_rows, match_rounds, slave_owner, slave_dofs, active_set, row_counts):
    positions = jnp.arange(MROWS, dtype=jnp.int32)
    live_rows = (active_set * (positions[None, None, :] < row_counts).astype(jnp.int32)).astype(jnp.float32)
    flat_index = (slave_owner[:, :, :, 0] * NB + slave_dofs).astype(jnp.int32)

    def jump(field):
        return apply_jump(field, match_rounds, mortar_rows, flat_index, live_rows)

    def operator(field):
        inner = jump(field)
        smoothed = jnp.einsum('kosbn,osbnm->kosbm', inner, inverse_blocks, precision=lax.Precision.HIGHEST)
        return jump(smoothed)
    gram_matrix = jnp.einsum('mosbn,losbn->oml', coarse_basis, coarse_basis, precision=lax.Precision.HIGHEST)
    factors = [jnp.linalg.cholesky(gram_matrix[organ]) for organ in range(ORGANS)]

    def project(resid):
        coeffs = jnp.einsum('kosbn,mosbn->kom', resid, coarse_basis, precision=lax.Precision.HIGHEST)
        solved = jnp.stack([jax.scipy.linalg.cho_solve((factors[organ], True), coeffs[:, organ, :].T).T for organ in range(ORGANS)], axis=1)
        return resid - jnp.einsum('kom,mosbn->kosbn', solved, coarse_basis, precision=lax.Precision.HIGHEST)
    solution = warm_start
    resid = dual_rhs - operator(warm_start)
    projected = project(resid)
    direction = projected
    rho_now = jnp.sum(resid * projected, axis=(1, 2, 3, 4))
    for iteration in range(ITERS):
        image = operator(direction)
        step_size = rho_now / jnp.sum(direction * image, axis=(1, 2, 3, 4))
        solution = solution + step_size[:, None, None, None, None] * direction
        if iteration < ITERS - 1:
            resid = resid - step_size[:, None, None, None, None] * image
            projected = project(resid)
            rho_new = jnp.sum(resid * projected, axis=(1, 2, 3, 4))
            direction = projected + (rho_new / rho_now)[:, None, None, None, None] * direction
            rho_now = rho_new
    return solution
```

```python
import functools

import jax
import jax.numpy as jnp
from jax import lax
from jax.experimental import pallas as pl
from jax.experimental.pallas import tpu as pltpu
from jax.sharding import PartitionSpec as P

ITERS = 3
CAP = 8
SUB_ROUNDS = 3
AXES = ("organ", "sub")
LANES = 128
F32 = jnp.float32
BF16 = jnp.bfloat16
VMEM_LIMIT = 16 * 2**20


def iota(shape, dim):
    return lax.broadcasted_iota(jnp.int32, shape, dim)


def halves(x):
    high = x.astype(BF16)
    return high, (x - high.astype(F32)).astype(BF16)


def thirds(x):
    high = x.astype(BF16)
    rest = x - high.astype(F32)
    middle = rest.astype(BF16)
    return high, middle, (rest - middle.astype(F32)).astype(BF16)


def bdot(a, b):
    return jnp.dot(a, b, preferred_element_type=F32)


def times(x, w_high, w_low):
    rows = x.shape[0]
    a, b, c = thirds(x)
    full = bdot(jnp.concatenate([a, b, c], axis=0), w_high)
    part = bdot(jnp.concatenate([a, b], axis=0), w_low)
    low = full[2 * rows :] + part[rows:]
    return full[:rows] + (full[rows : 2 * rows] + part[:rows] + low)


def times_split(x, w):
    rows = x.shape[0]
    a, b = halves(x)
    w_high, w_low = halves(w)
    full = bdot(jnp.concatenate([a, b], axis=0), w_high)
    return full[:rows] + (full[rows:] + bdot(a, w_low))


def square(x):
    rows, cols = x.shape
    if rows < LANES:
        x = jnp.concatenate([x, jnp.zeros((LANES - rows, cols), F32)], axis=0)
    if cols < LANES:
        x = jnp.concatenate([x, jnp.zeros((x.shape[0], LANES - cols), F32)], axis=1)
    return x.T


def pack(values, ends):
    pieces = [values[:, k * ends : (k + 1) * ends] for k in range(CAP)]
    return square(jnp.concatenate(pieces, axis=0))[:ends]


def unpack(lines, rows):
    ends = lines.shape[0]
    turned = square(lines)
    pieces = [turned[k * rows : (k + 1) * rows, :ends] for k in range(CAP)]
    return jnp.concatenate(pieces, axis=1)


def put(ref, per, line, value):
    ref[pl.ds(line, value.shape[0], stride=per), :] = value


def get(ref, per, line):
    return ref[pl.ds(line, ref.shape[0] // per, stride=per), :]


def to_column(row, base, rows):
    spread = jnp.broadcast_to(row, (rows, LANES))
    here = iota((rows, LANES), 1) == iota((rows, LANES), 0) + base
    return jnp.sum(jnp.where(here, spread, 0.0), axis=1, keepdims=True)


def at_lanes(column, base):
    rows = column.shape[0]
    here = iota((rows, LANES), 1) == iota((rows, LANES), 0) + base
    return jnp.where(here, column, 0.0)


def fold(x):
    return sum(x[:, i : i + LANES] for i in range(0, x.shape[1], LANES))


def dots_row(pairs, base=0):
    total = 0.0
    for place, (left, right) in enumerate(pairs):
        acc = sum(fold(left[f] * right[f]) for f in range(left.shape[0]))
        column = jnp.sum(acc, axis=1, keepdims=True)
        total = total + at_lanes(column, base + place * column.shape[0])
    return jnp.sum(total, axis=0, keepdims=True)


def coefficients_row(field, basis):
    total = 0.0
    blocks, directions = field.shape[0], field.shape[1]
    for m in range(basis.shape[0]):
        acc = sum(fold(field[f] * basis[m, f : f + 1, :]) for f in range(blocks))
        total = total + at_lanes(jnp.sum(acc, axis=1, keepdims=True), m * directions)
    return jnp.sum(total, axis=0, keepdims=True)


def contact(mine, theirs, per_mine, per_theirs, b_high, b_low):
    own = [get(mine, per_mine, i) for i in range(2)]
    other = [get(theirs, per_theirs, i) for i in range(2)]
    gaps = jnp.concatenate([own[0] + other[1], own[1] + other[0]], axis=0)
    directions = LANES // CAP
    return times(unpack(gaps, directions), b_high[...], b_low[...])


def send_contact(message, per, surface, t_high, t_low):
    devices = message.shape[0] // per
    lines = pack(times(surface, t_high[...], t_low[...]), 2 * devices)
    put(message, per, 0, lines[:devices])
    put(message, per, 1, lines[devices:])


def spread_rows(message, per, line, row):
    put(message, per, line, jnp.broadcast_to(row, (message.shape[0] // per, LANES)))


def ranks(owner_row, active_row, count):
    rows = owner_row.shape[1]
    up, across = iota((rows, rows), 0), iota((rows, rows), 1)
    diagonal = up == across

    def column(row):
        return jnp.sum(jnp.where(diagonal, row, 0), axis=1, keepdims=True)

    live_row = jnp.where(iota((1, rows), 1) < count, active_row, 0)
    owner_col, live_col = column(owner_row), column(live_row)
    same = owner_col == owner_row
    rank_col = jnp.sum(jnp.where(same & (across < up), live_row, 0), axis=1, keepdims=True)
    rank_row = jnp.sum(jnp.where(same & (up < across), live_col, 0), axis=0, keepdims=True)
    return column, live_row, live_col, owner_col, rank_row, rank_col


def setup_kernel(count, owner, dofs, active, basis, message):
    devices = message.shape[0]
    rows = owner.shape[1]
    column, live_row, _, _, _, rank_col = ranks(owner[...], active[...], count[0])
    named = (iota((devices, rows), 0) == owner[...]) & (live_row > 0)
    slots = jnp.where(iota((rows, LANES), 1) == rank_col, column(dofs[...]) + 1, 0)
    lines = jnp.dot(
        jnp.where(named, 1.0, 0.0),
        slots.astype(F32),
        precision=lax.Precision.HIGHEST,
        preferred_element_type=F32,
    )
    modes = basis.shape[0]
    lane = iota((1, LANES), 1)
    gram = jnp.zeros((1, LANES), F32)
    for i in range(modes):
        for j in range(i + 1):
            value = jnp.sum(fold(basis[i] * basis[j]), axis=0, keepdims=True)
            value = jnp.sum(value, axis=1, keepdims=True)
            gram = jnp.where(lane == LANES // 2 + 8 * i + j, value, gram)
    message[...] = jnp.where(iota((devices, LANES), 1) < CAP, lines, gram)


def slots_kernel(devices, count, owner, active, mortar, a_high, a_low, t_high, t_low):
    rows = owner.shape[1]
    ends = 2 * devices
    width = CAP * ends
    _, live_row, live_col, owner_col, rank_row, rank_col = ranks(
        owner[...], active[...], count[0]
    )
    slot_row = jnp.where(live_row > 0, rank_row * ends + owner[...], -1)
    slot_col = jnp.where(live_col > 0, rank_col * ends + owner_col, -1)
    pick = jnp.where(iota((width, rows), 0) == slot_row, 1.0, 0.0).astype(BF16)
    pick_t = jnp.where(iota((rows, width), 1) == slot_col, 1.0, 0.0).astype(BF16)
    for part, straight, turned in zip(
        halves(mortar[...]), (a_high, a_low), (t_high, t_low), strict=True
    ):
        straight[...] = bdot(pick, part).astype(BF16)
        turned[...] = bdot(part.astype(F32).T.astype(BF16), pick_t).astype(BF16)


def first_kernel(
    organs,
    matches,
    arrived,
    a_high,
    a_low,
    at_high,
    at_low,
    basis,
    start,
    right,
    message,
    b_high,
    t_high,
    modes_ref,
    *sends,
):
    devices = arrived.shape[0]
    subs = devices // organs
    ends = 2 * devices
    length = basis.shape[2]
    modes, blocks = basis.shape[0], basis.shape[1]
    directions = start.shape[1]
    dofs = arrived[...]
    place = iota((devices, length), 1).astype(F32) + 1.0
    for k in range(CAP):
        base = k * ends
        b_high[base : base + devices, :] = a_high[base : base + devices, :]
        unit = jnp.where(place == dofs[:, k : k + 1], -1.0, 0.0).astype(BF16)
        b_high[base + devices : base + ends, :] = unit
    turned = square(dofs)[:CAP, :devices]
    empty = jnp.zeros((1, devices), F32)
    pieces = []
    for k in range(CAP):
        pieces += [empty, turned[k : k + 1, :]]
    dof_row = jnp.concatenate(pieces, axis=1)
    place_t = iota((length, CAP * ends), 0).astype(F32) + 1.0
    unit_t = jnp.where(place_t == dof_row, -1.0, 0.0).astype(BF16)
    t_high[...] = at_high[...] + unit_t
    mine = lax.axis_index("organ") * subs
    total = jnp.sum(arrived[pl.ds(pl.multiple_of(mine, 8), subs), :], axis=0, keepdims=True)
    lane = iota((1, LANES), 1)

    def entry(i, j):
        here = lane == LANES // 2 + 8 * i + j
        return jnp.sum(jnp.where(here, total, 0.0), axis=1, keepdims=True)

    low, inverse = {}, {}
    for j in range(modes):
        pivot = entry(j, j) - sum(low[j, k] * low[j, k] for k in range(j))
        inverse[j, j] = 1.0 / jnp.sqrt(pivot)
        for i in range(j + 1, modes):
            value = entry(i, j) - sum(low[i, k] * low[j, k] for k in range(j))
            low[i, j] = value * inverse[j, j]
    for j in range(modes):
        for i in range(j + 1, modes):
            value = sum(low[i, k] * inverse[k, j] for k in range(j, i))
            inverse[i, j] = -inverse[i, i] * value
    for i in range(modes):
        modes_ref[i] = sum(inverse[i, j] * basis[j] for j in range(i + 1))
    for r in range(blocks):
        face = matches[r]
        sends[r][0:directions, :] = start[face]
        for m in range(modes):
            sends[r][directions + m : directions + m + 1, :] = modes_ref[m, pl.ds(face, 1), :]
        for m in range(modes, 8):
            sends[r][directions + m : directions + m + 1, :] = jnp.zeros((1, length), F32)
    first = [modes_ref[m, 0:1, :] for m in range(modes)]
    extra = jnp.zeros((2 * 16 - directions - modes, length), F32)
    both = jnp.concatenate([start[0]] + first + [extra], axis=0)
    values = times(both, t_high[...], at_low[...])
    lines = pack(values[:directions], ends)
    put(message, 4, 0, lines[:devices])
    put(message, 4, 1, lines[devices:])
    lines = pack(values[directions : directions + 8], ends)
    half = LANES // 2
    put(message, 4, 2, jnp.concatenate([lines[:devices, :half], lines[devices:, :half]], axis=1))
    spread_rows(message, 4, 3, coefficients_row(right, modes_ref))


def smooth(inner, matrices, smoothed):
    for f in range(inner.shape[0]):
        smoothed[f] = times_split(inner[f], matrices[f])


def jump_faces(matches, field, faces, result):
    rows = field.shape[1]
    for r, face in enumerate(faces):
        result[matches[r]] = field[matches[r]] - face[0:rows, :]


def start_kernel(
    organs, matches, sent, arrived, f0, f1, f2, f3, f4, start, modes_ref, b_high, b_low, t_high,
    t_low, matrices, message, smoothed, jump_modes, s0, s1, s2, s3, s4, inner,
):
    faces = (f0, f1, f2, f3, f4)
    devices = sent.shape[0] // 4
    subs = devices // organs
    directions = start.shape[1]
    modes, blocks = modes_ref.shape[0], modes_ref.shape[1]
    jump_faces(matches, start, faces, inner)
    inner[0] += contact(sent, arrived, 4, 4, b_high, b_low)
    smooth(inner, matrices, smoothed)
    send_contact(message, 2, smoothed[0], t_high, t_low)
    for r, out in enumerate((s0, s1, s2, s3, s4)):
        out[...] = smoothed[matches[r]]
    organ = lax.axis_index("organ")
    jump_modes[...] = jnp.zeros(jump_modes.shape, F32)
    for r in range(blocks):
        face = matches[r]
        for m in range(modes):
            own = modes_ref[m, pl.ds(face, 1), :]
            other = faces[r][directions + m : directions + m + 1, :]
            if r < SUB_ROUNDS:
                own = own - other
            else:
                partner = organ ^ (1 << (r - SUB_ROUNDS))
                jump_modes[face, pl.ds(m * organs + partner, 1), :] = -other
            jump_modes[face, pl.ds(m * organs + organ, 1), :] = own
    mine = get(sent, 4, 2)
    other = get(arrived, 4, 2)
    half = LANES // 2

    def lines(x):
        return jnp.concatenate([x[:, :half], x[:, half:]], axis=0)

    def swapped(x):
        return jnp.concatenate([x[:, half:], x[:, :half]], axis=0)

    own_rows = unpack(lines(mine), 8)
    other_rows = unpack(swapped(other), 8)
    source = lax.rem(iota(other_rows.shape, 1), devices) // subs
    stack = []
    for o in range(organs):
        owns = jnp.where(organ == o, 1.0, 0.0)
        stack.append(jnp.where(source == o, other_rows, 0.0) + owns * own_rows)
    added = times(jnp.concatenate(stack, axis=0), b_high[...], b_low[...])
    for o in range(organs):
        for m in range(modes):
            row = pl.ds(m * organs + o, 1)
            jump_modes[0, row, :] = jump_modes[0, row, :] + added[8 * o + m : 8 * o + m + 1]


def subtract_modes(field, columns, basis, f):
    value = field
    for m, column in enumerate(columns):
        value = value - column * basis[m, f : f + 1, :]
    return value


def residual_kernel(
    organs, matches, sent, arrived, first, f0, f1, f2, f3, f4, smoothed, right, modes_ref, b_high,
    b_low, t_high, t_low, message, resid, s0, s1, s2, s3, s4, image,
):
    devices = sent.shape[0] // 2
    subs = devices // organs
    blocks, directions = right.shape[0], right.shape[1]
    jump_faces(matches, smoothed, (f0, f1, f2, f3, f4), image)
    image[0] += contact(sent, arrived, 2, 2, b_high, b_low)
    mine = pl.multiple_of(lax.axis_index("organ") * subs * 4, 8)
    block = first[pl.ds(mine, subs * 4), :]
    here = lax.rem(iota(block.shape, 0), 4) == 3
    row = jnp.sum(jnp.where(here, block, 0.0), axis=0, keepdims=True)
    columns = [to_column(row, m * directions, directions) for m in range(modes_ref.shape[0])]
    for f in range(blocks):
        resid[f] = subtract_modes(right[f], columns, modes_ref, f) - image[f]
    send_residual(matches, resid, modes_ref, t_high, t_low, message, (s0, s1, s2, s3, s4))


def send_residual(matches, resid, modes_ref, t_high, t_low, message, sends):
    for r, out in enumerate(sends):
        out[...] = resid[matches[r]]
    send_contact(message, 3, resid[0], t_high, t_low)
    spread_rows(message, 3, 2, coefficients_row(resid, modes_ref))


def inner_kernel(organs, last, older, matches, *refs):
    sent, arrived, f0, f1, f2, f3, f4, resid, modes_ref, jump_modes = refs[:10]
    b_high, b_low, t_high, t_low, matrices = refs[10:15]
    rest = list(refs[15:])
    previous = rest.pop(0) if older else None
    message, projected, inner = rest[:3]
    smoothed = rest[3]
    sends = rest[4:]
    devices = sent.shape[0] // 3
    subs = devices // organs
    blocks, directions = resid.shape[0], resid.shape[1]
    modes = modes_ref.shape[0]
    parts = get(arrived, 3, 2)
    sums = [
        jnp.sum(parts[o * subs : (o + 1) * subs], axis=0, keepdims=True) for o in range(organs)
    ]
    organ = lax.axis_index("organ")
    own = sum(jnp.where(organ == o, 1.0, 0.0) * sums[o] for o in range(organs))
    columns = [to_column(own, m * directions, directions) for m in range(modes)]
    for f in range(blocks):
        projected[f] = subtract_modes(resid[f], columns, modes_ref, f)
    turned = square(jnp.concatenate(sums, axis=0))
    left = jnp.concatenate(
        [turned[m * directions : (m + 1) * directions, :organs] for m in range(8)], axis=1
    )
    jump_faces(matches, resid, (f0, f1, f2, f3, f4), inner)
    inner[0] += contact(sent, arrived, 3, 3, b_high, b_low)
    for f in range(blocks):
        inner[f] = inner[f] - times_split(left, jump_modes[f])
    smooth(inner, matrices, smoothed)
    pairs = [(projected, projected), (inner, smoothed)]
    if older:
        pairs.append((previous, smoothed))
    row = dots_row(pairs)
    if last:
        message[...] = jnp.broadcast_to(row, message.shape)
        return
    for r, out in enumerate(sends):
        out[...] = smoothed[matches[r]]
    send_contact(message, 3, smoothed[0], t_high, t_low)
    spread_rows(message, 3, 2, row)


def step_sizes(row, older, scalars, directions):
    rho = to_column(row, 0, directions)
    curvature = to_column(row, directions, directions)
    if not older:
        return rho, None, curvature, rho / curvature
    cross = to_column(row, 2 * directions, directions)
    beta = rho / scalars[0, :, 0:1]
    curvature = curvature + beta * (2.0 * cross + beta * scalars[1, :, 0:1])
    return rho, beta, curvature, rho / curvature


def outer_kernel(older, matches, *refs):
    sent, arrived, f0, f1, f2, f3, f4, projected, inner, smoothed, total, modes_ref = refs[:12]
    b_high, b_low, t_high, t_low = refs[12:16]
    rest = list(refs[16:])
    old_direction = old_inner = old_image = scalars = None
    if older:
        old_direction, old_inner, old_image, scalars = rest[:4]
        rest = rest[4:]
    message, resid, new_total, new_scalars, image = rest[:5]
    rest = rest[5:]
    if older:
        direction, new_inner = rest[:2]
        rest = rest[2:]
    blocks, directions = projected.shape[0], projected.shape[1]
    row = jnp.sum(get(arrived, 3, 2), axis=0, keepdims=True)
    rho, beta, curvature, step = step_sizes(row, older, scalars, directions)
    new_scalars[0] = jnp.broadcast_to(rho, (directions, LANES))
    new_scalars[1] = jnp.broadcast_to(curvature, (directions, LANES))
    jump_faces(matches, smoothed, (f0, f1, f2, f3, f4), image)
    image[0] += contact(sent, arrived, 3, 3, b_high, b_low)
    for f in range(blocks):
        if older:
            image[f] = image[f] + beta * old_image[f]
            direction[f] = projected[f] + beta * old_direction[f]
            new_inner[f] = inner[f] + beta * old_inner[f]
            new_total[f] = total[f] + step * direction[f]
        else:
            new_total[f] = total[f] + step * projected[f]
        resid[f] = projected[f] - step * image[f]
    send_residual(matches, resid, modes_ref, t_high, t_low, message, rest)


def last_kernel(arrived, projected, old_direction, total, scalars, out):
    blocks, directions = projected.shape[0], projected.shape[1]
    row = jnp.sum(arrived[...], axis=0, keepdims=True)
    _, beta, _, step = step_sizes(row, True, scalars, directions)
    for f in range(blocks):
        out[:, f, :] = total[f] + step * (projected[f] + beta * old_direction[f])


def call(kernel, outs, args, smem=0, scratch=(), cost=1_000_000):
    in_specs = [pl.BlockSpec(memory_space=pltpu.SMEM)] * smem
    in_specs += [pl.BlockSpec(memory_space=pltpu.VMEM)] * (len(args) - smem)
    return pl.pallas_call(
        kernel,
        out_shape=[jax.ShapeDtypeStruct(shape, kind) for shape, kind in outs],
        in_specs=in_specs,
        out_specs=[pl.BlockSpec(memory_space=pltpu.VMEM)] * len(outs),
        scratch_shapes=list(scratch),
        compiler_params=pltpu.CompilerParams(vmem_limit_bytes=VMEM_LIMIT),
        cost_estimate=pl.CostEstimate(flops=cost, bytes_accessed=cost, transcendentals=0),
    )(*args)


def from_partner(value, axis, apart):
    mask = 2**apart
    pairs = [(source, source ^ mask) for source in range(lax.axis_size(axis))]
    return lax.ppermute(value, axis, pairs)


def exchange(message):
    return lax.all_to_all(message, AXES, split_axis=0, concat_axis=0, tiled=True)


def swap_faces(faces):
    swapped = []
    for r, face in enumerate(faces):
        axis, apart = ("sub", r) if r < SUB_ROUNDS else ("organ", r - SUB_ROUNDS)
        swapped.append(from_partner(face, axis, apart))
    return swapped


def local(
    dual_rhs, warm_start, inverse_blocks, coarse_basis, mortar_rows, match_rounds, slave_owner,
    slave_dofs, active_set, row_counts,
):
    directions, blocks, length = dual_rhs.shape[0], dual_rhs.shape[3], dual_rhs.shape[4]
    rows = mortar_rows.shape[2]
    modes = coarse_basis.shape[0]
    organs, subs = lax.axis_size("organ"), lax.axis_size("sub")
    devices = organs * subs
    width = CAP * 2 * devices
    field = (blocks, directions, length)
    right = dual_rhs.reshape(directions, blocks, length).transpose(1, 0, 2)
    start = warm_start.reshape(directions, blocks, length).transpose(1, 0, 2)
    matrices = inverse_blocks.reshape(blocks, length, length)
    basis = coarse_basis.reshape(modes, blocks, length)
    mortar = mortar_rows.reshape(rows, length)
    matches = match_rounds.reshape(-1)
    owner = slave_owner.reshape(1, rows)
    dofs = slave_dofs.reshape(1, rows)
    active = active_set.reshape(1, rows)
    count = row_counts.reshape(1)
    face = ((directions, length), F32)
    whole = (field, F32)

    (setup,) = call(
        setup_kernel, [((devices, LANES), F32)], (count, owner, dofs, active, basis), smem=1
    )
    arrived = exchange(setup)
    a_high, a_low, at_high, t_low = call(
        functools.partial(slots_kernel, devices),
        [((width, length), BF16)] * 2 + [((length, width), BF16)] * 2,
        (count, owner, active, mortar),
        smem=1,
    )
    b_low = a_low

    sent, b_high, t_high, modes_ref, *faces = call(
        functools.partial(first_kernel, organs),
        [
            ((4 * devices, LANES), F32),
            ((width, length), BF16),
            ((length, width), BF16),
            ((modes, blocks, length), F32),
        ]
        + [((directions + 8, length), F32)] * blocks,
        (matches, arrived, a_high, a_low, at_high, t_low, basis, start, right),
        smem=1,
    )
    maps = (b_high, b_low, t_high, t_low)
    first = exchange(sent)
    faces = swap_faces(faces)

    message, smoothed, jump_modes, *sends = call(
        functools.partial(start_kernel, organs),
        [((2 * devices, LANES), F32), whole, ((blocks, 8 * organs, length), F32)]
        + [face] * blocks,
        (matches, sent, first, *faces, start, modes_ref, *maps, matrices),
        smem=1,
        scratch=[pltpu.VMEM(field, F32)],
    )
    arrived = exchange(message)
    faces = swap_faces(sends)

    sent, resid, *sends = call(
        functools.partial(residual_kernel, organs),
        [((3 * devices, LANES), F32), whole] + [face] * blocks,
        (matches, message, arrived, first, *faces, smoothed, right, modes_ref, *maps),
        smem=1,
        scratch=[pltpu.VMEM(field, F32)],
    )
    total = start
    direction = inner = image = scalars = None
    for step in range(ITERS):
        older, last = step > 0, step == ITERS - 1
        arrived = exchange(sent)
        faces = swap_faces(sends)
        previous = (inner,) if older else ()
        lines = devices if last else 3 * devices
        message, projected, new_inner, smoothed, *sends = call(
            functools.partial(inner_kernel, organs, last, older),
            [((lines, LANES), F32), whole, whole, whole] + ([] if last else [face] * blocks),
            (matches, sent, arrived, *faces, resid, modes_ref, jump_modes, *maps, matrices)
            + previous,
            smem=1,
        )
        arrived = exchange(message)
        if last:
            break
        faces = swap_faces(sends)
        old = (direction, inner, image, scalars) if older else ()
        sent, resid, total, scalars, image, *more = call(
            functools.partial(outer_kernel, older),
            [((3 * devices, LANES), F32), whole, whole, ((2, directions, LANES), F32), whole]
            + ([whole] * 2 if older else [])
            + [face] * blocks,
            (matches, message, arrived, *faces, projected, new_inner, smoothed, total, modes_ref)
            + maps
            + old,
            smem=1,
        )
        if older:
            direction, inner, *sends = more
        else:
            direction, inner, sends = projected, new_inner, more
    (result,) = call(
        last_kernel,
        [((directions, blocks, length), F32)],
        (arrived, projected, direction, total, scalars),
    )
    return result.reshape(dual_rhs.shape)


def solution(mesh):
    in_specs = (
        P(None, "organ", "sub", None, None),
        P(None, "organ", "sub", None, None),
        P("organ", "sub", None, None, None),
        P(None, "organ", "sub", None, None),
        P("organ", "sub", None, None),
        P("organ", "sub", None),
        P("organ", "sub", None, None),
        P("organ", "sub", None),
        P("organ", "sub", None),
        P("organ", "sub", None),
    )
    out_specs = P(None, "organ", "sub", None, None)
    return jax.shard_map(local, mesh=mesh, in_specs=in_specs, out_specs=out_specs, check_vma=False)
```

```python
import functools

import jax
import jax.numpy as jnp
from jax import lax
from jax.experimental import pallas as pl
from jax.experimental.pallas import tpu as pltpu
from jax.sharding import PartitionSpec as P

ITERS = 3
CAP = 8
SUB_ROUNDS = 3
ORDER = (2, 0, 1, 4, 3)
NEAR = 3
AXES = ("organ", "sub")
LANES = 128
F32 = jnp.float32
BF16 = jnp.bfloat16
VMEM_LIMIT = 24 * 2**20
COST = 2_000_000


def iota(shape, dim):
    return lax.broadcasted_iota(jnp.int32, shape, dim)


def halves(x):
    high = x.astype(BF16)
    return high, (x - high.astype(F32)).astype(BF16)


def thirds(x):
    high = x.astype(BF16)
    rest = x - high.astype(F32)
    middle = rest.astype(BF16)
    return high, middle, (rest - middle.astype(F32)).astype(BF16)


def bdot(a, b):
    return jnp.dot(a, b, preferred_element_type=F32)


def times(x, w_high, w_low):
    rows = x.shape[0]
    a, b, c = thirds(x)
    full = bdot(jnp.concatenate([a, b, c], axis=0), w_high)
    part = bdot(jnp.concatenate([a, b], axis=0), w_low)
    low = full[2 * rows :] + part[rows:]
    return full[:rows] + (full[rows : 2 * rows] + part[:rows] + low)


def times_split(x, w):
    rows = x.shape[0]
    a, b = halves(x)
    w_high, w_low = halves(w)
    full = bdot(jnp.concatenate([a, b], axis=0), w_high)
    return full[:rows] + (full[rows:] + bdot(a, w_low))


def square(x):
    rows, cols = x.shape
    if rows < LANES:
        x = jnp.concatenate([x, jnp.zeros((LANES - rows, cols), F32)], axis=0)
    if cols < LANES:
        x = jnp.concatenate([x, jnp.zeros((x.shape[0], LANES - cols), F32)], axis=1)
    return x.T


def pack(master, slave, devices):
    def stacked(x):
        pieces = [x[:, k * devices : (k + 1) * devices] for k in range(CAP)]
        return jnp.concatenate(pieces, axis=0)

    turned = square(jnp.concatenate([stacked(master), stacked(slave)], axis=1))
    return turned[:devices], turned[devices : 2 * devices]


def unpack(master, slave, rows):
    devices = master.shape[0]
    turned = square(jnp.concatenate([master, slave], axis=0))

    def laid(first):
        pieces = [
            turned[k * rows : (k + 1) * rows, first : first + devices] for k in range(CAP)
        ]
        return jnp.concatenate(pieces, axis=1)

    return laid(0), laid(devices)


def put(ref, per, line, value):
    ref[pl.ds(line, value.shape[0], stride=per), :] = value


def get(ref, per, line):
    return ref[pl.ds(line, ref.shape[0] // per, stride=per), :]


def to_column(row, base, rows):
    spread = jnp.broadcast_to(row, (rows, LANES))
    here = iota((rows, LANES), 1) == iota((rows, LANES), 0) + base
    return jnp.sum(jnp.where(here, spread, 0.0), axis=1, keepdims=True)


def at_lanes(column, base):
    rows = column.shape[0]
    here = iota((rows, LANES), 1) == iota((rows, LANES), 0) + base
    return jnp.where(here, column, 0.0)


def fold(x):
    return sum(x[:, i : i + LANES] for i in range(0, x.shape[1], LANES))


def dots_row(pairs, base=0):
    total = 0.0
    for place, (left, right) in enumerate(pairs):
        acc = sum(fold(left[f] * right[f]) for f in range(left.shape[0]))
        column = jnp.sum(acc, axis=1, keepdims=True)
        total = total + at_lanes(column, base + place * column.shape[0])
    return jnp.sum(total, axis=0, keepdims=True)


def coefficients_row(field, basis):
    total = 0.0
    blocks, directions = field.shape[0], field.shape[1]
    for m in range(basis.shape[0]):
        acc = sum(fold(field[f] * basis[m, f : f + 1, :]) for f in range(blocks))
        total = total + at_lanes(jnp.sum(acc, axis=1, keepdims=True), m * directions)
    return jnp.sum(total, axis=0, keepdims=True)


def exact(x, unit):
    rows = x.shape[0]
    full = bdot(jnp.concatenate(thirds(x), axis=0), unit)
    return full[:rows] + (full[rows : 2 * rows] + full[2 * rows :])


def contact(mine, theirs, per_mine, per_theirs, a_high, a_low, unit):
    own = [get(mine, per_mine, i) for i in range(2)]
    other = [get(theirs, per_theirs, i) for i in range(2)]
    master, slave = unpack(own[0] + other[1], own[1] + other[0], LANES // CAP)
    return times(master, a_high[...], a_low[...]) + exact(slave, unit[...])


def send_contact(message, per, surface, t_high, t_low, unit_t):
    devices = message.shape[0] // per
    master = times(surface, t_high[...], t_low[...])
    slave = exact(surface, unit_t[...])
    for line, value in enumerate(pack(master, slave, devices)):
        put(message, per, line, value)


def spread_rows(message, per, line, row):
    put(message, per, line, jnp.broadcast_to(row, (message.shape[0] // per, LANES)))


def ranks(owner_row, active_row, count):
    rows = owner_row.shape[1]
    up, across = iota((rows, rows), 0), iota((rows, rows), 1)
    diagonal = up == across

    def column(row):
        return jnp.sum(jnp.where(diagonal, row, 0), axis=1, keepdims=True)

    live_row = jnp.where(iota((1, rows), 1) < count, active_row, 0)
    owner_col, live_col = column(owner_row), column(live_row)
    same = owner_col == owner_row
    rank_col = jnp.sum(jnp.where(same & (across < up), live_row, 0), axis=1, keepdims=True)
    rank_row = jnp.sum(jnp.where(same & (up < across), live_col, 0), axis=0, keepdims=True)
    return column, live_row, live_col, owner_col, rank_row, rank_col


def load_modes(basis, modes, blocks):
    return [
        jnp.concatenate([basis[m * blocks + f] for f in range(blocks)], axis=0)
        for m in range(modes)
    ]


def setup_kernel(blocks, count, owner, dofs, active, basis, message):
    devices = message.ref.shape[0]
    rows = owner.shape[1]
    column, live_row, _, _, _, rank_col = ranks(owner[...], active[...], count[0])
    named = (iota((devices, rows), 0) == owner[...]) & (live_row > 0)
    slots = jnp.where(iota((rows, LANES), 1) == rank_col, column(dofs[...]) + 1, 0)
    lines = jnp.dot(
        jnp.where(named, 1.0, 0.0),
        slots.astype(F32),
        precision=lax.Precision.HIGHEST,
        preferred_element_type=F32,
    )
    modes = basis.shape[0] // blocks
    slabs = load_modes(basis, modes, blocks)
    lane = iota((1, LANES), 1)
    gram = jnp.zeros((1, LANES), F32)
    for i in range(modes):
        for j in range(i + 1):
            value = jnp.sum(fold(slabs[i] * slabs[j]), axis=0, keepdims=True)
            value = jnp.sum(value, axis=1, keepdims=True)
            gram = jnp.where(lane == LANES // 2 + 8 * i + j, value, gram)
    message.ref[...] = jnp.where(iota((devices, LANES), 1) < CAP, lines, gram)


def slots_kernel(
    devices, count, owner, active, mortar, start_rows, right_rows, a_high, a_low, t_high, t_low,
    start, right,
):
    rows = owner.shape[1]
    width = CAP * devices
    _, live_row, live_col, owner_col, rank_row, rank_col = ranks(
        owner[...], active[...], count[0]
    )
    slot_row = jnp.where(live_row > 0, rank_row * devices + owner[...], -1)
    slot_col = jnp.where(live_col > 0, rank_col * devices + owner_col, -1)
    pick = jnp.where(iota((width, rows), 0) == slot_row, 1.0, 0.0).astype(BF16)
    pick_t = jnp.where(iota((rows, width), 1) == slot_col, 1.0, 0.0).astype(BF16)
    blocks, directions = start.ref.shape[0], start.ref.shape[1]
    for source, target in ((start_rows(), start), (right_rows(), right)):
        for f in range(blocks):
            for c in range(directions):
                target.ref[f, c : c + 1, :] = source[c * blocks + f]
        target.flush()
    for part, straight, turned in zip(
        halves(mortar()[...]), (a_high, a_low), (t_high, t_low), strict=True
    ):
        straight.ref[...] = bdot(pick, part).astype(BF16)
        straight.flush()
        turned.ref[...] = bdot(part.astype(F32).T.astype(BF16), pick_t).astype(BF16)
        turned.flush()


def first_kernel(
    organs, matches, arrived, basis, start, t_high, t_low, right, message, unit_t, unit,
    modes_out, *sends,
):
    devices = arrived.shape[0]
    subs = devices // organs
    blocks = len(sends)
    modes = basis.shape[0] // blocks
    length = basis.shape[2]
    dofs = arrived[...]
    turned = square(dofs)[:CAP, :devices]
    dof_row = jnp.concatenate([turned[k : k + 1, :] for k in range(CAP)], axis=1)
    place_t = iota((length, CAP * devices), 0).astype(F32) + 1.0
    unit_t.ref[...] = jnp.where(place_t == dof_row, -1.0, 0.0).astype(BF16)
    unit_t.flush()
    mine = lax.axis_index("organ") * subs
    total = jnp.sum(arrived[pl.ds(pl.multiple_of(mine, 8), subs), :], axis=0, keepdims=True)
    lane = iota((1, LANES), 1)

    def entry(i, j):
        here = lane == LANES // 2 + 8 * i + j
        return jnp.sum(jnp.where(here, total, 0.0), axis=1, keepdims=True)

    low, inverse = {}, {}
    for j in range(modes):
        pivot = entry(j, j) - sum(low[j, k] * low[j, k] for k in range(j))
        inverse[j, j] = 1.0 / jnp.sqrt(pivot)
        for i in range(j + 1, modes):
            value = entry(i, j) - sum(low[i, k] * low[j, k] for k in range(j))
            low[i, j] = value * inverse[j, j]
    for j in range(modes):
        for i in range(j + 1, modes):
            value = sum(low[i, k] * inverse[k, j] for k in range(j, i))
            inverse[i, j] = -inverse[i, i] * value
    slabs = load_modes(basis, modes, blocks)
    modes_ref = modes_out.ref
    for i in range(modes):
        modes_ref[i] = sum(inverse[i, j] * slabs[j] for j in range(i + 1))
    modes_out.flush()
    start = start()
    directions = start.shape[1]
    for r in range(blocks):
        face = matches[r]
        send = sends[r].ref
        send[0:directions, :] = start[face]
        for m in range(modes):
            send[directions + m : directions + m + 1, :] = modes_ref[m, pl.ds(face, 1), :]
        for m in range(modes, 8):
            send[directions + m : directions + m + 1, :] = jnp.zeros((1, length), F32)
        sends[r].flush()
    first = [modes_ref[m, 0:1, :] for m in range(modes)]
    extra = jnp.zeros((2 * 16 - directions - modes, length), F32)
    both = jnp.concatenate([start[0]] + first + [extra], axis=0)
    master = times(both, t_high()[...], t_low()[...])
    slave = exact(both, unit_t.ref[...])
    for line, value in enumerate(pack(master[:directions], slave[:directions], devices)):
        put(message.ref, 4, line, value)
    rows = slice(directions, directions + 8)
    lines = pack(master[rows], slave[rows], devices)
    half = LANES // 2
    put(message.ref, 4, 2, jnp.concatenate([line[:, :half] for line in lines], axis=1))
    spread_rows(message.ref, 4, 3, coefficients_row(right(), modes_ref))
    message.flush()
    place = iota((devices, length), 1).astype(F32) + 1.0
    for k in range(CAP):
        block = jnp.where(place == dofs[:, k : k + 1], -1.0, 0.0).astype(BF16)
        unit.ref[k * devices : (k + 1) * devices, :] = block


def smooth(inner, near, far, smoothed, f):
    early = near.shape[0]
    matrix = near[f] if f < early else far(f - early)[...]
    smoothed[f] = times_split(inner[f], matrix)


def fetch(matrices, near, sems):
    copies = [
        pltpu.make_async_copy(matrices.at[f], near.at[f], sems.at[f])
        for f in range(near.shape[0])
    ]
    for copy in copies:
        copy.start()
    return copies


def subtract_modes(field, columns, basis, f):
    value = field
    for m, column in enumerate(columns):
        value = value - column * basis[m, f : f + 1, :]
    return value


def start_contact(
    organs, arrived, sent, start, a_high, a_low, unit, modes_ref, right, matrices, new_right,
    base, added, near, sems,
):
    sent, start, maps = sent(), start(), (a_high(), a_low(), unit())
    copies = fetch(matrices, near, sems)
    devices = sent.shape[0] // 4
    subs = devices // organs
    blocks, directions = start.shape[0], start.shape[1]
    base[...] = start[...]
    base[0] += contact(sent, arrived, 4, 4, *maps)
    modes_ref, right = modes_ref(), right()
    organ = lax.axis_index("organ")
    block = arrived[pl.ds(pl.multiple_of(organ * subs * 4, 8), subs * 4), :]
    here = lax.rem(iota(block.shape, 0), 4) == 3
    row = jnp.sum(jnp.where(here, block, 0.0), axis=0, keepdims=True)
    columns = [to_column(row, m * directions, directions) for m in range(modes_ref.shape[0])]
    for f in range(blocks):
        new_right.ref[f] = subtract_modes(right[f], columns, modes_ref, f)
    new_right.flush()
    half = LANES // 2
    mine, other = get(sent, 4, 2), get(arrived, 4, 2)
    own_rows = unpack(mine[:, :half], mine[:, half:], 8)
    other_rows = unpack(other[:, half:], other[:, :half], 8)
    source = lax.rem(iota(own_rows[0].shape, 1), devices) // subs
    stacks = []
    for own_half, other_half in zip(own_rows, other_rows, strict=True):
        stack = []
        for o in range(organs):
            owns = jnp.where(organ == o, 1.0, 0.0)
            stack.append(jnp.where(source == o, other_half, 0.0) + owns * own_half)
        stacks.append(jnp.concatenate(stack, axis=0))
    added[...] = times(stacks[0], maps[0][...], maps[1][...]) + exact(stacks[1], maps[2][...])
    for copy in copies:
        copy.wait()


def start_kernel(
    organs, matches, f0, f1, f2, f3, f4, base, added, near, t_high, t_low, unit_t, modes_ref, far,
    message, smoothed_out, jump_out, s0, s1, s2, s3, s4, inner,
):
    faces = (f0, f1, f2, f3, f4)
    smoothed = smoothed_out.ref
    blocks, directions = base.shape[0], base.shape[1]
    for r, face in zip(ORDER, faces, strict=True):
        inner[matches[r]] = base[matches[r]] - face[0:directions, :]
    for f in range(blocks):
        smooth(inner, near, far, smoothed, f)
    for r, send in enumerate((s0, s1, s2, s3, s4)):
        send(smoothed.at[matches[r]])
    smoothed_out.flush()
    send_contact(message.ref, 2, smoothed[0], t_high(), t_low(), unit_t())
    message.flush()
    modes_ref = modes_ref()
    modes = modes_ref.shape[0]
    jump_modes = jump_out.ref
    organ = lax.axis_index("organ")
    jump_modes[...] = jnp.zeros(jump_modes.shape, F32)
    for r, values in zip(ORDER, faces, strict=True):
        face = matches[r]
        for m in range(modes):
            own = modes_ref[m, pl.ds(face, 1), :]
            other = values[directions + m : directions + m + 1, :]
            if r < SUB_ROUNDS:
                own = own - other
            else:
                partner = organ ^ (1 << (r - SUB_ROUNDS))
                jump_modes[face, pl.ds(m * organs + partner, 1), :] = -other
            jump_modes[face, pl.ds(m * organs + organ, 1), :] = own
    for o in range(organs):
        for m in range(modes):
            row = pl.ds(m * organs + o, 1)
            jump_modes[0, row, :] = jump_modes[0, row, :] + added[8 * o + m : 8 * o + m + 1, :]


def residual_contact(arrived, sent, smoothed, a_high, a_low, unit, right, part):
    sent, smoothed, right = sent(), smoothed(), right()
    part[...] = right[...] - smoothed[...]
    part[0] -= contact(sent, arrived, 2, 2, a_high(), a_low(), unit())


def residual_kernel(
    matches, f0, f1, f2, f3, f4, part, t_high, t_low, unit_t, modes_ref, message, resid, *sends
):
    for r, face in zip(ORDER, (f0, f1, f2, f3, f4), strict=True):
        resid.ref[matches[r]] = part[matches[r]] + face[...]
    send_residual(matches, resid, modes_ref, (t_high, t_low, unit_t), message, sends)


def send_residual(matches, resid, modes_ref, maps, message, sends):
    for r, send in enumerate(sends):
        send(resid.ref.at[matches[r]])
    resid.flush()
    send_contact(message.ref, 4, resid.ref[0], *(late() for late in maps))
    spread_rows(message.ref, 4, 2, coefficients_row(resid.ref, modes_ref()))
    message.flush()


def inner_contact(
    organs, arrived, sent, resid, a_high, a_low, unit, modes_ref, jump_modes, matrices,
    projected_out, base, near, norms, sems,
):
    sent, resid, maps = sent(), resid(), (a_high(), a_low(), unit())
    modes_ref, jump_modes = modes_ref(), jump_modes()
    copies = fetch(matrices, near, sems)
    devices = sent.shape[0] // 4
    subs = devices // organs
    blocks, directions = resid.shape[0], resid.shape[1]
    parts = get(arrived, 4, 2)
    sums = [
        jnp.sum(parts[o * subs : (o + 1) * subs], axis=0, keepdims=True) for o in range(organs)
    ]
    added = contact(sent, arrived, 4, 4, *maps)
    turned = square(jnp.concatenate(sums, axis=0))
    left = jnp.concatenate(
        [turned[m * directions : (m + 1) * directions, :organs] for m in range(8)], axis=1
    )
    organ = lax.axis_index("organ")
    own = sum(jnp.where(organ == o, 1.0, 0.0) * sums[o] for o in range(organs))
    columns = [to_column(own, m * directions, directions) for m in range(modes_ref.shape[0])]
    projected = projected_out.ref
    for f in range(blocks):
        projected[f] = subtract_modes(resid[f], columns, modes_ref, f)
    projected_out.flush()
    for f in range(blocks):
        value = resid[f] - times_split(left, jump_modes[f])
        base[f] = value + added if f == 0 else value
    norms[...] = jnp.broadcast_to(dots_row([(projected, projected)]), norms.shape)
    for copy in copies:
        copy.wait()


def inner_kernel(last, older, matches, f0, f1, f2, f3, f4, base, near, norms, *refs):
    rest = list(refs)
    previous = rest.pop(0) if older else None
    maps = None if last else rest[:3]
    far, message = rest[0 if last else 3 :][:2]
    rest = rest[2 if last else 5 :]
    if last:
        inner, smoothed = rest
    else:
        inner_out, smoothed_out = rest[:2]
        inner, smoothed = inner_out.ref, smoothed_out.ref
    for r, face in zip(ORDER, (f0, f1, f2, f3, f4), strict=True):
        inner[matches[r]] = base[matches[r]] - face[...]
    for f in range(inner.shape[0]):
        smooth(inner, near, far, smoothed, f)
    if not last:
        for r, send in enumerate(rest[2:]):
            send(smoothed.at[matches[r]])
        inner_out.flush()
        smoothed_out.flush()
        send_contact(message.ref, 4, smoothed[0], *(late() for late in maps))
    directions = inner.shape[1]
    pairs = [(inner, smoothed)]
    if older:
        pairs.append((previous(), smoothed))
    row = dots_row(pairs, directions) + norms[0:1, :]
    if last:
        message.ref[...] = jnp.broadcast_to(row, message.ref.shape)
    else:
        spread_rows(message.ref, 4, 2, row)


def step_sizes(row, older, scalars, directions):
    rho = to_column(row, 0, directions)
    curvature = to_column(row, directions, directions)
    if not older:
        return rho, None, curvature, rho / curvature
    cross = to_column(row, 2 * directions, directions)
    beta = rho / scalars[0, :, 0:1]
    curvature = curvature + beta * (2.0 * cross + beta * scalars[1, :, 0:1])
    return rho, beta, curvature, rho / curvature


def outer_contact(older, arrived, sent, smoothed, a_high, a_low, unit, projected, *refs):
    rest = list(refs)
    old_image = scalars = None
    if older:
        old_image, scalars = rest[0](), rest[1]()
        rest = rest[2:]
    new_scalars, part, steps, image = rest
    sent, smoothed, projected = sent(), smoothed(), projected()
    blocks, directions = smoothed.shape[0], smoothed.shape[1]
    row = jnp.sum(get(arrived, 4, 2), axis=0, keepdims=True)
    rho, beta, curvature, step = step_sizes(row, older, scalars, directions)
    wide = (directions, LANES)
    for place, column in enumerate((rho, curvature, step) + ((beta,) if older else ())):
        new_scalars.ref[place] = jnp.broadcast_to(column, wide)
    new_scalars.flush()
    steps[...] = jnp.broadcast_to(step, wide)
    added = contact(sent, arrived, 4, 4, a_high(), a_low(), unit())
    for f in range(blocks):
        value = smoothed[f]
        if f == 0:
            value = value + added
        if older:
            value = value + beta * old_image[f]
        image[f] = value
        part[f] = projected[f] - step * value


def outer_kernel(older, matches, f0, f1, f2, f3, f4, part, steps, image, *refs):
    t_high, t_low, unit_t, modes_ref = refs[:4]
    rest = list(refs[4:])
    if older:
        message, resid = rest[:2]
        sends = rest[2:]
    else:
        message, resid, new_image = rest[:3]
        sends = rest[3:]
    step = steps[:, 0:1]
    for r, face in zip(ORDER, (f0, f1, f2, f3, f4), strict=True):
        resid.ref[matches[r]] = part[matches[r]] + step * face[...]
        if not older:
            new_image.ref[matches[r]] = image[matches[r]] - face[...]
    send_residual(matches, resid, modes_ref, (t_high, t_low, unit_t), message, sends)


def update_kernel(older, projected, inner, total, scalars, *refs):
    projected, inner, total, scalars = (late() for late in (projected, inner, total, scalars))
    rest = list(refs)
    step = scalars[2, :, 0:1]
    if not older:
        for f in range(total.shape[0]):
            rest[0].ref[f] = total[f] + step * projected[f]
        return
    old_direction, old_inner = rest[0](), rest[1]()
    new_total, direction, new_inner = (out.ref for out in rest[2:])
    beta = scalars[3, :, 0:1]
    for f in range(total.shape[0]):
        value = projected[f] + beta * old_direction[f]
        direction[f] = value
        new_total[f] = total[f] + step * value
        new_inner[f] = inner[f] + beta * old_inner[f]


def last_kernel(arrived, projected, old_direction, total, scalars, out):
    projected, old_direction, total, scalars = (
        late() for late in (projected, old_direction, total, scalars)
    )
    blocks, directions = projected.shape[0], projected.shape[1]
    row = jnp.sum(arrived[...], axis=0, keepdims=True)
    _, beta, _, step = step_sizes(row, True, scalars, directions)
    for f in range(blocks):
        value = total[f] + step * (projected[f] + beta * old_direction[f])
        for c in range(directions):
            out.ref[c * blocks + f] = value[c : c + 1]


class Late:
    def __init__(self, source, target, sems):
        self.target = target
        if sems.shape[0] == 1:
            self.copies = [pltpu.make_async_copy(source, target, sems.at[0])]
        else:
            self.copies = [
                pltpu.make_async_copy(source.at[i], target.at[i], sems.at[i])
                for i in range(sems.shape[0])
            ]
        self.waiting = [True] * len(self.copies)
        for copy in self.copies:
            copy.start()

    def __call__(self, part=None):
        for i, copy in enumerate(self.copies):
            if self.waiting[i] and part in (None, i):
                copy.wait()
                self.waiting[i] = False
        return self.target if part is None else self.target.at[part]


class Send:
    def __init__(self, target, sem):
        self.target, self.sem, self.copy = target, sem, None

    def __call__(self, source):
        self.copy = pltpu.make_async_copy(source, self.target, self.sem)
        self.copy.start()


class Out:
    def __init__(self, ref, target, sem):
        self.ref = ref
        self.copy = pltpu.make_async_copy(ref, target, sem)
        self.started = False

    def flush(self):
        if not self.started:
            self.copy.start()
            self.started = True


def call(kernel, outs, args, late=(), smem=0, near=(), sends=(), scratch=(), whole=(), far=()):
    n_late, n_out, n_arg, n_near = len(late), len(outs), len(args), len(near)

    def body(*refs):
        refs = list(refs)

        def take(n):
            taken = refs[:n]
            del refs[:n]
            return taken

        given, sources, lasting = take(n_arg), take(n_late), take(len(whole))
        remote = take(len(far))
        targets, ports, close = take(n_out), take(len(sends)), take(n_near)
        buffers, ahead, results = take(n_late), take(len(far)), take(n_out)
        extra = take(len(scratch))
        in_sems, far_sems, out_sem = take(n_late), take(len(far)), refs[0]
        lates = [Late(s, b, m) for s, b, m in zip(sources, buffers, in_sems, strict=True)]
        for source, buffer, sem in zip(remote, ahead, far_sems, strict=True):
            skip = source.shape[0] - buffer.shape[0]
            lates.append(Late(source.at[pl.ds(skip, buffer.shape[0])], buffer, sem))
        written = [Out(r, t, out_sem.at[i]) for i, (r, t) in enumerate(zip(results, targets))]
        posts = [Send(t, out_sem.at[n_out + i]) for i, t in enumerate(ports)]
        kernel(*given, *lates, *lasting, *written, *posts, *close, *extra)
        for item in lates:
            item()
        for item in written:
            item.flush()
        for item in written + posts:
            item.copy.wait()

    in_specs = [pl.BlockSpec(memory_space=pltpu.SMEM)] * smem
    in_specs += [pl.BlockSpec(memory_space=pltpu.VMEM)] * (n_arg - smem)
    remote = tuple(late) + tuple(whole) + tuple(a for a, _ in far)
    in_specs += [pl.BlockSpec(memory_space=pltpu.HBM)] * len(remote)
    out_specs = [pl.BlockSpec(memory_space=pltpu.HBM)] * (n_out + len(sends))
    out_specs += [pl.BlockSpec(memory_space=pltpu.VMEM)] * n_near
    scratch_shapes = [pltpu.VMEM(a.shape, a.dtype) for a in late]
    scratch_shapes += [pltpu.VMEM((n,) + a.shape[1:], a.dtype) for a, n in far]
    scratch_shapes += [pltpu.VMEM(shape, kind) for shape, kind in outs]
    scratch_shapes += list(scratch)
    scratch_shapes += [pltpu.SemaphoreType.DMA((1,))] * n_late
    scratch_shapes += [pltpu.SemaphoreType.DMA((n,)) for _, n in far]
    scratch_shapes += [pltpu.SemaphoreType.DMA((max(n_out + len(sends), 1),))]
    return pl.pallas_call(
        body,
        out_shape=[pltpu.HBM(shape, kind) for shape, kind in tuple(outs) + tuple(sends)]
        + [pltpu.VMEM(shape, kind) for shape, kind in near],
        in_specs=in_specs,
        out_specs=out_specs,
        scratch_shapes=scratch_shapes,
        compiler_params=pltpu.CompilerParams(vmem_limit_bytes=VMEM_LIMIT),
        cost_estimate=pl.CostEstimate(
            flops=COST, bytes_accessed=COST, transcendentals=0
        ),
    )(*args, *(pltpu.with_memory_space_constraint(a, pltpu.HBM) for a in remote))


def from_partner(value, axis, apart):
    mask = 2**apart
    pairs = [(source, source ^ mask) for source in range(lax.axis_size(axis))]
    return lax.ppermute(value, axis, pairs)


def exchange(message):
    return lax.all_to_all(message, AXES, split_axis=0, concat_axis=0, tiled=True)


def swap_faces(faces):
    swapped = []
    for r in ORDER:
        axis, apart = ("sub", r) if r < SUB_ROUNDS else ("organ", r - SUB_ROUNDS)
        swapped.append(from_partner(faces[r], axis, apart))
    return swapped


def local(
    dual_rhs, warm_start, inverse_blocks, coarse_basis, mortar_rows, match_rounds, slave_owner,
    slave_dofs, active_set, row_counts,
):
    directions, blocks, length = dual_rhs.shape[0], dual_rhs.shape[3], dual_rhs.shape[4]
    rows = mortar_rows.shape[2]
    modes = coarse_basis.shape[0]
    organs, subs = lax.axis_size("organ"), lax.axis_size("sub")
    devices = organs * subs
    width = CAP * devices
    field = (blocks, directions, length)
    right_rows = dual_rhs.reshape(directions * blocks, 1, length)
    start_rows = warm_start.reshape(directions * blocks, 1, length)
    matrices = inverse_blocks.reshape(blocks, length, length)
    basis = coarse_basis.reshape(modes * blocks, 1, length)
    mortar = mortar_rows.reshape(rows, length)
    matches = match_rounds.reshape(-1)
    owner = slave_owner.reshape(1, rows)
    dofs = slave_dofs.reshape(1, rows)
    active = active_set.reshape(1, rows)
    count = row_counts.reshape(1)
    face = ((directions, length), F32)
    whole = (field, F32)
    message_line = ((4 * devices, LANES), F32)

    sends = [face] * blocks
    near_shape = ((NEAR, length, length), F32)
    fetching = [pltpu.SemaphoreType.DMA((NEAR,))]
    far = ((matrices, blocks - NEAR),)

    (setup,) = call(
        functools.partial(setup_kernel, blocks),
        [((devices, LANES), F32)],
        (count, owner, dofs, active, basis),
        smem=1,
    )
    arrived = exchange(setup)
    a_high, a_low, t_high, t_low, start, right = call(
        functools.partial(slots_kernel, devices),
        [((width, length), BF16)] * 2 + [((length, width), BF16)] * 2 + [whole] * 2,
        (count, owner, active),
        (mortar, start_rows, right_rows),
        smem=1,
    )
    sent, unit_t, unit, modes_ref, *faces = call(
        functools.partial(first_kernel, organs),
        [
            message_line,
            ((length, width), BF16),
            ((width, length), BF16),
            ((modes, blocks, length), F32),
        ]
        + [((directions + 8, length), F32)] * blocks,
        (matches, arrived, basis),
        (start, t_high, t_low, right),
        smem=1,
    )
    forth = (a_high, a_low, unit)
    back = (t_high, t_low, unit_t)
    arrived = exchange(sent)
    faces = swap_faces(faces)
    right, base, added, near = call(
        functools.partial(start_contact, organs),
        [whole],
        (arrived,),
        (sent, start) + forth + (modes_ref, right),
        whole=(matrices,),
        near=[whole, ((8 * organs, length), F32), near_shape],
        scratch=fetching,
    )
    message, smoothed, jump_modes, *posts = call(
        functools.partial(start_kernel, organs),
        [((2 * devices, LANES), F32), whole, ((blocks, 8 * organs, length), F32)],
        (matches, *faces, base, added, near),
        back + (modes_ref,),
        far=far,
        smem=1,
        sends=sends,
        scratch=[pltpu.VMEM(field, F32)],
    )
    arrived = exchange(message)
    faces = swap_faces(posts)
    (part,) = call(
        residual_contact, [], (arrived,), (message, smoothed) + forth + (right,), near=[whole]
    )
    sent, resid, *posts = call(
        residual_kernel,
        [message_line, whole],
        (matches, *faces, part),
        back + (modes_ref,),
        smem=1,
        sends=sends,
    )
    total = start
    direction = inner = image = scalars = None
    for step in range(ITERS):
        older, last = step > 0, step == ITERS - 1
        arrived = exchange(sent)
        faces = swap_faces(posts)
        projected, base, near, norms = call(
            functools.partial(inner_contact, organs),
            [whole],
            (arrived,),
            (sent, resid) + forth + (modes_ref, jump_modes),
            whole=(matrices,),
            near=[whole, near_shape, ((8, LANES), F32)],
            scratch=fetching,
        )
        previous = (inner,) if older else ()
        if last:
            (message,) = call(
                functools.partial(inner_kernel, last, older),
                [((devices, LANES), F32)],
                (matches, *faces, base, near, norms),
                previous,
                far=far,
                smem=1,
                scratch=[pltpu.VMEM(field, F32)] * 2,
            )
            arrived = exchange(message)
            break
        message, new_inner, smoothed, *posts = call(
            functools.partial(inner_kernel, last, older),
            [message_line, whole, whole],
            (matches, *faces, base, near, norms),
            previous + back,
            far=far,
            smem=1,
            sends=sends,
        )
        arrived = exchange(message)
        faces = swap_faces(posts)
        new_scalars, part, steps, image_part = call(
            functools.partial(outer_contact, older),
            [((4, directions, LANES), F32)],
            (arrived,),
            (message, smoothed) + forth + (projected,) + ((image, scalars) if older else ()),
            near=[whole, ((directions, LANES), F32), whole],
        )
        sent, resid, *posts = call(
            functools.partial(outer_kernel, older),
            [message_line, whole] + ([] if older else [whole]),
            (matches, *faces, part, steps, image_part),
            back + (modes_ref,),
            smem=1,
            sends=sends,
        )
        if not older:
            image, *posts = posts
        scalars = new_scalars
        updated = call(
            functools.partial(update_kernel, older),
            [whole] * (3 if older else 1),
            (),
            (projected, new_inner, total, scalars) + ((direction, inner) if older else ()),
        )
        if older:
            total, direction, inner = updated
        else:
            (total,) = updated
            direction, inner = projected, new_inner
    (result,) = call(
        last_kernel,
        [((directions * blocks, 1, length), F32)],
        (arrived,),
        (projected, direction, total, scalars),
    )
    return result.reshape(dual_rhs.shape)


def solution(mesh):
    in_specs = (
        P(None, "organ", "sub", None, None),
        P(None, "organ", "sub", None, None),
        P("organ", "sub", None, None, None),
        P(None, "organ", "sub", None, None),
        P("organ", "sub", None, None),
        P("organ", "sub", None),
        P("organ", "sub", None, None),
        P("organ", "sub", None),
        P("organ", "sub", None),
        P("organ", "sub", None),
    )
    out_specs = P(None, "organ", "sub", None, None)
    return jax.shard_map(local, mesh=mesh, in_specs=in_specs, out_specs=out_specs, check_vma=False)
```

```python
import functools

import jax
import jax.numpy as jnp
from jax import lax
from jax.experimental import pallas as pl
from jax.experimental.pallas import tpu as pltpu
from jax.sharding import PartitionSpec as P

ITERS = 3
CAP = 8
SUB_ROUNDS = 3
ORDER = (2, 0, 1, 4, 3)
AXES = ("organ", "sub")
LANES = 128
F32 = jnp.float32
BF16 = jnp.bfloat16
VMEM_LIMIT = 24 * 2**20
COST = 2_000_000
BRING = 1


def iota(shape, dim):
    return lax.broadcasted_iota(jnp.int32, shape, dim)


def halves(x):
    high = x.astype(BF16)
    return high, (x - high.astype(F32)).astype(BF16)


def thirds(x):
    high = x.astype(BF16)
    rest = x - high.astype(F32)
    middle = rest.astype(BF16)
    return high, middle, (rest - middle.astype(F32)).astype(BF16)


def bdot(a, b):
    return jnp.dot(a, b, preferred_element_type=F32)


def times(x, w_high, w_low):
    rows = x.shape[0]
    a, b, c = thirds(x)
    full = bdot(jnp.concatenate([a, b, c], axis=0), w_high)
    part = bdot(jnp.concatenate([a, b], axis=0), w_low)
    low = full[2 * rows :] + part[rows:]
    return full[:rows] + (full[rows : 2 * rows] + part[:rows] + low)


def times_split(x, w):
    rows = x.shape[0]
    a, b = halves(x)
    w_high, w_low = halves(w)
    full = bdot(jnp.concatenate([a, b], axis=0), w_high)
    return full[:rows] + (full[rows:] + bdot(a, w_low))


def square(x):
    rows, cols = x.shape
    if rows < LANES:
        x = jnp.concatenate([x, jnp.zeros((LANES - rows, cols), F32)], axis=0)
    if cols < LANES:
        x = jnp.concatenate([x, jnp.zeros((x.shape[0], LANES - cols), F32)], axis=1)
    return x.T


def pack(master, slave, devices):
    def stacked(x):
        pieces = [x[:, k * devices : (k + 1) * devices] for k in range(CAP)]
        return jnp.concatenate(pieces, axis=0)

    turned = square(jnp.concatenate([stacked(master), stacked(slave)], axis=1))
    return turned[:devices], turned[devices : 2 * devices]


def unpack(master, slave, rows):
    devices = master.shape[0]
    turned = square(jnp.concatenate([master, slave], axis=0))

    def laid(first):
        pieces = [
            turned[k * rows : (k + 1) * rows, first : first + devices] for k in range(CAP)
        ]
        return jnp.concatenate(pieces, axis=1)

    return laid(0), laid(devices)


def put(ref, per, line, value):
    ref[pl.ds(line, value.shape[0], stride=per), :] = value


def get(ref, per, line):
    return ref[pl.ds(line, ref.shape[0] // per, stride=per), :]


def to_column(row, base, rows):
    spread = jnp.broadcast_to(row, (rows, LANES))
    here = iota((rows, LANES), 1) == iota((rows, LANES), 0) + base
    return jnp.sum(jnp.where(here, spread, 0.0), axis=1, keepdims=True)


def at_lanes(column, base):
    rows = column.shape[0]
    here = iota((rows, LANES), 1) == iota((rows, LANES), 0) + base
    return jnp.where(here, column, 0.0)


def fold(x):
    return sum(x[:, i : i + LANES] for i in range(0, x.shape[1], LANES))


def dots_row(pairs, base=0):
    total = 0.0
    for place, (left, right) in enumerate(pairs):
        acc = sum(fold(left[f] * right[f]) for f in range(left.shape[0]))
        column = jnp.sum(acc, axis=1, keepdims=True)
        total = total + at_lanes(column, base + place * column.shape[0])
    return jnp.sum(total, axis=0, keepdims=True)


def coefficients_row(field, basis):
    total = 0.0
    blocks, directions = field.shape[0], field.shape[1]
    for m in range(basis.shape[0]):
        acc = sum(fold(field[f] * basis[m, f : f + 1, :]) for f in range(blocks))
        total = total + at_lanes(jnp.sum(acc, axis=1, keepdims=True), m * directions)
    return jnp.sum(total, axis=0, keepdims=True)


def exact(x, unit):
    rows = x.shape[0]
    full = bdot(jnp.concatenate(thirds(x), axis=0), unit)
    return full[:rows] + (full[rows : 2 * rows] + full[2 * rows :])


def contact(mine, theirs, per_mine, per_theirs, a_high, a_low, unit):
    own = [get(mine, per_mine, i) for i in range(2)]
    other = [get(theirs, per_theirs, i) for i in range(2)]
    master, slave = unpack(own[0] + other[1], own[1] + other[0], LANES // CAP)
    return times(master, a_high[...], a_low[...]) + exact(slave, unit[...])


def send_contact(message, per, surface, t_high, t_low, unit_t):
    devices = message.shape[0] // per
    master = times(surface, t_high[...], t_low[...])
    slave = exact(surface, unit_t[...])
    for line, value in enumerate(pack(master, slave, devices)):
        put(message, per, line, value)


def spread_rows(message, per, line, row):
    put(message, per, line, jnp.broadcast_to(row, (message.shape[0] // per, LANES)))


def ranks(owner_row, active_row, count):
    rows = owner_row.shape[1]
    up, across = iota((rows, rows), 0), iota((rows, rows), 1)
    diagonal = up == across

    def column(row):
        return jnp.sum(jnp.where(diagonal, row, 0), axis=1, keepdims=True)

    live_row = jnp.where(iota((1, rows), 1) < count, active_row, 0)
    owner_col, live_col = column(owner_row), column(live_row)
    same = owner_col == owner_row
    rank_col = jnp.sum(jnp.where(same & (across < up), live_row, 0), axis=1, keepdims=True)
    rank_row = jnp.sum(jnp.where(same & (up < across), live_col, 0), axis=0, keepdims=True)
    return column, live_row, live_col, owner_col, rank_row, rank_col


def load_modes(basis, modes, blocks):
    return [
        jnp.concatenate([basis[m * blocks + f] for f in range(blocks)], axis=0)
        for m in range(modes)
    ]


def setup_kernel(blocks, count, owner, dofs, active, basis, message):
    devices = message.ref.shape[0]
    owner, dofs, active, basis = owner(), dofs(), active(), basis()
    rows = owner.shape[1]
    column, live_row, _, _, _, rank_col = ranks(owner[...], active[...], count[0])
    named = (iota((devices, rows), 0) == owner[...]) & (live_row > 0)
    slots = jnp.where(iota((rows, LANES), 1) == rank_col, column(dofs[...]) + 1, 0)
    lines = jnp.dot(
        jnp.where(named, 1.0, 0.0),
        slots.astype(F32),
        precision=lax.Precision.HIGHEST,
        preferred_element_type=F32,
    )
    modes = basis.shape[0] // blocks
    slabs = load_modes(basis, modes, blocks)
    lane = iota((1, LANES), 1)
    gram = jnp.zeros((1, LANES), F32)
    for i in range(modes):
        for j in range(i + 1):
            value = jnp.sum(fold(slabs[i] * slabs[j]), axis=0, keepdims=True)
            value = jnp.sum(value, axis=1, keepdims=True)
            gram = jnp.where(lane == LANES // 2 + 8 * i + j, value, gram)
    message.ref[...] = jnp.where(iota((devices, LANES), 1) < CAP, lines, gram)


def slots_kernel(
    devices, count, owner, active, mortar, start_rows, right_rows, a_high, a_low, t_high, t_low,
    start, right,
):
    owner, active = owner(), active()
    rows = owner.shape[1]
    width = CAP * devices
    _, live_row, live_col, owner_col, rank_row, rank_col = ranks(
        owner[...], active[...], count[0]
    )
    slot_row = jnp.where(live_row > 0, rank_row * devices + owner[...], -1)
    slot_col = jnp.where(live_col > 0, rank_col * devices + owner_col, -1)
    pick = jnp.where(iota((width, rows), 0) == slot_row, 1.0, 0.0).astype(BF16)
    pick_t = jnp.where(iota((rows, width), 1) == slot_col, 1.0, 0.0).astype(BF16)
    blocks, directions = start.ref.shape[0], start.ref.shape[1]
    for source, target in ((start_rows(), start), (right_rows(), right)):
        for f in range(blocks):
            for c in range(directions):
                target.ref[f, c : c + 1, :] = source[c * blocks + f]
        target.flush()
    for part, straight, turned in zip(
        halves(mortar()[...]), (a_high, a_low), (t_high, t_low), strict=True
    ):
        straight.ref[...] = bdot(pick, part).astype(BF16)
        straight.flush()
        turned.ref[...] = bdot(part.astype(F32).T.astype(BF16), pick_t).astype(BF16)
        turned.flush()


def first_kernel(
    organs, matches, arrived, basis, start, t_high, t_low, right, message, unit_t, unit,
    modes_out, *sends,
):
    devices = arrived.shape[0]
    subs = devices // organs
    blocks = len(sends)
    basis = basis()
    modes = basis.shape[0] // blocks
    length = basis.shape[2]
    dofs = arrived[...]
    turned = square(dofs)[:CAP, :devices]
    dof_row = jnp.concatenate([turned[k : k + 1, :] for k in range(CAP)], axis=1)
    place_t = iota((length, CAP * devices), 0).astype(F32) + 1.0
    unit_t.ref[...] = jnp.where(place_t == dof_row, -1.0, 0.0).astype(BF16)
    unit_t.flush()
    mine = lax.axis_index("organ") * subs
    total = jnp.sum(arrived[pl.ds(pl.multiple_of(mine, 8), subs), :], axis=0, keepdims=True)
    lane = iota((1, LANES), 1)

    def entry(i, j):
        here = lane == LANES // 2 + 8 * i + j
        return jnp.sum(jnp.where(here, total, 0.0), axis=1, keepdims=True)

    low, inverse = {}, {}
    for j in range(modes):
        pivot = entry(j, j) - sum(low[j, k] * low[j, k] for k in range(j))
        inverse[j, j] = 1.0 / jnp.sqrt(pivot)
        for i in range(j + 1, modes):
            value = entry(i, j) - sum(low[i, k] * low[j, k] for k in range(j))
            low[i, j] = value * inverse[j, j]
    for j in range(modes):
        for i in range(j + 1, modes):
            value = sum(low[i, k] * inverse[k, j] for k in range(j, i))
            inverse[i, j] = -inverse[i, i] * value
    slabs = load_modes(basis, modes, blocks)
    modes_ref = modes_out.ref
    for i in range(modes):
        modes_ref[i] = sum(inverse[i, j] * slabs[j] for j in range(i + 1))
    modes_out.flush()
    start = start()
    directions = start.shape[1]
    for r in range(blocks):
        face = matches[r]
        send = sends[r].ref
        send[0:directions, :] = start[face]
        for m in range(modes):
            send[directions + m : directions + m + 1, :] = modes_ref[m, pl.ds(face, 1), :]
        for m in range(modes, 8):
            send[directions + m : directions + m + 1, :] = jnp.zeros((1, length), F32)
        sends[r].flush()
    first = [modes_ref[m, 0:1, :] for m in range(modes)]
    extra = jnp.zeros((2 * 16 - directions - modes, length), F32)
    both = jnp.concatenate([start[0]] + first + [extra], axis=0)
    master = times(both, t_high()[...], t_low()[...])
    slave = exact(both, unit_t.ref[...])
    for line, value in enumerate(pack(master[:directions], slave[:directions], devices)):
        put(message.ref, 4, line, value)
    rows = slice(directions, directions + 8)
    lines = pack(master[rows], slave[rows], devices)
    half = LANES // 2
    put(message.ref, 4, 2, jnp.concatenate([line[:, :half] for line in lines], axis=1))
    spread_rows(message.ref, 4, 3, coefficients_row(right(), modes_ref))
    message.flush()
    place = iota((devices, length), 1).astype(F32) + 1.0
    for k in range(CAP):
        block = jnp.where(place == dofs[:, k : k + 1], -1.0, 0.0).astype(BF16)
        unit.ref[k * devices : (k + 1) * devices, :] = block


def smooth(inner, near, smoothed, f):
    smoothed[f] = times_split(inner[f], near[f])


def subtract_modes(field, columns, basis, f):
    value = field
    for m, column in enumerate(columns):
        value = value - column * basis[m, f : f + 1, :]
    return value


def start_contact(
    organs, arrived, sent, start, a_high, a_low, unit, modes_ref, right, new_right,
    base, added,
):
    sent, start, maps = sent(), start(), (a_high(), a_low(), unit())
    devices = sent.shape[0] // 4
    subs = devices // organs
    blocks, directions = start.shape[0], start.shape[1]
    base[...] = start[...]
    base[0] += contact(sent, arrived, 4, 4, *maps)
    modes_ref, right = modes_ref(), right()
    organ = lax.axis_index("organ")
    block = arrived[pl.ds(pl.multiple_of(organ * subs * 4, 8), subs * 4), :]
    here = lax.rem(iota(block.shape, 0), 4) == 3
    row = jnp.sum(jnp.where(here, block, 0.0), axis=0, keepdims=True)
    columns = [to_column(row, m * directions, directions) for m in range(modes_ref.shape[0])]
    for f in range(blocks):
        new_right.ref[f] = subtract_modes(right[f], columns, modes_ref, f)
    new_right.flush()
    half = LANES // 2
    mine, other = get(sent, 4, 2), get(arrived, 4, 2)
    own_rows = unpack(mine[:, :half], mine[:, half:], 8)
    other_rows = unpack(other[:, half:], other[:, :half], 8)
    source = lax.rem(iota(own_rows[0].shape, 1), devices) // subs
    stacks = []
    for own_half, other_half in zip(own_rows, other_rows, strict=True):
        stack = []
        for o in range(organs):
            owns = jnp.where(organ == o, 1.0, 0.0)
            stack.append(jnp.where(source == o, other_half, 0.0) + owns * own_half)
        stacks.append(jnp.concatenate(stack, axis=0))
    added[...] = times(stacks[0], maps[0][...], maps[1][...]) + exact(stacks[1], maps[2][...])


def start_kernel(
    organs, matches, f0, f1, f2, f3, f4, base, added, t_high, t_low, unit_t, near, modes_ref,
    message, smoothed_out, jump_out, s0, s1, s2, s3, s4, inner,
):
    faces = (f0, f1, f2, f3, f4)
    smoothed = smoothed_out.ref
    blocks, directions = base.shape[0], base.shape[1]
    for r, face in zip(ORDER, faces, strict=True):
        inner[matches[r]] = base[matches[r]] - face[0:directions, :]
    for f in range(blocks):
        smooth(inner, near, smoothed, f)
    for r, send in enumerate((s0, s1, s2, s3, s4)):
        send(smoothed.at[matches[r]])
    smoothed_out.flush()
    send_contact(message.ref, 2, smoothed[0], t_high, t_low, unit_t)
    message.flush()
    modes = modes_ref.shape[0]
    jump_modes = jump_out.ref
    organ = lax.axis_index("organ")
    jump_modes[...] = jnp.zeros(jump_modes.shape, F32)
    for r, values in zip(ORDER, faces, strict=True):
        face = matches[r]
        for m in range(modes):
            own = modes_ref[m, pl.ds(face, 1), :]
            other = values[directions + m : directions + m + 1, :]
            if r < SUB_ROUNDS:
                own = own - other
            else:
                partner = organ ^ (1 << (r - SUB_ROUNDS))
                jump_modes[face, pl.ds(m * organs + partner, 1), :] = -other
            jump_modes[face, pl.ds(m * organs + organ, 1), :] = own
    for o in range(organs):
        for m in range(modes):
            row = pl.ds(m * organs + o, 1)
            jump_modes[0, row, :] = jump_modes[0, row, :] + added[8 * o + m : 8 * o + m + 1, :]


def residual_contact(arrived, sent, smoothed, a_high, a_low, unit, right, part):
    sent, smoothed, right = sent(), smoothed(), right()
    part[...] = right[...] - smoothed[...]
    part[0] -= contact(sent, arrived, 2, 2, a_high(), a_low(), unit())


def residual_kernel(
    matches, f0, f1, f2, f3, f4, part, t_high, t_low, unit_t, modes_ref, message, resid, *sends
):
    for r, face in zip(ORDER, (f0, f1, f2, f3, f4), strict=True):
        resid.ref[matches[r]] = part[matches[r]] + face[...]
    send_residual(matches, resid, modes_ref, (t_high, t_low, unit_t), message, sends)


def send_residual(matches, resid, modes_ref, maps, message, sends):
    for r, send in enumerate(sends):
        send(resid.ref.at[matches[r]])
    resid.flush()
    send_contact(message.ref, 4, resid.ref[0], *maps)
    spread_rows(message.ref, 4, 2, coefficients_row(resid.ref, modes_ref))
    message.flush()


def inner_contact(
    organs, arrived, sent, resid, a_high, a_low, unit, modes_ref, jump_modes, projected_out, base,
    norms,
):
    sent, resid, maps = sent(), resid(), (a_high(), a_low(), unit())
    modes_ref, jump_modes = modes_ref(), jump_modes()
    devices = sent.shape[0] // 4
    subs = devices // organs
    blocks, directions = resid.shape[0], resid.shape[1]
    parts = get(arrived, 4, 2)
    sums = [
        jnp.sum(parts[o * subs : (o + 1) * subs], axis=0, keepdims=True) for o in range(organs)
    ]
    added = contact(sent, arrived, 4, 4, *maps)
    turned = square(jnp.concatenate(sums, axis=0))
    left = jnp.concatenate(
        [turned[m * directions : (m + 1) * directions, :organs] for m in range(8)], axis=1
    )
    organ = lax.axis_index("organ")
    own = sum(jnp.where(organ == o, 1.0, 0.0) * sums[o] for o in range(organs))
    columns = [to_column(own, m * directions, directions) for m in range(modes_ref.shape[0])]
    projected = projected_out.ref
    for f in range(blocks):
        projected[f] = subtract_modes(resid[f], columns, modes_ref, f)
    projected_out.flush()
    for f in range(blocks):
        value = resid[f] - times_split(left, jump_modes[f])
        base[f] = value + added if f == 0 else value
    norms[...] = jnp.broadcast_to(dots_row([(projected, projected)]), norms.shape)


def inner_kernel(last, older, matches, f0, f1, f2, f3, f4, base, norms, near, *refs):
    rest = list(refs)
    previous = rest.pop(0) if older else None
    maps = None if last else rest[:3]
    message = rest[0 if last else 3]
    rest = rest[1 if last else 4 :]
    if last:
        inner, smoothed = rest
    else:
        inner_out, smoothed_out = rest[:2]
        inner, smoothed = inner_out.ref, smoothed_out.ref
    for r, face in zip(ORDER, (f0, f1, f2, f3, f4), strict=True):
        inner[matches[r]] = base[matches[r]] - face[...]
    for f in range(inner.shape[0]):
        smooth(inner, near, smoothed, f)
    if not last:
        for r, send in enumerate(rest[2:]):
            send(smoothed.at[matches[r]])
        inner_out.flush()
        smoothed_out.flush()
        send_contact(message.ref, 4, smoothed[0], *maps)
    directions = inner.shape[1]
    pairs = [(inner, smoothed)]
    if older:
        pairs.append((previous, smoothed))
    row = dots_row(pairs, directions) + norms[0:1, :]
    if last:
        message.ref[...] = jnp.broadcast_to(row, message.ref.shape)
    else:
        spread_rows(message.ref, 4, 2, row)


def step_sizes(row, older, scalars, directions):
    rho = to_column(row, 0, directions)
    curvature = to_column(row, directions, directions)
    if not older:
        return rho, None, curvature, rho / curvature
    cross = to_column(row, 2 * directions, directions)
    beta = rho / scalars[0, :, 0:1]
    curvature = curvature + beta * (2.0 * cross + beta * scalars[1, :, 0:1])
    return rho, beta, curvature, rho / curvature


def outer_contact(older, arrived, sent, smoothed, a_high, a_low, unit, projected, *refs):
    rest = list(refs)
    old_image = scalars = None
    if older:
        old_image, scalars = rest[0](), rest[1]()
        rest = rest[2:]
    new_scalars, part, steps, image = rest
    sent, smoothed, projected = sent(), smoothed(), projected()
    blocks, directions = smoothed.shape[0], smoothed.shape[1]
    row = jnp.sum(get(arrived, 4, 2), axis=0, keepdims=True)
    rho, beta, curvature, step = step_sizes(row, older, scalars, directions)
    wide = (directions, LANES)
    for place, column in enumerate((rho, curvature, step) + ((beta,) if older else ())):
        new_scalars.ref[place] = jnp.broadcast_to(column, wide)
    new_scalars.flush()
    steps[...] = jnp.broadcast_to(step, wide)
    added = contact(sent, arrived, 4, 4, a_high(), a_low(), unit())
    for f in range(blocks):
        value = smoothed[f]
        if f == 0:
            value = value + added
        if older:
            value = value + beta * old_image[f]
        image[f] = value
        part[f] = projected[f] - step * value


def outer_kernel(older, matches, f0, f1, f2, f3, f4, part, steps, image, *refs):
    t_high, t_low, unit_t, modes_ref = refs[:4]
    rest = list(refs[4:])
    if older:
        message, resid = rest[:2]
        sends = rest[2:]
    else:
        message, resid, new_image = rest[:3]
        sends = rest[3:]
    step = steps[:, 0:1]
    for r, face in zip(ORDER, (f0, f1, f2, f3, f4), strict=True):
        resid.ref[matches[r]] = part[matches[r]] + step * face[...]
        if not older:
            new_image.ref[matches[r]] = image[matches[r]] - face[...]
    send_residual(matches, resid, modes_ref, (t_high, t_low, unit_t), message, sends)


def update_kernel(older, projected, inner, total, scalars, *refs):
    projected, inner, total, scalars = (late() for late in (projected, inner, total, scalars))
    rest = list(refs)
    step = scalars[2, :, 0:1]
    if not older:
        for f in range(total.shape[0]):
            rest[0].ref[f] = total[f] + step * projected[f]
        return
    old_direction, old_inner = rest[0](), rest[1]()
    new_total, direction, new_inner = (out.ref for out in rest[2:])
    beta = scalars[3, :, 0:1]
    for f in range(total.shape[0]):
        value = projected[f] + beta * old_direction[f]
        direction[f] = value
        new_total[f] = total[f] + step * value
        new_inner[f] = inner[f] + beta * old_inner[f]


def last_kernel(arrived, projected, old_direction, total, scalars, out):
    projected, old_direction, total, scalars = (
        late() for late in (projected, old_direction, total, scalars)
    )
    blocks, directions = projected.shape[0], projected.shape[1]
    row = jnp.sum(arrived[...], axis=0, keepdims=True)
    _, beta, _, step = step_sizes(row, True, scalars, directions)
    for f in range(blocks):
        value = total[f] + step * (projected[f] + beta * old_direction[f])
        for c in range(directions):
            out.ref[c * blocks + f] = value[c : c + 1]


class Late:
    def __init__(self, source, target, sem):
        self.target, self.waiting = target, True
        self.copy = pltpu.make_async_copy(source, target, sem)
        self.copy.start()

    def __call__(self):
        if self.waiting:
            self.copy.wait()
            self.waiting = False
        return self.target


class Send:
    def __init__(self, target, sem):
        self.target, self.sem, self.copy = target, sem, None

    def __call__(self, source):
        self.copy = pltpu.make_async_copy(source, self.target, self.sem)
        self.copy.start()


class Out:
    def __init__(self, ref, target, sem):
        self.ref = ref
        self.copy = pltpu.make_async_copy(ref, target, sem)
        self.started = False

    def flush(self):
        if not self.started:
            self.copy.start()
            self.started = True


def call(kernel, outs, args, late=(), smem=0, near=(), sends=(), scratch=(), bring=()):
    n_late, n_out, n_arg, n_near = len(late), len(outs), len(args), len(near)
    brought = [(a.shape, a.dtype) for a in bring]

    def body(*refs):
        refs = list(refs)

        def take(n):
            taken = refs[:n]
            del refs[:n]
            return taken

        given, sources, origins = take(n_arg), take(n_late), take(len(bring))
        targets, ports, close = take(n_out), take(len(sends)), take(n_near)
        goals = take(len(bring))
        buffers, results = take(n_late), take(n_out)
        extra = take(len(scratch))
        in_sem, bring_sem, out_sem = refs
        lates = [Late(s, b, in_sem.at[i]) for i, (s, b) in enumerate(zip(sources, buffers))]
        written = [Out(r, t, out_sem.at[i]) for i, (r, t) in enumerate(zip(results, targets))]
        posts = [Send(t, out_sem.at[n_out + i]) for i, t in enumerate(ports)]
        copies = []
        for i, (origin, goal) in enumerate(zip(origins, goals, strict=True)):
            copies.append(pltpu.make_async_copy(origin, goal, bring_sem.at[i]))
        for copy in copies:
            copy.start(priority=BRING)
        kernel(*given, *lates, *written, *posts, *close, *extra)
        for item in lates:
            item()
        for copy in copies:
            copy.wait()
        for item in written:
            item.flush()
        for item in written + posts:
            item.copy.wait()

    in_specs = [pl.BlockSpec(memory_space=pltpu.SMEM)] * smem
    in_specs += [pl.BlockSpec(memory_space=pltpu.VMEM)] * (n_arg - smem)
    remote = tuple(late) + tuple(bring)
    in_specs += [pl.BlockSpec(memory_space=pltpu.HBM)] * len(remote)
    out_specs = [pl.BlockSpec(memory_space=pltpu.HBM)] * (n_out + len(sends))
    out_specs += [pl.BlockSpec(memory_space=pltpu.VMEM)] * (n_near + len(bring))
    scratch_shapes = [pltpu.VMEM(a.shape, a.dtype) for a in late]
    scratch_shapes += [pltpu.VMEM(shape, kind) for shape, kind in outs]
    scratch_shapes += list(scratch)
    counts = (n_late, len(bring), n_out + len(sends))
    scratch_shapes += [pltpu.SemaphoreType.DMA((max(n, 1),)) for n in counts]
    return pl.pallas_call(
        body,
        out_shape=[pltpu.HBM(shape, kind) for shape, kind in tuple(outs) + tuple(sends)]
        + [pltpu.VMEM(shape, kind) for shape, kind in list(near) + brought],
        in_specs=in_specs,
        out_specs=out_specs,
        scratch_shapes=scratch_shapes,
        compiler_params=pltpu.CompilerParams(vmem_limit_bytes=VMEM_LIMIT),
        cost_estimate=pl.CostEstimate(flops=COST, bytes_accessed=COST, transcendentals=0),
    )(*args, *(pltpu.with_memory_space_constraint(a, pltpu.HBM) for a in remote))


def from_partner(value, axis, apart):
    mask = 2**apart
    pairs = [(source, source ^ mask) for source in range(lax.axis_size(axis))]
    return lax.ppermute(value, axis, pairs)


def exchange(message):
    return lax.all_to_all(message, AXES, split_axis=0, concat_axis=0, tiled=True)


def swap_faces(faces):
    swapped = []
    for r in ORDER:
        axis, apart = ("sub", r) if r < SUB_ROUNDS else ("organ", r - SUB_ROUNDS)
        swapped.append(from_partner(faces[r], axis, apart))
    return swapped


def local(
    dual_rhs, warm_start, inverse_blocks, coarse_basis, mortar_rows, match_rounds, slave_owner,
    slave_dofs, active_set, row_counts,
):
    directions, blocks, length = dual_rhs.shape[0], dual_rhs.shape[3], dual_rhs.shape[4]
    rows = mortar_rows.shape[2]
    modes = coarse_basis.shape[0]
    organs, subs = lax.axis_size("organ"), lax.axis_size("sub")
    devices = organs * subs
    width = CAP * devices
    field = (blocks, directions, length)
    right_rows = dual_rhs.reshape(directions * blocks, 1, length)
    start_rows = warm_start.reshape(directions * blocks, 1, length)
    matrices = inverse_blocks.reshape(blocks, length, length)
    basis = coarse_basis.reshape(modes * blocks, 1, length)
    mortar = mortar_rows.reshape(rows, length)
    matches = match_rounds.reshape(-1)
    owner = slave_owner.reshape(1, rows)
    dofs = slave_dofs.reshape(1, rows)
    active = active_set.reshape(1, rows)
    count = row_counts.reshape(1)
    face = ((directions, length), F32)
    whole = (field, F32)
    message_line = ((4 * devices, LANES), F32)

    sends = [face] * blocks
    near_matrices = (matrices,)

    (setup,) = call(
        functools.partial(setup_kernel, blocks),
        [((devices, LANES), F32)],
        (count,),
        (owner, dofs, active, basis),
        smem=1,
    )
    arrived = exchange(setup)
    a_high, a_low, t_high, t_low, start, right = call(
        functools.partial(slots_kernel, devices),
        [((width, length), BF16)] * 2 + [((length, width), BF16)] * 2 + [whole] * 2,
        (count,),
        (owner, active, mortar, start_rows, right_rows),
        smem=1,
    )
    sent, unit_t, unit, modes_ref, *faces = call(
        functools.partial(first_kernel, organs),
        [
            message_line,
            ((length, width), BF16),
            ((width, length), BF16),
            ((modes, blocks, length), F32),
        ]
        + [((directions + 8, length), F32)] * blocks,
        (matches, arrived),
        (basis, start, t_high, t_low, right),
        smem=1,
    )
    forth = (a_high, a_low, unit)
    back = (t_high, t_low, unit_t)
    back_modes = back + (modes_ref,)
    arrived = exchange(sent)
    faces = swap_faces(faces)
    right, base, added, *maps, modes_near, near = call(
        functools.partial(start_contact, organs),
        [whole],
        (arrived,),
        (sent, start) + forth + (modes_ref, right),
        near=[whole, ((8 * organs, length), F32)],
        bring=back_modes + near_matrices,
    )
    message, smoothed, jump_modes, *posts = call(
        functools.partial(start_kernel, organs),
        [((2 * devices, LANES), F32), whole, ((blocks, 8 * organs, length), F32)],
        (matches, *faces, base, added, *maps, near, modes_near),
        smem=1,
        sends=sends,
        scratch=[pltpu.VMEM(field, F32)],
    )
    arrived = exchange(message)
    faces = swap_faces(posts)
    part, *maps = call(
        residual_contact,
        [],
        (arrived,),
        (message, smoothed) + forth + (right,),
        near=[whole],
        bring=back_modes,
    )
    sent, resid, *posts = call(
        residual_kernel,
        [message_line, whole],
        (matches, *faces, part, *maps),
        smem=1,
        sends=sends,
    )
    total = start
    direction = inner = image = scalars = None
    for step in range(ITERS):
        older, last = step > 0, step == ITERS - 1
        arrived = exchange(sent)
        faces = swap_faces(posts)
        ahead = near_matrices + ((inner,) if older else ()) + (() if last else back)
        projected, base, norms, *ahead = call(
            functools.partial(inner_contact, organs),
            [whole],
            (arrived,),
            (sent, resid) + forth + (modes_ref, jump_modes),
            near=[whole, ((8, LANES), F32)],
            bring=ahead,
        )
        if last:
            (message,) = call(
                functools.partial(inner_kernel, last, older),
                [((devices, LANES), F32)],
                (matches, *faces, base, norms, *ahead),
                        smem=1,
                scratch=[pltpu.VMEM(field, F32)] * 2,
            )
            arrived = exchange(message)
            break
        message, new_inner, smoothed, *posts = call(
            functools.partial(inner_kernel, last, older),
            [message_line, whole, whole],
            (matches, *faces, base, norms, *ahead),
                smem=1,
            sends=sends,
        )
        arrived = exchange(message)
        faces = swap_faces(posts)
        new_scalars, part, steps, image_part, *maps = call(
            functools.partial(outer_contact, older),
            [((4, directions, LANES), F32)],
            (arrived,),
            (message, smoothed) + forth + (projected,) + ((image, scalars) if older else ()),
            near=[whole, ((directions, LANES), F32), whole],
            bring=back_modes,
        )
        sent, resid, *posts = call(
            functools.partial(outer_kernel, older),
            [message_line, whole] + ([] if older else [whole]),
            (matches, *faces, part, steps, image_part, *maps),
            smem=1,
            sends=sends,
        )
        if not older:
            image, *posts = posts
        scalars = new_scalars
        updated = call(
            functools.partial(update_kernel, older),
            [whole] * (3 if older else 1),
            (),
            (projected, new_inner, total, scalars) + ((direction, inner) if older else ()),
        )
        if older:
            total, direction, inner = updated
        else:
            (total,) = updated
            direction, inner = projected, new_inner
    (result,) = call(
        last_kernel,
        [((directions * blocks, 1, length), F32)],
        (arrived,),
        (projected, direction, total, scalars),
    )
    return result.reshape(dual_rhs.shape)


def solution(mesh):
    in_specs = (
        P(None, "organ", "sub", None, None),
        P(None, "organ", "sub", None, None),
        P("organ", "sub", None, None, None),
        P(None, "organ", "sub", None, None),
        P("organ", "sub", None, None),
        P("organ", "sub", None),
        P("organ", "sub", None, None),
        P("organ", "sub", None),
        P("organ", "sub", None),
        P("organ", "sub", None),
    )
    out_specs = P(None, "organ", "sub", None, None)
    return jax.shard_map(local, mesh=mesh, in_specs=in_specs, out_specs=out_specs, check_vma=False)
```

```python
import functools

import jax
import jax.numpy as jnp
from jax import lax
from jax.experimental import pallas as pl
from jax.experimental.pallas import tpu as pltpu
from jax.sharding import PartitionSpec as P

ITERS = 3
CAP = 8
SUB_ROUNDS = 3
ORDER = (2, 0, 1, 4, 3)
AXES = ("organ", "sub")
LANES = 128
F32 = jnp.float32
BF16 = jnp.bfloat16
VMEM_LIMIT = 24 * 2**20
COST = 2_000_000
BRING = 1
BAND = 256


def iota(shape, dim):
    return lax.broadcasted_iota(jnp.int32, shape, dim)


def halves(x):
    high = x.astype(BF16)
    return high, (x - high.astype(F32)).astype(BF16)


def thirds(x):
    high = x.astype(BF16)
    rest = x - high.astype(F32)
    middle = rest.astype(BF16)
    return high, middle, (rest - middle.astype(F32)).astype(BF16)


def bdot(a, b):
    return jnp.dot(a, b, preferred_element_type=F32)


def times(x, w_high, w_low):
    rows = x.shape[0]
    a, b, c = thirds(x)
    full = bdot(jnp.concatenate([a, b, c], axis=0), w_high)
    part = bdot(jnp.concatenate([a, b], axis=0), w_low)
    low = full[2 * rows :] + part[rows:]
    return full[:rows] + (full[rows : 2 * rows] + part[:rows] + low)


def times_split(x, w):
    rows = x.shape[0]
    a, b = halves(x)
    w_high, w_low = halves(w)
    full = bdot(jnp.concatenate([a, b], axis=0), w_high)
    return full[:rows] + (full[rows:] + bdot(a, w_low))


def square(x):
    rows, cols = x.shape
    if rows < LANES:
        x = jnp.concatenate([x, jnp.zeros((LANES - rows, cols), F32)], axis=0)
    if cols < LANES:
        x = jnp.concatenate([x, jnp.zeros((x.shape[0], LANES - cols), F32)], axis=1)
    return x.T


def pack(master, slave, devices):
    def stacked(x):
        pieces = [x[:, k * devices : (k + 1) * devices] for k in range(CAP)]
        return jnp.concatenate(pieces, axis=0)

    turned = square(jnp.concatenate([stacked(master), stacked(slave)], axis=1))
    return turned[:devices], turned[devices : 2 * devices]


def unpack(master, slave, rows):
    devices = master.shape[0]
    turned = square(jnp.concatenate([master, slave], axis=0))

    def laid(first):
        pieces = [
            turned[k * rows : (k + 1) * rows, first : first + devices] for k in range(CAP)
        ]
        return jnp.concatenate(pieces, axis=1)

    return laid(0), laid(devices)


def put(ref, per, line, value):
    ref[pl.ds(line, value.shape[0], stride=per), :] = value


def get(ref, per, line):
    return ref[pl.ds(line, ref.shape[0] // per, stride=per), :]


def to_column(row, base, rows):
    spread = jnp.broadcast_to(row, (rows, LANES))
    here = iota((rows, LANES), 1) == iota((rows, LANES), 0) + base
    return jnp.sum(jnp.where(here, spread, 0.0), axis=1, keepdims=True)


def at_lanes(column, base):
    rows = column.shape[0]
    here = iota((rows, LANES), 1) == iota((rows, LANES), 0) + base
    return jnp.where(here, column, 0.0)


def fold(x):
    return sum(x[:, i : i + LANES] for i in range(0, x.shape[1], LANES))


def dots_row(pairs, base=0):
    total = 0.0
    for place, (left, right) in enumerate(pairs):
        acc = sum(fold(left[f] * right[f]) for f in range(left.shape[0]))
        column = jnp.sum(acc, axis=1, keepdims=True)
        total = total + at_lanes(column, base + place * column.shape[0])
    return jnp.sum(total, axis=0, keepdims=True)


def coefficients_row(field, basis):
    total = 0.0
    blocks, directions = field.shape[0], field.shape[1]
    for m in range(basis.shape[0]):
        acc = sum(fold(field[f] * basis[m, f : f + 1, :]) for f in range(blocks))
        total = total + at_lanes(jnp.sum(acc, axis=1, keepdims=True), m * directions)
    return jnp.sum(total, axis=0, keepdims=True)


def exact(x, unit):
    rows = x.shape[0]
    full = bdot(jnp.concatenate(thirds(x), axis=0), unit)
    return full[:rows] + (full[rows : 2 * rows] + full[2 * rows :])


def contact(mine, theirs, per_mine, per_theirs, a_high, a_low, unit):
    own = [get(mine, per_mine, i) for i in range(2)]
    other = [get(theirs, per_theirs, i) for i in range(2)]
    master, slave = unpack(own[0] + other[1], own[1] + other[0], LANES // CAP)
    return times(master, a_high[...], a_low[...]) + exact(slave, unit[...])


def send_contact(message, per, surface, t_high, t_low, unit_t):
    devices = message.shape[0] // per
    master = times(surface, t_high[...], t_low[...])
    slave = exact(surface, unit_t[...])
    for line, value in enumerate(pack(master, slave, devices)):
        put(message, per, line, value)


def spread_rows(message, per, line, row):
    put(message, per, line, jnp.broadcast_to(row, (message.shape[0] // per, LANES)))


def ranks(owner_row, active_row, count):
    rows = owner_row.shape[1]
    up, across = iota((rows, rows), 0), iota((rows, rows), 1)
    diagonal = up == across

    def column(row):
        return jnp.sum(jnp.where(diagonal, row, 0), axis=1, keepdims=True)

    live_row = jnp.where(iota((1, rows), 1) < count, active_row, 0)
    owner_col, live_col = column(owner_row), column(live_row)
    same = owner_col == owner_row
    rank_col = jnp.sum(jnp.where(same & (across < up), live_row, 0), axis=1, keepdims=True)
    rank_row = jnp.sum(jnp.where(same & (up < across), live_col, 0), axis=0, keepdims=True)
    return column, live_row, live_col, owner_col, rank_row, rank_col


def load_modes(basis, modes, blocks):
    return [
        jnp.concatenate([basis[m * blocks + f] for f in range(blocks)], axis=0)
        for m in range(modes)
    ]


def setup_kernel(blocks, count, owner, dofs, active, basis, message):
    devices = message.ref.shape[0]
    owner, dofs, active, basis = owner(), dofs(), active(), basis()
    rows = owner.shape[1]
    column, live_row, _, _, _, rank_col = ranks(owner[...], active[...], count[0])
    named = (iota((devices, rows), 0) == owner[...]) & (live_row > 0)
    slots = jnp.where(iota((rows, LANES), 1) == rank_col, column(dofs[...]) + 1, 0)
    lines = jnp.dot(
        jnp.where(named, 1.0, 0.0),
        slots.astype(F32),
        precision=lax.Precision.HIGHEST,
        preferred_element_type=F32,
    )
    modes = basis.shape[0] // blocks
    slabs = load_modes(basis, modes, blocks)
    lane = iota((1, LANES), 1)
    gram = jnp.zeros((1, LANES), F32)
    for i in range(modes):
        for j in range(i + 1):
            value = jnp.sum(fold(slabs[i] * slabs[j]), axis=0, keepdims=True)
            value = jnp.sum(value, axis=1, keepdims=True)
            gram = jnp.where(lane == LANES // 2 + 8 * i + j, value, gram)
    message.ref[...] = jnp.where(iota((devices, LANES), 1) < CAP, lines, gram)


def slots_kernel(
    devices, count, owner, active, mortar, start_rows, right_rows, a_high, a_low, t_high, t_low,
    start, right,
):
    owner, active = owner(), active()
    rows = owner.shape[1]
    width = CAP * devices
    _, live_row, live_col, owner_col, rank_row, rank_col = ranks(
        owner[...], active[...], count[0]
    )
    slot_row = jnp.where(live_row > 0, rank_row * devices + owner[...], -1)
    slot_col = jnp.where(live_col > 0, rank_col * devices + owner_col, -1)
    pick = jnp.where(iota((width, rows), 0) == slot_row, 1.0, 0.0).astype(BF16)
    pick_t = jnp.where(iota((rows, width), 1) == slot_col, 1.0, 0.0).astype(BF16)
    blocks, directions = start.ref.shape[0], start.ref.shape[1]
    for source, target in ((start_rows(), start), (right_rows(), right)):
        for f in range(blocks):
            for c in range(directions):
                target.ref[f, c : c + 1, :] = source[c * blocks + f]
        target.flush()
    for part, straight, turned in zip(
        halves(mortar()[...]), (a_high, a_low), (t_high, t_low), strict=True
    ):
        straight.ref[...] = bdot(pick, part).astype(BF16)
        straight.flush()
        turned.ref[...] = bdot(part.astype(F32).T.astype(BF16), pick_t).astype(BF16)
        turned.flush()


def first_kernel(
    organs, arrived, matches, basis, start, t_high, t_low, right, message, unit_t, unit,
    modes_out, *sends,
):
    devices = arrived.shape[0]
    subs = devices // organs
    blocks = len(sends)
    basis = basis()
    modes = basis.shape[0] // blocks
    length = basis.shape[2]
    dofs = arrived[...]
    turned = square(dofs)[:CAP, :devices]
    dof_row = jnp.concatenate([turned[k : k + 1, :] for k in range(CAP)], axis=1)
    place_t = iota((length, CAP * devices), 0).astype(F32) + 1.0
    unit_t.ref[...] = jnp.where(place_t == dof_row, -1.0, 0.0).astype(BF16)
    unit_t.flush()
    mine = lax.axis_index("organ") * subs
    total = jnp.sum(arrived[pl.ds(pl.multiple_of(mine, 8), subs), :], axis=0, keepdims=True)
    lane = iota((1, LANES), 1)

    def entry(i, j):
        here = lane == LANES // 2 + 8 * i + j
        return jnp.sum(jnp.where(here, total, 0.0), axis=1, keepdims=True)

    low, inverse = {}, {}
    for j in range(modes):
        pivot = entry(j, j) - sum(low[j, k] * low[j, k] for k in range(j))
        inverse[j, j] = 1.0 / jnp.sqrt(pivot)
        for i in range(j + 1, modes):
            value = entry(i, j) - sum(low[i, k] * low[j, k] for k in range(j))
            low[i, j] = value * inverse[j, j]
    for j in range(modes):
        for i in range(j + 1, modes):
            value = sum(low[i, k] * inverse[k, j] for k in range(j, i))
            inverse[i, j] = -inverse[i, i] * value
    slabs = load_modes(basis, modes, blocks)
    modes_ref = modes_out.ref
    for i in range(modes):
        modes_ref[i] = sum(inverse[i, j] * slabs[j] for j in range(i + 1))
    modes_out.flush()
    start, matches = start(), matches()
    directions = start.shape[1]
    for r in range(blocks):
        face = matches[r]
        send = sends[r].ref
        send[0:directions, :] = start[face]
        for m in range(modes):
            send[directions + m : directions + m + 1, :] = modes_ref[m, pl.ds(face, 1), :]
        for m in range(modes, 8):
            send[directions + m : directions + m + 1, :] = jnp.zeros((1, length), F32)
        sends[r].flush()
    first = [modes_ref[m, 0:1, :] for m in range(modes)]
    extra = jnp.zeros((2 * 16 - directions - modes, length), F32)
    both = jnp.concatenate([start[0]] + first + [extra], axis=0)
    master = times(both, t_high()[...], t_low()[...])
    slave = exact(both, unit_t.ref[...])
    for line, value in enumerate(pack(master[:directions], slave[:directions], devices)):
        put(message.ref, 4, line, value)
    rows = slice(directions, directions + 8)
    lines = pack(master[rows], slave[rows], devices)
    half = LANES // 2
    put(message.ref, 4, 2, jnp.concatenate([line[:, :half] for line in lines], axis=1))
    spread_rows(message.ref, 4, 3, coefficients_row(right(), modes_ref))
    message.flush()
    place = iota((devices, length), 1).astype(F32) + 1.0
    for k in range(CAP):
        block = jnp.where(place == dofs[:, k : k + 1], -1.0, 0.0).astype(BF16)
        unit.ref[k * devices : (k + 1) * devices, :] = block


def turned_dot(a, b):
    return lax.dot_general(a, b, (((1,), (1,)), ((), ())), preferred_element_type=F32)


def times_symmetric(x, parts, f):
    rows = x.shape[0]
    a, b = halves(x)
    stacked = jnp.concatenate([a, b], axis=0)
    pieces = []
    first = 0
    for part in parts:
        w_high, w_low = halves(part[f])
        depth, width = w_high.shape
        here = slice(first, first + depth)
        after = slice(first + depth, first + width)
        high, low = bdot(stacked[:, here], w_high), bdot(a[:, here], w_low)
        value = high[:rows] + (high[rows:] + low)
        pieces.append((first, value))
        if width > depth:
            high = turned_dot(stacked[:, after], w_high[:, depth:])
            low = turned_dot(a[:, after], w_low[:, depth:])
            pieces.append((first, high[:rows] + (high[rows:] + low)))
        first += depth
    bands = []
    edges = [0]
    for part in parts:
        edges.append(edges[-1] + part.shape[1])
    for start, stop in zip(edges[:-1], edges[1:], strict=True):
        total = 0.0
        for begin, value in pieces:
            if begin <= start and stop <= begin + value.shape[1]:
                total = total + value[:, start - begin : stop - begin]
        bands.append(total)
    return jnp.concatenate(bands, axis=1)


def smooth(inner, near, smoothed, f):
    smoothed[f] = times_symmetric(inner[f], near, f)


def subtract_modes(field, columns, basis, f):
    value = field
    for m, column in enumerate(columns):
        value = value - column * basis[m, f : f + 1, :]
    return value


def start_contact(
    organs, arrived, sent, start, a_high, a_low, unit, modes_ref, right, new_right,
    base, added,
):
    sent, start, maps = sent(), start(), (a_high(), a_low(), unit())
    devices = sent.shape[0] // 4
    subs = devices // organs
    blocks, directions = start.shape[0], start.shape[1]
    base[...] = start[...]
    base[0] += contact(sent, arrived, 4, 4, *maps)
    modes_ref, right = modes_ref(), right()
    organ = lax.axis_index("organ")
    block = arrived[pl.ds(pl.multiple_of(organ * subs * 4, 8), subs * 4), :]
    here = lax.rem(iota(block.shape, 0), 4) == 3
    row = jnp.sum(jnp.where(here, block, 0.0), axis=0, keepdims=True)
    columns = [to_column(row, m * directions, directions) for m in range(modes_ref.shape[0])]
    for f in range(blocks):
        new_right.ref[f] = subtract_modes(right[f], columns, modes_ref, f)
    new_right.flush()
    half = LANES // 2
    mine, other = get(sent, 4, 2), get(arrived, 4, 2)
    own_rows = unpack(mine[:, :half], mine[:, half:], 8)
    other_rows = unpack(other[:, half:], other[:, :half], 8)
    source = lax.rem(iota(own_rows[0].shape, 1), devices) // subs
    stacks = []
    for own_half, other_half in zip(own_rows, other_rows, strict=True):
        stack = []
        for o in range(organs):
            owns = jnp.where(organ == o, 1.0, 0.0)
            stack.append(jnp.where(source == o, other_half, 0.0) + owns * own_half)
        stacks.append(jnp.concatenate(stack, axis=0))
    added[...] = times(stacks[0], maps[0][...], maps[1][...]) + exact(stacks[1], maps[2][...])


def start_kernel(
    organs, bands, matches, f0, f1, f2, f3, f4, base, added, *refs
):
    near, rest = refs[:bands], refs[bands:]
    t_high, t_low, unit_t, modes_ref, message, smoothed_out, jump_out = rest[:7]
    s0, s1, s2, s3, s4, inner = rest[7:]
    faces = (f0, f1, f2, f3, f4)
    smoothed = smoothed_out.ref
    blocks, directions = base.shape[0], base.shape[1]
    for r, face in zip(ORDER, faces, strict=True):
        inner[matches[r]] = base[matches[r]] - face[0:directions, :]
    for f in range(blocks):
        smooth(inner, near, smoothed, f)
        if f == 0:
            send_contact(message.ref, 2, smoothed[0], t_high, t_low, unit_t)
            message.flush()
    for r, send in enumerate((s0, s1, s2, s3, s4)):
        send(smoothed.at[matches[r]])
    smoothed_out.flush()
    modes = modes_ref.shape[0]
    jump_modes = jump_out.ref
    organ = lax.axis_index("organ")
    jump_modes[...] = jnp.zeros(jump_modes.shape, F32)
    for r, values in zip(ORDER, faces, strict=True):
        face = matches[r]
        for m in range(modes):
            own = modes_ref[m, pl.ds(face, 1), :]
            other = values[directions + m : directions + m + 1, :]
            if r < SUB_ROUNDS:
                own = own - other
            else:
                partner = organ ^ (1 << (r - SUB_ROUNDS))
                jump_modes[face, pl.ds(m * organs + partner, 1), :] = -other
            jump_modes[face, pl.ds(m * organs + organ, 1), :] = own
    for o in range(organs):
        for m in range(modes):
            row = pl.ds(m * organs + o, 1)
            jump_modes[0, row, :] = jump_modes[0, row, :] + added[8 * o + m : 8 * o + m + 1, :]


def residual_contact(arrived, sent, smoothed, a_high, a_low, unit, right, part):
    sent, smoothed, right = sent(), smoothed(), right()
    part[...] = right[...] - smoothed[...]
    part[0] -= contact(sent, arrived, 2, 2, a_high(), a_low(), unit())


def residual_kernel(
    matches, f0, f1, f2, f3, f4, part, t_high, t_low, unit_t, modes_ref, message, resid, *sends
):
    for r, face in zip(ORDER, (f0, f1, f2, f3, f4), strict=True):
        resid.ref[matches[r]] = part[matches[r]] + face[...]
    send_residual(matches, resid, modes_ref, (t_high, t_low, unit_t), message, sends)


def send_residual(matches, resid, modes_ref, maps, message, sends):
    for r, send in enumerate(sends):
        send(resid.ref.at[matches[r]])
    resid.flush()
    send_contact(message.ref, 4, resid.ref[0], *maps)
    spread_rows(message.ref, 4, 2, coefficients_row(resid.ref, modes_ref))
    message.flush()


def inner_contact(
    organs, steps, arrived, sent, resid, a_high, a_low, unit, modes_ref, jump_modes, *refs
):
    rest = list(refs)
    if steps:
        start, behind, jumps, sizes = (
            rest[0],
            *(rest[1 + i * steps : 1 + (i + 1) * steps] for i in range(3)),
        )
        projected, total, direction, jumped, last_size, base, norms = rest[1 + 3 * steps :]
    else:
        projected_out, base, norms = rest
        projected = projected_out.ref
    sent, resid, maps = sent(), resid(), (a_high(), a_low(), unit())
    modes_ref, jump_modes = modes_ref(), jump_modes()
    devices = sent.shape[0] // 4
    subs = devices // organs
    blocks, directions = resid.shape[0], resid.shape[1]
    parts = get(arrived, 4, 2)
    sums = [
        jnp.sum(parts[o * subs : (o + 1) * subs], axis=0, keepdims=True) for o in range(organs)
    ]
    added = contact(sent, arrived, 4, 4, *maps)
    turned = square(jnp.concatenate(sums, axis=0))
    left = jnp.concatenate(
        [turned[m * directions : (m + 1) * directions, :organs] for m in range(8)], axis=1
    )
    organ = lax.axis_index("organ")
    own = sum(jnp.where(organ == o, 1.0, 0.0) * sums[o] for o in range(organs))
    columns = [to_column(own, m * directions, directions) for m in range(modes_ref.shape[0])]
    for f in range(blocks):
        projected[f] = subtract_modes(resid[f], columns, modes_ref, f)
    if not steps:
        projected_out.flush()
    for f in range(blocks):
        value = resid[f] - times_split(left, jump_modes[f])
        base[f] = value + added if f == 0 else value
    norms[...] = jnp.broadcast_to(dots_row([(projected, projected)]), norms.shape)
    if steps:
        start = start()
        behind, jumps, sizes = ([late() for late in group] for group in (behind, jumps, sizes))
        last_size[...] = sizes[-1][...]
        for f in range(blocks):
            value = behind[0][f]
            sum_up = start[f] + sizes[0][2, :, 0:1] * value
            for field, size in zip(behind[1:], sizes[1:], strict=True):
                value = field[f] + size[3, :, 0:1] * value
                sum_up = sum_up + size[2, :, 0:1] * value
            total[f] = sum_up
            direction[f] = value
            value = jumps[0][f]
            for field, size in zip(jumps[1:], sizes[1:], strict=True):
                value = field[f] + size[3, :, 0:1] * value
            jumped[f] = value


def inner_kernel(bands, last, older, matches, f0, f1, f2, f3, f4, base, norms, *refs):
    near, rest = refs[:bands], list(refs[bands:])
    previous = rest.pop(0) if older else None
    maps = None if last else rest[:3]
    message = rest[0 if last else 3]
    rest = rest[1 if last else 4 :]
    if last:
        inner, smoothed = rest
    else:
        inner_out, smoothed_out = rest[:2]
        inner, smoothed = inner_out.ref, smoothed_out.ref
    for r, face in zip(ORDER, (f0, f1, f2, f3, f4), strict=True):
        inner[matches[r]] = base[matches[r]] - face[...]
    if not last:
        inner_out.flush()
    for f in range(inner.shape[0]):
        smooth(inner, near, smoothed, f)
        if f == 0 and not last:
            send_contact(message.ref, 4, smoothed[0], *maps)
    if not last:
        for r, send in enumerate(rest[2:]):
            send(smoothed.at[matches[r]])
        smoothed_out.flush()
    directions = inner.shape[1]
    pairs = [(inner, smoothed)]
    if older:
        pairs.append((previous, smoothed))
    row = dots_row(pairs, directions) + norms[0:1, :]
    if last:
        message.ref[...] = jnp.broadcast_to(row, message.ref.shape)
    else:
        spread_rows(message.ref, 4, 2, row)


def step_sizes(row, older, scalars, directions):
    rho = to_column(row, 0, directions)
    curvature = to_column(row, directions, directions)
    if not older:
        return rho, None, curvature, rho / curvature
    cross = to_column(row, 2 * directions, directions)
    beta = rho / scalars[0, :, 0:1]
    curvature = curvature + beta * (2.0 * cross + beta * scalars[1, :, 0:1])
    return rho, beta, curvature, rho / curvature


def outer_contact(older, arrived, sent, smoothed, a_high, a_low, unit, projected, *refs):
    rest = list(refs)
    old_image = scalars = None
    if older:
        old_image, scalars, new_scalars, part, steps, image = rest
        old_image, scalars = old_image(), scalars()
    else:
        new_scalars, part, steps, image = rest
    sent, smoothed, projected = sent(), smoothed(), projected()
    blocks, directions = smoothed.shape[0], smoothed.shape[1]
    row = jnp.sum(get(arrived, 4, 2), axis=0, keepdims=True)
    rho, beta, curvature, step = step_sizes(row, older, scalars, directions)
    wide = (directions, LANES)
    for place, column in enumerate((rho, curvature, step) + ((beta,) if older else ())):
        new_scalars.ref[place] = jnp.broadcast_to(column, wide)
    new_scalars.flush()
    steps[...] = jnp.broadcast_to(step, wide)
    added = contact(sent, arrived, 4, 4, a_high(), a_low(), unit())
    for f in range(blocks):
        value = smoothed[f]
        if f == 0:
            value = value + added
        if older:
            value = value + beta * old_image[f]
        image[f] = value
        part[f] = projected[f] - step * value


def outer_kernel(older, matches, f0, f1, f2, f3, f4, part, steps, image, *refs):
    t_high, t_low, unit_t, modes_ref = refs[:4]
    rest = list(refs[4:])
    if older:
        message, resid = rest[:2]
        sends = rest[2:]
    else:
        message, resid, new_image = rest[:3]
        sends = rest[3:]
    step = steps[:, 0:1]
    for r, face in zip(ORDER, (f0, f1, f2, f3, f4), strict=True):
        resid.ref[matches[r]] = part[matches[r]] + step * face[...]
        if not older:
            new_image.ref[matches[r]] = image[matches[r]] - face[...]
    send_residual(matches, resid, modes_ref, (t_high, t_low, unit_t), message, sends)


def last_kernel(arrived, projected, old_direction, total, scalars, out):
    blocks, directions = projected.shape[0], projected.shape[1]
    row = jnp.sum(arrived[...], axis=0, keepdims=True)
    _, beta, _, step = step_sizes(row, True, scalars, directions)
    for f in range(blocks):
        value = total[f] + step * (projected[f] + beta * old_direction[f])
        for c in range(directions):
            out.ref[c * blocks + f] = value[c : c + 1]


class Late:
    def __init__(self, source, target, sem):
        self.target, self.waiting = target, True
        self.copy = pltpu.make_async_copy(source, target, sem)
        self.copy.start()

    def __call__(self):
        if self.waiting:
            self.copy.wait()
            self.waiting = False
        return self.target


class Send:
    def __init__(self, target, sem):
        self.target, self.sem, self.copy = target, sem, None

    def __call__(self, source):
        self.copy = pltpu.make_async_copy(source, self.target, self.sem)
        self.copy.start()


class Out:
    def __init__(self, ref, target, sem):
        self.ref = ref
        self.copy = pltpu.make_async_copy(ref, target, sem)
        self.started = False

    def flush(self):
        if not self.started:
            self.copy.start()
            self.started = True


def call(kernel, outs, args, late=(), smem=0, near=(), sends=(), scratch=(), bring=(), held=0):
    n_late, n_out, n_arg, n_near = len(late), len(outs), len(args), len(near)
    bring = [item if isinstance(item, tuple) else (item, item.shape, None) for item in bring]
    brought = [(shape, a.dtype) for a, shape, _ in bring]

    def body(*refs):
        refs = list(refs)

        def take(n):
            taken = refs[:n]
            del refs[:n]
            return taken

        given, sources, origins = take(n_arg), take(n_late), take(len(bring))
        targets, ports, close = take(n_out), take(len(sends)), take(n_near)
        goals = take(len(bring))
        buffers, results = take(n_late), take(n_out)
        extra = take(len(scratch))
        in_sem, bring_sem, out_sem = refs
        lates = [Late(s, b, in_sem.at[i]) for i, (s, b) in enumerate(zip(sources, buffers))]
        written = [Out(r, t, out_sem.at[i]) for i, (r, t) in enumerate(zip(results, targets))]
        posts = [Send(t, out_sem.at[n_out + i]) for i, t in enumerate(ports)]
        copies = []
        for i, (origin, goal) in enumerate(zip(origins, goals, strict=True)):
            first = bring[i][2]
            if first is not None:
                rows, columns = goal.shape[1], goal.shape[2]
                origin = origin.at[:, pl.ds(first, rows), pl.ds(first, columns)]
            copies.append(pltpu.make_async_copy(origin, goal, bring_sem.at[i]))
        for copy in copies:
            copy.start(priority=BRING)
        kernel(*given, *lates, *written, *posts, *close, *extra)
        for item in lates:
            item()
        for copy in copies:
            copy.wait()
        for item in written:
            item.flush()
        for item in written + posts:
            item.copy.wait()

    in_specs = [pl.BlockSpec(memory_space=pltpu.SMEM)] * smem
    in_specs += [pl.BlockSpec(memory_space=pltpu.VMEM)] * (n_arg - smem)
    remote = tuple(late) + tuple(a for a, _, _ in bring)
    in_specs += [pl.BlockSpec(memory_space=pltpu.HBM)] * len(remote)
    out_specs = [pl.BlockSpec(memory_space=pltpu.HBM)] * (n_out + len(sends))
    out_specs += [pl.BlockSpec(memory_space=pltpu.VMEM)] * (n_near + len(bring))
    scratch_shapes = [pltpu.SMEM(a.shape, a.dtype) for a in late[:held]]
    scratch_shapes += [pltpu.VMEM(a.shape, a.dtype) for a in late[held:]]
    scratch_shapes += [pltpu.VMEM(shape, kind) for shape, kind in outs]
    scratch_shapes += list(scratch)
    counts = (n_late, len(bring), n_out + len(sends))
    scratch_shapes += [pltpu.SemaphoreType.DMA((max(n, 1),)) for n in counts]
    return pl.pallas_call(
        body,
        out_shape=[pltpu.HBM(shape, kind) for shape, kind in tuple(outs) + tuple(sends)]
        + [pltpu.VMEM(shape, kind) for shape, kind in list(near) + brought],
        in_specs=in_specs,
        out_specs=out_specs,
        scratch_shapes=scratch_shapes,
        compiler_params=pltpu.CompilerParams(vmem_limit_bytes=VMEM_LIMIT),
        cost_estimate=pl.CostEstimate(flops=COST, bytes_accessed=COST, transcendentals=0),
    )(*args, *(pltpu.with_memory_space_constraint(a, pltpu.HBM) for a in remote))


def from_partner(value, axis, apart):
    mask = 2**apart
    pairs = [(source, source ^ mask) for source in range(lax.axis_size(axis))]
    return lax.ppermute(value, axis, pairs)


def exchange(message):
    return lax.all_to_all(message, AXES, split_axis=0, concat_axis=0, tiled=True)


def swap_faces(faces):
    swapped = []
    for r in ORDER:
        axis, apart = ("sub", r) if r < SUB_ROUNDS else ("organ", r - SUB_ROUNDS)
        swapped.append(from_partner(faces[r], axis, apart))
    return swapped


def local(
    dual_rhs, warm_start, inverse_blocks, coarse_basis, mortar_rows, match_rounds, slave_owner,
    slave_dofs, active_set, row_counts,
):
    directions, blocks, length = dual_rhs.shape[0], dual_rhs.shape[3], dual_rhs.shape[4]
    rows = mortar_rows.shape[2]
    modes = coarse_basis.shape[0]
    organs, subs = lax.axis_size("organ"), lax.axis_size("sub")
    devices = organs * subs
    width = CAP * devices
    field = (blocks, directions, length)
    right_rows = dual_rhs.reshape(directions * blocks, 1, length)
    start_rows = warm_start.reshape(directions * blocks, 1, length)
    matrices = inverse_blocks.reshape(blocks, length, length)
    basis = coarse_basis.reshape(modes * blocks, 1, length)
    mortar = mortar_rows.reshape(rows, length)
    matches = match_rounds.reshape(-1)
    owner = slave_owner.reshape(1, rows)
    dofs = slave_dofs.reshape(1, rows)
    active = active_set.reshape(1, rows)
    count = row_counts.reshape(1)
    face = ((directions, length), F32)
    whole = (field, F32)
    message_line = ((4 * devices, LANES), F32)

    sends = [face] * blocks
    near_matrices, first = [], 0
    while first < length:
        rows = min(BAND, length - first)
        near_matrices.append((matrices, (blocks, rows, length - first), first))
        first += rows
    near_matrices = tuple(near_matrices)
    bands = len(near_matrices)

    (setup,) = call(
        functools.partial(setup_kernel, blocks),
        [((devices, LANES), F32)],
        (count,),
        (owner, dofs, active, basis),
        smem=1,
    )
    arrived = exchange(setup)
    a_high, a_low, t_high, t_low, start, right = call(
        functools.partial(slots_kernel, devices),
        [((width, length), BF16)] * 2 + [((length, width), BF16)] * 2 + [whole] * 2,
        (count,),
        (owner, active, mortar, start_rows, right_rows),
        smem=1,
    )
    sent, unit_t, unit, modes_ref, *faces = call(
        functools.partial(first_kernel, organs),
        [
            message_line,
            ((length, width), BF16),
            ((width, length), BF16),
            ((modes, blocks, length), F32),
        ]
        + [((directions + 8, length), F32)] * blocks,
        (arrived,),
        (matches, basis, start, t_high, t_low, right),
        held=1,
    )
    forth = (a_high, a_low, unit)
    back = (t_high, t_low, unit_t)
    back_modes = back + (modes_ref,)
    arrived = exchange(sent)
    faces = swap_faces(faces)
    right, base, added, *more = call(
        functools.partial(start_contact, organs),
        [whole],
        (arrived,),
        (sent, start) + forth + (modes_ref, right),
        near=[whole, ((8 * organs, length), F32)],
        bring=near_matrices + back_modes,
    )
    message, smoothed, jump_modes, *posts = call(
        functools.partial(start_kernel, organs, bands),
        [((2 * devices, LANES), F32), whole, ((blocks, 8 * organs, length), F32)],
        (matches, *faces, base, added, *more),
        smem=1,
        sends=sends,
        scratch=[pltpu.VMEM(field, F32)],
    )
    arrived = exchange(message)
    faces = swap_faces(posts)
    part, *maps = call(
        residual_contact,
        [],
        (arrived,),
        (message, smoothed) + forth + (right,),
        near=[whole],
        bring=back_modes,
    )
    sent, resid, *posts = call(
        residual_kernel,
        [message_line, whole],
        (matches, *faces, part, *maps),
        smem=1,
        sends=sends,
    )
    image = None
    size = (4, directions, LANES)
    fields, jumps, scalars = [], [], []
    for step in range(ITERS):
        older, last = step > 0, step == ITERS - 1
        arrived = exchange(sent)
        faces = swap_faces(posts)
        history = (start, *fields, *jumps, *scalars) if last else ()
        more_near = [whole] * 3 + [(size, F32)] if last else []
        ahead = () if last else back
        if older and not last:
            ahead = (jumps[-1],) + ahead
        projected, *more = call(
            functools.partial(inner_contact, organs, step if last else 0),
            [] if last else [whole],
            (arrived,),
            (sent, resid) + forth + (modes_ref, jump_modes) + history,
            near=([whole] + more_near if last else []) + [whole, ((8, LANES), F32)],
            bring=near_matrices + ahead,
        )
        if last:
            total, direction, jumped, last_size, base, norms, *near = more
            (message,) = call(
                functools.partial(inner_kernel, bands, last, older),
                [((devices, LANES), F32)],
                (matches, *faces, base, norms, *near, jumped),
                smem=1,
                scratch=[pltpu.VMEM(field, F32)] * 2,
            )
            arrived = exchange(message)
            break
        message, inner, smoothed, *posts = call(
            functools.partial(inner_kernel, bands, last, older),
            [message_line, whole, whole],
            (matches, *faces, *more),
            smem=1,
            sends=sends,
        )
        arrived = exchange(message)
        faces = swap_faces(posts)
        old = (image, scalars[-1]) if older else ()
        new_scalars, *more = call(
            functools.partial(outer_contact, older),
            [(size, F32)],
            (arrived,),
            (message, smoothed) + forth + (projected,) + old,
            near=[whole, ((directions, LANES), F32), whole],
            bring=back_modes,
        )
        sent, resid, *posts = call(
            functools.partial(outer_kernel, older),
            [message_line, whole] + ([] if older else [whole]),
            (matches, *faces, *more),
            smem=1,
            sends=sends,
        )
        if not older:
            image, *posts = posts
        fields.append(projected)
        jumps.append(inner)
        scalars.append(new_scalars)
    (result,) = call(
        last_kernel,
        [((directions * blocks, 1, length), F32)],
        (arrived, projected, direction, total, last_size),
    )
    return result.reshape(dual_rhs.shape)


def solution(mesh):
    in_specs = (
        P(None, "organ", "sub", None, None),
        P(None, "organ", "sub", None, None),
        P("organ", "sub", None, None, None),
        P(None, "organ", "sub", None, None),
        P("organ", "sub", None, None),
        P("organ", "sub", None),
        P("organ", "sub", None, None),
        P("organ", "sub", None),
        P("organ", "sub", None),
        P("organ", "sub", None),
    )
    out_specs = P(None, "organ", "sub", None, None)
    return jax.shard_map(local, mesh=mesh, in_specs=in_specs, out_specs=out_specs, check_vma=False)
```

```python
import functools

import jax
import jax.numpy as jnp
from jax import lax
from jax.experimental import pallas as pl
from jax.experimental.pallas import tpu as pltpu
from jax.sharding import PartitionSpec as P

ITERS = 3
CAP = 8
SUB_ROUNDS = 3
ORDER = (2, 0, 1, 4, 3)
AXES = ("organ", "sub")
LANES = 128
F32 = jnp.float32
BF16 = jnp.bfloat16
VMEM_LIMIT = 24 * 2**20
COST = 2_000_000
BAND = 256


def iota(shape, dim):
    return lax.broadcasted_iota(jnp.int32, shape, dim)


def halves(x):
    high = x.astype(BF16)
    return high, (x - high.astype(F32)).astype(BF16)


def thirds(x):
    high = x.astype(BF16)
    rest = x - high.astype(F32)
    middle = rest.astype(BF16)
    return high, middle, (rest - middle.astype(F32)).astype(BF16)


def bdot(a, b):
    return jnp.dot(a, b, preferred_element_type=F32)


def turned_dot(a, b):
    return lax.dot_general(a, b, (((1,), (1,)), ((), ())), preferred_element_type=F32)


def times(x, w_high, w_low, dot=bdot):
    rows = x.shape[0]
    a, b, c = thirds(x)
    full = dot(jnp.concatenate([a, b, c], axis=0), w_high)
    part = dot(jnp.concatenate([a, b], axis=0), w_low)
    low = full[2 * rows :] + part[rows:]
    return full[:rows] + (full[rows : 2 * rows] + part[:rows] + low)


def times_split(x, w):
    rows = x.shape[0]
    a, b = halves(x)
    w_high, w_low = halves(w)
    full = bdot(jnp.concatenate([a, b], axis=0), w_high)
    return full[:rows] + (full[rows:] + bdot(a, w_low))


def square(x):
    rows, cols = x.shape
    if rows < LANES:
        x = jnp.concatenate([x, jnp.zeros((LANES - rows, cols), F32)], axis=0)
    if cols < LANES:
        x = jnp.concatenate([x, jnp.zeros((x.shape[0], LANES - cols), F32)], axis=1)
    return x.T


def pack(master, slave, devices):
    def stacked(x):
        pieces = [x[:, k * devices : (k + 1) * devices] for k in range(CAP)]
        return jnp.concatenate(pieces, axis=0)

    turned = square(jnp.concatenate([stacked(master), stacked(slave)], axis=1))
    return turned[:devices], turned[devices : 2 * devices]


def unpack(master, slave, rows):
    devices = master.shape[0]
    turned = square(jnp.concatenate([master, slave], axis=0))

    def laid(first):
        pieces = [
            turned[k * rows : (k + 1) * rows, first : first + devices] for k in range(CAP)
        ]
        return jnp.concatenate(pieces, axis=1)

    return laid(0), laid(devices)


def put(ref, per, line, value):
    ref[pl.ds(line, value.shape[0], stride=per), :] = value


def get(ref, per, line):
    return ref[pl.ds(line, ref.shape[0] // per, stride=per), :]


def to_column(row, base, rows):
    spread = jnp.broadcast_to(row, (rows, LANES))
    here = iota((rows, LANES), 1) == iota((rows, LANES), 0) + base
    return jnp.sum(jnp.where(here, spread, 0.0), axis=1, keepdims=True)


def at_lanes(column, base):
    rows = column.shape[0]
    here = iota((rows, LANES), 1) == iota((rows, LANES), 0) + base
    return jnp.where(here, column, 0.0)


def fold(x):
    return sum(x[:, i : i + LANES] for i in range(0, x.shape[1], LANES))


def dots_row(pairs, base=0):
    total = 0.0
    for place, (left, right) in enumerate(pairs):
        acc = sum(fold(left[f] * right[f]) for f in range(left.shape[0]))
        column = jnp.sum(acc, axis=1, keepdims=True)
        total = total + at_lanes(column, base + place * column.shape[0])
    return jnp.sum(total, axis=0, keepdims=True)


def coefficients_row(field, basis):
    total = 0.0
    blocks, directions = field.shape[0], field.shape[1]
    for m in range(basis.shape[0]):
        acc = sum(fold(field[f] * basis[m, f : f + 1, :]) for f in range(blocks))
        total = total + at_lanes(jnp.sum(acc, axis=1, keepdims=True), m * directions)
    return jnp.sum(total, axis=0, keepdims=True)


def exact(x, unit, dot=bdot):
    rows = x.shape[0]
    full = dot(jnp.concatenate(thirds(x), axis=0), unit)
    return full[:rows] + (full[rows : 2 * rows] + full[2 * rows :])


def contact(mine, theirs, per_mine, per_theirs, a_high, a_low, unit):
    own = [get(mine, per_mine, i) for i in range(2)]
    other = [get(theirs, per_theirs, i) for i in range(2)]
    master, slave = unpack(own[0] + other[1], own[1] + other[0], LANES // CAP)
    return times(master, a_high[...], a_low[...]) + exact(slave, unit[...])


def send_contact(message, per, surface, a_high, a_low, unit):
    devices = message.shape[0] // per
    master = times(surface, a_high[...], a_low[...], turned_dot)
    slave = exact(surface, unit[...], turned_dot)
    for line, value in enumerate(pack(master, slave, devices)):
        put(message, per, line, value)


def spread_rows(message, per, line, row):
    put(message, per, line, jnp.broadcast_to(row, (message.shape[0] // per, LANES)))


def ranks(owner_row, active_row, count):
    rows = owner_row.shape[1]
    up, across = iota((rows, rows), 0), iota((rows, rows), 1)
    diagonal = up == across

    def column(row):
        return jnp.sum(jnp.where(diagonal, row, 0), axis=1, keepdims=True)

    live_row = jnp.where(iota((1, rows), 1) < count, active_row, 0)
    owner_col, live_col = column(owner_row), column(live_row)
    same = owner_col == owner_row
    rank_col = jnp.sum(jnp.where(same & (across < up), live_row, 0), axis=1, keepdims=True)
    rank_row = jnp.sum(jnp.where(same & (up < across), live_col, 0), axis=0, keepdims=True)
    return column, live_row, rank_row, rank_col


def load_modes(basis, modes, blocks):
    return [
        jnp.concatenate([basis[m * blocks + f] for f in range(blocks)], axis=0)
        for m in range(modes)
    ]


def setup_kernel(blocks, count, owner, dofs, active, basis, message):
    devices = message.ref.shape[0]
    owner, dofs, active, basis = owner(), dofs(), active(), basis()
    rows = owner.shape[1]
    column, live_row, _, rank_col = ranks(owner[...], active[...], count[0])
    named = (iota((devices, rows), 0) == owner[...]) & (live_row > 0)
    slots = jnp.where(iota((rows, LANES), 1) == rank_col, column(dofs[...]) + 1, 0)
    lines = jnp.dot(
        jnp.where(named, 1.0, 0.0),
        slots.astype(F32),
        precision=lax.Precision.HIGHEST,
        preferred_element_type=F32,
    )
    modes = basis.shape[0] // blocks
    slabs = load_modes(basis, modes, blocks)
    lane = iota((1, LANES), 1)
    gram = jnp.zeros((1, LANES), F32)
    for i in range(modes):
        for j in range(i + 1):
            value = jnp.sum(fold(slabs[i] * slabs[j]), axis=0, keepdims=True)
            value = jnp.sum(value, axis=1, keepdims=True)
            gram = jnp.where(lane == LANES // 2 + 8 * i + j, value, gram)
    message.ref[...] = jnp.where(iota((devices, LANES), 1) < CAP, lines, gram)


def slots_kernel(
    devices, count, owner, active, mortar, start_rows, right_rows, a_high, a_low, start, right
):
    owner, active = owner(), active()
    rows = owner.shape[1]
    width = CAP * devices
    _, live_row, rank_row, _ = ranks(owner[...], active[...], count[0])
    slot_row = jnp.where(live_row > 0, rank_row * devices + owner[...], -1)
    pick = jnp.where(iota((width, rows), 0) == slot_row, 1.0, 0.0).astype(BF16)
    blocks, directions = start.ref.shape[0], start.ref.shape[1]
    for source, target in ((start_rows(), start), (right_rows(), right)):
        for f in range(blocks):
            for c in range(directions):
                target.ref[f, c : c + 1, :] = source[c * blocks + f]
        target.flush()
    for part, target in zip(halves(mortar()[...]), (a_high, a_low), strict=True):
        target.ref[...] = bdot(pick, part).astype(BF16)
        target.flush()


def first_kernel(
    organs, arrived, matches, basis, start, a_high, a_low, right, message, unit, modes_out, *sends
):
    devices = arrived.shape[0]
    subs = devices // organs
    blocks = len(sends)
    basis = basis()
    modes = basis.shape[0] // blocks
    length = basis.shape[2]
    dofs = arrived[...]
    place = iota((devices, length), 1).astype(F32) + 1.0
    for k in range(CAP):
        block = jnp.where(place == dofs[:, k : k + 1], -1.0, 0.0).astype(BF16)
        unit.ref[k * devices : (k + 1) * devices, :] = block
    unit.flush()
    mine = lax.axis_index("organ") * subs
    total = jnp.sum(arrived[pl.ds(pl.multiple_of(mine, 8), subs), :], axis=0, keepdims=True)
    lane = iota((1, LANES), 1)

    def entry(i, j):
        here = lane == LANES // 2 + 8 * i + j
        return jnp.sum(jnp.where(here, total, 0.0), axis=1, keepdims=True)

    low, inverse = {}, {}
    for j in range(modes):
        pivot = entry(j, j) - sum(low[j, k] * low[j, k] for k in range(j))
        inverse[j, j] = 1.0 / jnp.sqrt(pivot)
        for i in range(j + 1, modes):
            value = entry(i, j) - sum(low[i, k] * low[j, k] for k in range(j))
            low[i, j] = value * inverse[j, j]
    for j in range(modes):
        for i in range(j + 1, modes):
            value = sum(low[i, k] * inverse[k, j] for k in range(j, i))
            inverse[i, j] = -inverse[i, i] * value
    slabs = load_modes(basis, modes, blocks)
    modes_ref = modes_out.ref
    for i in range(modes):
        modes_ref[i] = sum(inverse[i, j] * slabs[j] for j in range(i + 1))
    modes_out.flush()
    start, matches = start(), matches()
    directions = start.shape[1]
    for r in range(blocks):
        face = matches[r]
        send = sends[r].ref
        send[0:directions, :] = start[face]
        for m in range(modes):
            send[directions + m : directions + m + 1, :] = modes_ref[m, pl.ds(face, 1), :]
        for m in range(modes, 8):
            send[directions + m : directions + m + 1, :] = jnp.zeros((1, length), F32)
        sends[r].flush()
    first = [modes_ref[m, 0:1, :] for m in range(modes)]
    extra = jnp.zeros((2 * 16 - directions - modes, length), F32)
    both = jnp.concatenate([start[0]] + first + [extra], axis=0)
    master = times(both, a_high()[...], a_low()[...], turned_dot)
    slave = exact(both, unit.ref[...], turned_dot)
    for line, value in enumerate(pack(master[:directions], slave[:directions], devices)):
        put(message.ref, 4, line, value)
    rows = slice(directions, directions + 8)
    lines = pack(master[rows], slave[rows], devices)
    half = LANES // 2
    put(message.ref, 4, 2, jnp.concatenate([line[:, :half] for line in lines], axis=1))
    spread_rows(message.ref, 4, 3, coefficients_row(right(), modes_ref))
    message.flush()


def times_symmetric(x, parts, f):
    rows = x.shape[0]
    a, b = halves(x)
    stacked = jnp.concatenate([a, b], axis=0)
    pieces = []
    first = 0
    for part in parts:
        w_high, w_low = halves(part[f])
        depth, width = w_high.shape
        here = slice(first, first + depth)
        after = slice(first + depth, first + width)
        high, low = bdot(stacked[:, here], w_high), bdot(a[:, here], w_low)
        value = high[:rows] + (high[rows:] + low)
        pieces.append((first, value))
        if width > depth:
            high = turned_dot(stacked[:, after], w_high[:, depth:])
            low = turned_dot(a[:, after], w_low[:, depth:])
            pieces.append((first, high[:rows] + (high[rows:] + low)))
        first += depth
    bands = []
    edges = [0]
    for part in parts:
        edges.append(edges[-1] + part.shape[1])
    for start, stop in zip(edges[:-1], edges[1:], strict=True):
        total = 0.0
        for begin, value in pieces:
            if begin <= start and stop <= begin + value.shape[1]:
                total = total + value[:, start - begin : stop - begin]
        bands.append(total)
    return jnp.concatenate(bands, axis=1)


def smooth(inner, near, smoothed, f):
    smoothed[f] = times_symmetric(inner[f], near, f)


def subtract_modes(field, columns, basis, f):
    value = field
    for m, column in enumerate(columns):
        value = value - column * basis[m, f : f + 1, :]
    return value


def start_contact(
    organs, arrived, sent, start, right, a_high, a_low, unit, modes_ref, new_right, base, added
):
    sent, start, maps = sent(), start(), (a_high(), a_low(), unit())
    devices = sent.shape[0] // 4
    subs = devices // organs
    blocks, directions = start.shape[0], start.shape[1]
    base[...] = start[...]
    base[0] += contact(sent, arrived, 4, 4, *maps)
    modes_ref, right = modes_ref(), right()
    organ = lax.axis_index("organ")
    block = arrived[pl.ds(pl.multiple_of(organ * subs * 4, 8), subs * 4), :]
    here = lax.rem(iota(block.shape, 0), 4) == 3
    row = jnp.sum(jnp.where(here, block, 0.0), axis=0, keepdims=True)
    columns = [to_column(row, m * directions, directions) for m in range(modes_ref.shape[0])]
    for f in range(blocks):
        new_right.ref[f] = subtract_modes(right[f], columns, modes_ref, f)
    new_right.flush()
    half = LANES // 2
    mine, other = get(sent, 4, 2), get(arrived, 4, 2)
    own_rows = unpack(mine[:, :half], mine[:, half:], 8)
    other_rows = unpack(other[:, half:], other[:, :half], 8)
    source = lax.rem(iota(own_rows[0].shape, 1), devices) // subs
    stacks = []
    for own_half, other_half in zip(own_rows, other_rows, strict=True):
        stack = []
        for o in range(organs):
            owns = jnp.where(organ == o, 1.0, 0.0)
            stack.append(jnp.where(source == o, other_half, 0.0) + owns * own_half)
        stacks.append(jnp.concatenate(stack, axis=0))
    added[...] = times(stacks[0], maps[0][...], maps[1][...]) + exact(stacks[1], maps[2][...])


def start_kernel(
    organs, bands, matches, f0, f1, f2, f3, f4, base, added, a_high, a_low, unit, modes_ref, *refs
):
    near, rest = refs[:bands], refs[bands:]
    message, smoothed_out, jump_out, s0, s1, s2, s3, s4, inner = rest
    faces = (f0, f1, f2, f3, f4)
    smoothed = smoothed_out.ref
    blocks, directions = base.shape[0], base.shape[1]
    for r, face in zip(ORDER, faces, strict=True):
        inner[matches[r]] = base[matches[r]] - face[0:directions, :]
    for f in range(blocks):
        smooth(inner, near, smoothed, f)
        if f == 0:
            send_contact(message.ref, 2, smoothed[0], a_high, a_low, unit)
            message.flush()
    for r, send in enumerate((s0, s1, s2, s3, s4)):
        send(smoothed.at[matches[r]])
    smoothed_out.flush()
    modes = modes_ref.shape[0]
    jump_modes = jump_out.ref
    organ = lax.axis_index("organ")
    jump_modes[...] = jnp.zeros(jump_modes.shape, F32)
    for r, values in zip(ORDER, faces, strict=True):
        face = matches[r]
        for m in range(modes):
            own = modes_ref[m, pl.ds(face, 1), :]
            other = values[directions + m : directions + m + 1, :]
            if r < SUB_ROUNDS:
                own = own - other
            else:
                partner = organ ^ (1 << (r - SUB_ROUNDS))
                jump_modes[face, pl.ds(m * organs + partner, 1), :] = -other
            jump_modes[face, pl.ds(m * organs + organ, 1), :] = own
    for o in range(organs):
        for m in range(modes):
            row = pl.ds(m * organs + o, 1)
            jump_modes[0, row, :] = jump_modes[0, row, :] + added[8 * o + m : 8 * o + m + 1, :]


def residual_contact(arrived, sent, smoothed, right, a_high, a_low, unit, part):
    sent, smoothed, right = sent(), smoothed(), right()
    part[...] = right[...] - smoothed[...]
    part[0] -= contact(sent, arrived, 2, 2, a_high(), a_low(), unit())


def residual_kernel(
    matches, f0, f1, f2, f3, f4, part, a_high, a_low, unit, modes_ref, message, resid, *sends
):
    for r, face in zip(ORDER, (f0, f1, f2, f3, f4), strict=True):
        resid.ref[matches[r]] = part[matches[r]] + face[...]
    send_residual(matches, resid, modes_ref, (a_high, a_low, unit), message, sends)


def send_residual(matches, resid, modes_ref, maps, message, sends):
    for r, send in enumerate(sends):
        send(resid.ref.at[matches[r]])
    resid.flush()
    send_contact(message.ref, 4, resid.ref[0], *maps)
    spread_rows(message.ref, 4, 2, coefficients_row(resid.ref, modes_ref))
    message.flush()


def inner_contact(
    organs, steps, arrived, sent, resid, modes_ref, jump_modes, *refs
):
    rest = list(refs)
    a_high, a_low, unit = (rest.pop(0) for _ in range(3))
    if steps:
        start, behind, jumps, sizes = (
            rest[0],
            *(rest[1 + i * steps : 1 + (i + 1) * steps] for i in range(3)),
        )
        projected, total, direction, jumped, last_size, base, norms = rest[1 + 3 * steps :]
    else:
        projected_out, base, norms = rest
        projected = projected_out.ref
    sent, resid, maps = sent(), resid(), (a_high(), a_low(), unit())
    modes_ref, jump_modes = modes_ref(), jump_modes()
    devices = sent.shape[0] // 4
    subs = devices // organs
    blocks, directions = resid.shape[0], resid.shape[1]
    parts = get(arrived, 4, 2)
    sums = [
        jnp.sum(parts[o * subs : (o + 1) * subs], axis=0, keepdims=True) for o in range(organs)
    ]
    added = contact(sent, arrived, 4, 4, *maps)
    turned = square(jnp.concatenate(sums, axis=0))
    left = jnp.concatenate(
        [turned[m * directions : (m + 1) * directions, :organs] for m in range(8)], axis=1
    )
    organ = lax.axis_index("organ")
    own = sum(jnp.where(organ == o, 1.0, 0.0) * sums[o] for o in range(organs))
    columns = [to_column(own, m * directions, directions) for m in range(modes_ref.shape[0])]
    for f in range(blocks):
        projected[f] = subtract_modes(resid[f], columns, modes_ref, f)
    if not steps:
        projected_out.flush()
    for f in range(blocks):
        value = resid[f] - times_split(left, jump_modes[f])
        base[f] = value + added if f == 0 else value
    norms[...] = jnp.broadcast_to(dots_row([(projected, projected)]), norms.shape)
    if steps:
        start = start()
        behind, jumps, sizes = ([late() for late in group] for group in (behind, jumps, sizes))
        last_size[...] = sizes[-1][...]
        for f in range(blocks):
            value = behind[0][f]
            sum_up = start[f] + sizes[0][2, :, 0:1] * value
            for field, size in zip(behind[1:], sizes[1:], strict=True):
                value = field[f] + size[3, :, 0:1] * value
                sum_up = sum_up + size[2, :, 0:1] * value
            total[f] = sum_up
            direction[f] = value
            value = jumps[0][f]
            for field, size in zip(jumps[1:], sizes[1:], strict=True):
                value = field[f] + size[3, :, 0:1] * value
            jumped[f] = value


def inner_kernel(bands, last, older, matches, f0, f1, f2, f3, f4, base, norms, *refs):
    maps, rest = (None, refs) if last else (refs[:3], refs[3:])
    near, rest = rest[:bands], list(rest[bands:])
    previous = rest.pop(0) if older else None
    message = rest.pop(0)
    if last:
        inner, smoothed = rest
    else:
        inner_out, smoothed_out = rest[:2]
        inner, smoothed = inner_out.ref, smoothed_out.ref
    for r, face in zip(ORDER, (f0, f1, f2, f3, f4), strict=True):
        inner[matches[r]] = base[matches[r]] - face[...]
    if not last:
        inner_out.flush()
    for f in range(inner.shape[0]):
        smooth(inner, near, smoothed, f)
        if f == 0 and not last:
            send_contact(message.ref, 4, smoothed[0], *maps)
    if not last:
        for r, send in enumerate(rest[2:]):
            send(smoothed.at[matches[r]])
        smoothed_out.flush()
    directions = inner.shape[1]
    pairs = [(inner, smoothed)]
    if older:
        pairs.append((previous, smoothed))
    row = dots_row(pairs, directions) + norms[0:1, :]
    if last:
        message.ref[...] = jnp.broadcast_to(row, message.ref.shape)
    else:
        spread_rows(message.ref, 4, 2, row)


def step_sizes(row, older, scalars, directions):
    rho = to_column(row, 0, directions)
    curvature = to_column(row, directions, directions)
    if not older:
        return rho, None, curvature, rho / curvature
    cross = to_column(row, 2 * directions, directions)
    beta = rho / scalars[0, :, 0:1]
    curvature = curvature + beta * (2.0 * cross + beta * scalars[1, :, 0:1])
    return rho, beta, curvature, rho / curvature


def outer_contact(older, arrived, sent, smoothed, projected, *refs):
    rest = list(refs)
    old_image = scalars = None
    if older:
        old_image, scalars = rest[0](), rest[1]()
        rest = rest[2:]
    a_high, a_low, unit, new_scalars, part, steps, image = rest
    sent, smoothed, projected = sent(), smoothed(), projected()
    blocks, directions = smoothed.shape[0], smoothed.shape[1]
    row = jnp.sum(get(arrived, 4, 2), axis=0, keepdims=True)
    rho, beta, curvature, step = step_sizes(row, older, scalars, directions)
    wide = (directions, LANES)
    for place, column in enumerate((rho, curvature, step) + ((beta,) if older else ())):
        new_scalars.ref[place] = jnp.broadcast_to(column, wide)
    new_scalars.flush()
    steps[...] = jnp.broadcast_to(step, wide)
    added = contact(sent, arrived, 4, 4, a_high(), a_low(), unit())
    for f in range(blocks):
        value = smoothed[f]
        if f == 0:
            value = value + added
        if older:
            value = value + beta * old_image[f]
        image[f] = value
        part[f] = projected[f] - step * value


def outer_kernel(older, matches, f0, f1, f2, f3, f4, part, steps, image, *refs):
    a_high, a_low, unit, modes_ref = refs[:4]
    rest = list(refs[4:])
    if older:
        message, resid = rest[:2]
        sends = rest[2:]
    else:
        message, resid, new_image = rest[:3]
        sends = rest[3:]
    step = steps[:, 0:1]
    for r, face in zip(ORDER, (f0, f1, f2, f3, f4), strict=True):
        resid.ref[matches[r]] = part[matches[r]] + step * face[...]
        if not older:
            new_image.ref[matches[r]] = image[matches[r]] - face[...]
    send_residual(matches, resid, modes_ref, (a_high, a_low, unit), message, sends)


def last_kernel(arrived, projected, old_direction, total, scalars, out):
    blocks, directions = projected.shape[0], projected.shape[1]
    row = jnp.sum(arrived[...], axis=0, keepdims=True)
    _, beta, _, step = step_sizes(row, True, scalars, directions)
    for f in range(blocks):
        value = total[f] + step * (projected[f] + beta * old_direction[f])
        for c in range(directions):
            out.ref[c * blocks + f] = value[c : c + 1]


class Late:
    def __init__(self, source, target, sem, priority=0):
        self.target, self.waiting, self.priority = target, True, priority
        self.copy = pltpu.make_async_copy(source, target, sem)

    def start(self):
        self.copy.start(priority=self.priority)

    def __call__(self):
        if self.waiting:
            self.copy.wait()
            self.waiting = False
        return self.target


class Send:
    def __init__(self, target, sem):
        self.target, self.sem, self.copy = target, sem, None

    def __call__(self, source):
        self.copy = pltpu.make_async_copy(source, self.target, self.sem)
        self.copy.start()


class Out:
    def __init__(self, ref, target, sem):
        self.ref = ref
        self.copy = pltpu.make_async_copy(ref, target, sem)
        self.started = False

    def flush(self):
        if not self.started:
            self.copy.start()
            self.started = True


def call(kernel, outs, args, late=(), smem=0, near=(), sends=(), scratch=(), bring=(), held=0, shared=0):
    n_late, n_out, n_arg, n_near = len(late), len(outs), len(args), len(near)
    bring = [item if isinstance(item, tuple) else (item, item.shape, None) for item in bring]
    brought = [(shape, a.dtype) for a, shape, _ in bring]

    def body(*refs):
        refs = list(refs)

        def take(n):
            taken = refs[:n]
            del refs[:n]
            return taken

        given, sources, origins = take(n_arg), take(n_late), take(len(bring))
        targets, ports, close = take(n_out), take(len(sends)), take(n_near)
        goals = take(len(bring))
        buffers, results = take(n_late), take(n_out)
        extra = take(len(scratch))
        in_sem, bring_sem, out_sem = refs
        copies = []
        for i, (origin, goal) in enumerate(zip(origins, goals, strict=True)):
            first = bring[i][2]
            if first is not None:
                rows, columns = goal.shape[1], goal.shape[2]
                origin = origin.at[:, pl.ds(first, rows), pl.ds(first, columns)]
            copies.append(Late(origin, goal, bring_sem.at[i], 0 if i < shared else 1))
        lates = [Late(s, b, in_sem.at[i]) for i, (s, b) in enumerate(zip(sources, buffers))]
        for item in copies[:shared] + lates + copies[shared:]:
            item.start()
        written = [Out(r, t, out_sem.at[i]) for i, (r, t) in enumerate(zip(results, targets))]
        posts = [Send(t, out_sem.at[n_out + i]) for i, t in enumerate(ports)]
        kernel(*given, *lates, *copies[:shared], *written, *posts, *close, *extra)
        for item in lates + copies:
            item()
        for item in written:
            item.flush()
        for item in written + posts:
            item.copy.wait()

    in_specs = [pl.BlockSpec(memory_space=pltpu.SMEM)] * smem
    in_specs += [pl.BlockSpec(memory_space=pltpu.VMEM)] * (n_arg - smem)
    remote = tuple(late) + tuple(a for a, _, _ in bring)
    in_specs += [pl.BlockSpec(memory_space=pltpu.HBM)] * len(remote)
    out_specs = [pl.BlockSpec(memory_space=pltpu.HBM)] * (n_out + len(sends))
    out_specs += [pl.BlockSpec(memory_space=pltpu.VMEM)] * (n_near + len(bring))
    scratch_shapes = [pltpu.SMEM(a.shape, a.dtype) for a in late[:held]]
    scratch_shapes += [pltpu.VMEM(a.shape, a.dtype) for a in late[held:]]
    scratch_shapes += [pltpu.VMEM(shape, kind) for shape, kind in outs]
    scratch_shapes += list(scratch)
    counts = (n_late, len(bring), n_out + len(sends))
    scratch_shapes += [pltpu.SemaphoreType.DMA((max(n, 1),)) for n in counts]
    return pl.pallas_call(
        body,
        out_shape=[pltpu.HBM(shape, kind) for shape, kind in tuple(outs) + tuple(sends)]
        + [pltpu.VMEM(shape, kind) for shape, kind in list(near) + brought],
        in_specs=in_specs,
        out_specs=out_specs,
        scratch_shapes=scratch_shapes,
        compiler_params=pltpu.CompilerParams(vmem_limit_bytes=VMEM_LIMIT),
        cost_estimate=pl.CostEstimate(flops=COST, bytes_accessed=COST, transcendentals=0),
    )(*args, *(pltpu.with_memory_space_constraint(a, pltpu.HBM) for a in remote))


def from_partner(value, axis, apart):
    mask = 2**apart
    pairs = [(source, source ^ mask) for source in range(lax.axis_size(axis))]
    return lax.ppermute(value, axis, pairs)


def exchange(message):
    return lax.all_to_all(message, AXES, split_axis=0, concat_axis=0, tiled=True)


def swap_faces(faces):
    swapped = []
    for r in ORDER:
        axis, apart = ("sub", r) if r < SUB_ROUNDS else ("organ", r - SUB_ROUNDS)
        swapped.append(from_partner(faces[r], axis, apart))
    return swapped


def local(
    dual_rhs, warm_start, inverse_blocks, coarse_basis, mortar_rows, match_rounds, slave_owner,
    slave_dofs, active_set, row_counts,
):
    directions, blocks, length = dual_rhs.shape[0], dual_rhs.shape[3], dual_rhs.shape[4]
    rows = mortar_rows.shape[2]
    modes = coarse_basis.shape[0]
    organs, subs = lax.axis_size("organ"), lax.axis_size("sub")
    devices = organs * subs
    width = CAP * devices
    field = (blocks, directions, length)
    right_rows = dual_rhs.reshape(directions * blocks, 1, length)
    start_rows = warm_start.reshape(directions * blocks, 1, length)
    matrices = inverse_blocks.reshape(blocks, length, length)
    basis = coarse_basis.reshape(modes * blocks, 1, length)
    mortar = mortar_rows.reshape(rows, length)
    matches = match_rounds.reshape(-1)
    owner = slave_owner.reshape(1, rows)
    dofs = slave_dofs.reshape(1, rows)
    active = active_set.reshape(1, rows)
    count = row_counts.reshape(1)
    face = ((directions, length), F32)
    whole = (field, F32)
    message_line = ((4 * devices, LANES), F32)

    sends = [face] * blocks
    near_matrices, first = [], 0
    while first < length:
        rows = min(BAND, length - first)
        near_matrices.append((matrices, (blocks, rows, length - first), first))
        first += rows
    near_matrices = tuple(near_matrices)
    bands = len(near_matrices)

    (setup,) = call(
        functools.partial(setup_kernel, blocks),
        [((devices, LANES), F32)],
        (count,),
        (owner, dofs, active, basis),
        smem=1,
    )
    arrived = exchange(setup)
    a_high, a_low, start, right = call(
        functools.partial(slots_kernel, devices),
        [((width, length), BF16)] * 2 + [whole] * 2,
        (count,),
        (owner, active, mortar, start_rows, right_rows),
        smem=1,
    )
    sent, unit, modes_ref, *faces = call(
        functools.partial(first_kernel, organs),
        [
            message_line,
            ((width, length), BF16),
            ((modes, blocks, length), F32),
        ]
        + [((directions + 8, length), F32)] * blocks,
        (arrived,),
        (matches, basis, start, a_high, a_low, right),
        held=1,
    )
    maps = (a_high, a_low, unit)
    arrived = exchange(sent)
    faces = swap_faces(faces)
    right, base, added, *more = call(
        functools.partial(start_contact, organs),
        [whole],
        (arrived,),
        (sent, start, right),
        near=[whole, ((8 * organs, length), F32)],
        bring=maps + (modes_ref,) + near_matrices,
        shared=4,
    )
    message, smoothed, jump_modes, *posts = call(
        functools.partial(start_kernel, organs, bands),
        [((2 * devices, LANES), F32), whole, ((blocks, 8 * organs, length), F32)],
        (matches, *faces, base, added, *more),
        smem=1,
        sends=sends,
        scratch=[pltpu.VMEM(field, F32)],
    )
    arrived = exchange(message)
    faces = swap_faces(posts)
    part, *more = call(
        residual_contact,
        [],
        (arrived,),
        (message, smoothed, right),
        near=[whole],
        bring=maps + (modes_ref,),
        shared=3,
    )
    sent, resid, *posts = call(
        residual_kernel,
        [message_line, whole],
        (matches, *faces, part, *more),
        smem=1,
        sends=sends,
    )
    image = None
    size = (4, directions, LANES)
    fields, jumps, scalars = [], [], []
    for step in range(ITERS):
        older, last = step > 0, step == ITERS - 1
        arrived = exchange(sent)
        faces = swap_faces(posts)
        history = (start, *fields, *jumps, *scalars) if last else ()
        more_near = [whole] * 3 + [(size, F32)] if last else []
        ahead = (jumps[-1],) if older and not last else ()
        projected, *more = call(
            functools.partial(inner_contact, organs, step if last else 0),
            [] if last else [whole],
            (arrived,),
            (sent, resid, modes_ref, jump_modes) + (maps if last else ()) + history,
            near=([whole] + more_near if last else []) + [whole, ((8, LANES), F32)],
            bring=(() if last else maps) + near_matrices + ahead,
            shared=0 if last else 3,
        )
        if last:
            total, direction, jumped, last_size, base, norms, *near = more
            (message,) = call(
                functools.partial(inner_kernel, bands, last, older),
                [((devices, LANES), F32)],
                (matches, *faces, base, norms, *near, jumped),
                smem=1,
                scratch=[pltpu.VMEM(field, F32)] * 2,
            )
            arrived = exchange(message)
            break
        message, inner, smoothed, *posts = call(
            functools.partial(inner_kernel, bands, last, older),
            [message_line, whole, whole],
            (matches, *faces, *more),
            smem=1,
            sends=sends,
        )
        arrived = exchange(message)
        faces = swap_faces(posts)
        old = (image, scalars[-1]) if older else ()
        new_scalars, *more = call(
            functools.partial(outer_contact, older),
            [(size, F32)],
            (arrived,),
            (message, smoothed, projected) + old,
            near=[whole, ((directions, LANES), F32), whole],
            bring=maps + (modes_ref,),
            shared=3,
        )
        sent, resid, *posts = call(
            functools.partial(outer_kernel, older),
            [message_line, whole] + ([] if older else [whole]),
            (matches, *faces, *more),
            smem=1,
            sends=sends,
        )
        if not older:
            image, *posts = posts
        fields.append(projected)
        jumps.append(inner)
        scalars.append(new_scalars)
    (result,) = call(
        last_kernel,
        [((directions * blocks, 1, length), F32)],
        (arrived, projected, direction, total, last_size),
    )
    return result.reshape(dual_rhs.shape)


def solution(mesh):
    in_specs = (
        P(None, "organ", "sub", None, None),
        P(None, "organ", "sub", None, None),
        P("organ", "sub", None, None, None),
        P(None, "organ", "sub", None, None),
        P("organ", "sub", None, None),
        P("organ", "sub", None),
        P("organ", "sub", None, None),
        P("organ", "sub", None),
        P("organ", "sub", None),
        P("organ", "sub", None),
    )
    out_specs = P(None, "organ", "sub", None, None)
    return jax.shard_map(local, mesh=mesh, in_specs=in_specs, out_specs=out_specs, check_vma=False)
```

```python
import functools

import jax
import jax.numpy as jnp
from jax import lax
from jax.experimental import pallas as pl
from jax.experimental.pallas import tpu as pltpu
from jax.sharding import PartitionSpec as P

ITERS = 3
CAP = 8
SUB_ROUNDS = 3
ORDER = (2, 0, 1, 4, 3)
AXES = ("organ", "sub")
LANES = 128
F32 = jnp.float32
BF16 = jnp.bfloat16
VMEM_LIMIT = 24 * 2**20
COST = 2_000_000
BAND = 256


def iota(shape, dim):
    return lax.broadcasted_iota(jnp.int32, shape, dim)


def halves(x):
    high = x.astype(BF16)
    return high, (x - high.astype(F32)).astype(BF16)


def thirds(x):
    high = x.astype(BF16)
    rest = x - high.astype(F32)
    middle = rest.astype(BF16)
    return high, middle, (rest - middle.astype(F32)).astype(BF16)


def bdot(a, b):
    return jnp.dot(a, b, preferred_element_type=F32)


def turned_dot(a, b):
    return lax.dot_general(a, b, (((1,), (1,)), ((), ())), preferred_element_type=F32)


def times(x, w_high, w_low, dot=bdot):
    rows = x.shape[0]
    a, b, c = thirds(x)
    full = dot(jnp.concatenate([a, b, c], axis=0), w_high)
    part = dot(jnp.concatenate([a, b], axis=0), w_low)
    low = full[2 * rows :] + part[rows:]
    return full[:rows] + (full[rows : 2 * rows] + part[:rows] + low)


def times_split(x, w):
    rows = x.shape[0]
    a, b = halves(x)
    w_high, w_low = halves(w)
    full = bdot(jnp.concatenate([a, b], axis=0), w_high)
    return full[:rows] + (full[rows:] + bdot(a, w_low))


def square(x):
    rows, cols = x.shape
    if rows < LANES:
        x = jnp.concatenate([x, jnp.zeros((LANES - rows, cols), F32)], axis=0)
    if cols < LANES:
        x = jnp.concatenate([x, jnp.zeros((x.shape[0], LANES - cols), F32)], axis=1)
    return x.T


def pack(master, slave, devices):
    def stacked(x):
        pieces = [x[:, k * devices : (k + 1) * devices] for k in range(CAP)]
        return jnp.concatenate(pieces, axis=0)

    turned = square(jnp.concatenate([stacked(master), stacked(slave)], axis=1))
    return turned[:devices], turned[devices : 2 * devices]


def unpack(master, slave, rows):
    devices = master.shape[0]
    turned = square(jnp.concatenate([master, slave], axis=0))

    def laid(first):
        pieces = [
            turned[k * rows : (k + 1) * rows, first : first + devices] for k in range(CAP)
        ]
        return jnp.concatenate(pieces, axis=1)

    return laid(0), laid(devices)


def put(ref, per, line, value):
    ref[pl.ds(line, value.shape[0], stride=per), :] = value


def get(ref, per, line):
    return ref[pl.ds(line, ref.shape[0] // per, stride=per), :]


def to_column(row, base, rows):
    spread = jnp.broadcast_to(row, (rows, LANES))
    here = iota((rows, LANES), 1) == iota((rows, LANES), 0) + base
    return jnp.sum(jnp.where(here, spread, 0.0), axis=1, keepdims=True)


def at_lanes(column, base):
    rows = column.shape[0]
    here = iota((rows, LANES), 1) == iota((rows, LANES), 0) + base
    return jnp.where(here, column, 0.0)


def fold(x):
    return sum(x[:, i : i + LANES] for i in range(0, x.shape[1], LANES))


def dots_row(pairs, base=0):
    total = 0.0
    for place, (left, right) in enumerate(pairs):
        acc = sum(fold(left[f] * right[f]) for f in range(left.shape[0]))
        column = jnp.sum(acc, axis=1, keepdims=True)
        total = total + at_lanes(column, base + place * column.shape[0])
    return jnp.sum(total, axis=0, keepdims=True)


def coefficients_row(field, basis):
    total = 0.0
    blocks, directions = field.shape[0], field.shape[1]
    for m in range(basis.shape[0]):
        acc = sum(fold(field[f] * basis[m, f : f + 1, :]) for f in range(blocks))
        total = total + at_lanes(jnp.sum(acc, axis=1, keepdims=True), m * directions)
    return jnp.sum(total, axis=0, keepdims=True)


def exact(x, unit, dot=bdot):
    rows = x.shape[0]
    full = dot(jnp.concatenate(thirds(x), axis=0), unit)
    return full[:rows] + (full[rows : 2 * rows] + full[2 * rows :])


def contact(mine, theirs, per_mine, per_theirs, a_high, a_low, unit):
    own = [get(mine, per_mine, i) for i in range(2)]
    other = [get(theirs, per_theirs, i) for i in range(2)]
    master, slave = unpack(own[0] + other[1], own[1] + other[0], LANES // CAP)
    return times(master, a_high[...], a_low[...]) + exact(slave, unit[...])


def send_contact(message, per, surface, a_high, a_low, unit):
    devices = message.shape[0] // per
    master = times(surface, a_high[...], a_low[...], turned_dot)
    slave = exact(surface, unit[...], turned_dot)
    for line, value in enumerate(pack(master, slave, devices)):
        put(message, per, line, value)


def spread_rows(message, per, line, row):
    put(message, per, line, jnp.broadcast_to(row, (message.shape[0] // per, LANES)))


def ranks(owner_row, active_row, count):
    rows = owner_row.shape[1]
    up, across = iota((rows, rows), 0), iota((rows, rows), 1)
    diagonal = up == across

    def column(row):
        return jnp.sum(jnp.where(diagonal, row, 0), axis=1, keepdims=True)

    live_row = jnp.where(iota((1, rows), 1) < count, active_row, 0)
    owner_col, live_col = column(owner_row), column(live_row)
    same = owner_col == owner_row
    rank_col = jnp.sum(jnp.where(same & (across < up), live_row, 0), axis=1, keepdims=True)
    rank_row = jnp.sum(jnp.where(same & (up < across), live_col, 0), axis=0, keepdims=True)
    return column, live_row, rank_row, rank_col


def load_modes(basis, modes, blocks):
    return [
        jnp.concatenate([basis[m * blocks + f] for f in range(blocks)], axis=0)
        for m in range(modes)
    ]


def setup_kernel(blocks, count, owner, dofs, active, basis, message):
    devices = message.ref.shape[0]
    owner, dofs, active, basis = owner(), dofs(), active(), basis()
    rows = owner.shape[1]
    column, live_row, _, rank_col = ranks(owner[...], active[...], count[0])
    named = (iota((devices, rows), 0) == owner[...]) & (live_row > 0)
    slots = jnp.where(iota((rows, LANES), 1) == rank_col, column(dofs[...]) + 1, 0)
    lines = jnp.dot(
        jnp.where(named, 1.0, 0.0),
        slots.astype(F32),
        precision=lax.Precision.HIGHEST,
        preferred_element_type=F32,
    )
    modes = basis.shape[0] // blocks
    slabs = load_modes(basis, modes, blocks)
    lane = iota((1, LANES), 1)
    gram = jnp.zeros((1, LANES), F32)
    for i in range(modes):
        for j in range(i + 1):
            value = jnp.sum(fold(slabs[i] * slabs[j]), axis=0, keepdims=True)
            value = jnp.sum(value, axis=1, keepdims=True)
            gram = jnp.where(lane == LANES // 2 + 8 * i + j, value, gram)
    message.ref[...] = jnp.where(iota((devices, LANES), 1) < CAP, lines, gram)


def slots_kernel(
    devices, count, owner, active, mortar, start_rows, right_rows, basis, a_high, a_low, start,
    right, products,
):
    owner, active = owner(), active()
    rows = owner.shape[1]
    width = CAP * devices
    _, live_row, rank_row, _ = ranks(owner[...], active[...], count[0])
    slot_row = jnp.where(live_row > 0, rank_row * devices + owner[...], -1)
    pick = jnp.where(iota((width, rows), 0) == slot_row, 1.0, 0.0).astype(BF16)
    blocks, directions = start.ref.shape[0], start.ref.shape[1]
    for source, target in ((start_rows(), start), (right_rows(), right)):
        for f in range(blocks):
            for c in range(directions):
                target.ref[f, c : c + 1, :] = source[c * blocks + f]
        target.flush()
    for part, target in zip(halves(mortar()[...]), (a_high, a_low), strict=True):
        target.ref[...] = bdot(pick, part).astype(BF16)
        target.flush()
    basis = basis()
    modes, length = basis.shape[0] // blocks, basis.shape[2]
    first = [basis[m * blocks] for m in range(modes)]
    extra = jnp.zeros((2 * 16 - directions - modes, length), F32)
    both = jnp.concatenate([start.ref[0]] + first + [extra], axis=0)
    products.ref[...] = times(both, a_high.ref[...], a_low.ref[...], turned_dot)


def first_kernel(
    organs, arrived, matches, basis, start, products, right, message, unit, modes_out, *sends
):
    devices = arrived.shape[0]
    subs = devices // organs
    blocks = len(sends)
    basis = basis()
    modes = basis.shape[0] // blocks
    length = basis.shape[2]
    dofs = arrived[...]
    place = iota((devices, length), 1).astype(F32) + 1.0
    for k in range(CAP):
        block = jnp.where(place == dofs[:, k : k + 1], -1.0, 0.0).astype(BF16)
        unit.ref[k * devices : (k + 1) * devices, :] = block
    unit.flush()
    mine = lax.axis_index("organ") * subs
    total = jnp.sum(arrived[pl.ds(pl.multiple_of(mine, 8), subs), :], axis=0, keepdims=True)
    lane = iota((1, LANES), 1)

    def entry(i, j):
        here = lane == LANES // 2 + 8 * i + j
        return jnp.sum(jnp.where(here, total, 0.0), axis=1, keepdims=True)

    low, inverse = {}, {}
    for j in range(modes):
        pivot = entry(j, j) - sum(low[j, k] * low[j, k] for k in range(j))
        inverse[j, j] = 1.0 / jnp.sqrt(pivot)
        for i in range(j + 1, modes):
            value = entry(i, j) - sum(low[i, k] * low[j, k] for k in range(j))
            low[i, j] = value * inverse[j, j]
    for j in range(modes):
        for i in range(j + 1, modes):
            value = sum(low[i, k] * inverse[k, j] for k in range(j, i))
            inverse[i, j] = -inverse[i, i] * value
    slabs = load_modes(basis, modes, blocks)
    modes_ref = modes_out.ref
    for i in range(modes):
        modes_ref[i] = sum(inverse[i, j] * slabs[j] for j in range(i + 1))
    modes_out.flush()
    start, matches = start(), matches()
    directions = start.shape[1]
    for r in range(blocks):
        face = matches[r]
        send = sends[r].ref
        send[0:directions, :] = start[face]
        for m in range(modes):
            send[directions + m : directions + m + 1, :] = modes_ref[m, pl.ds(face, 1), :]
        for m in range(modes, 8):
            send[directions + m : directions + m + 1, :] = jnp.zeros((1, length), F32)
        sends[r].flush()
    first = [modes_ref[m, 0:1, :] for m in range(modes)]
    extra = jnp.zeros((2 * 16 - directions - modes, length), F32)
    both = jnp.concatenate([start[0]] + first + [extra], axis=0)
    products = products()
    turned_modes = [
        sum(inverse[i, j] * products[directions + j : directions + j + 1, :] for j in range(i + 1))
        for i in range(modes)
    ]
    none = jnp.zeros((8 - modes, products.shape[1]), F32)
    turned_modes = jnp.concatenate(turned_modes + [none], axis=0)
    slave = exact(both, unit.ref[...], turned_dot)
    for line, value in enumerate(pack(products[0:directions, :], slave[:directions], devices)):
        put(message.ref, 4, line, value)
    rows = slice(directions, directions + 8)
    lines = pack(turned_modes, slave[rows], devices)
    half = LANES // 2
    put(message.ref, 4, 2, jnp.concatenate([line[:, :half] for line in lines], axis=1))
    spread_rows(message.ref, 4, 3, coefficients_row(right(), modes_ref))
    message.flush()


def times_symmetric(x, parts, f):
    rows = x.shape[0]
    a, b = halves(x)
    stacked = jnp.concatenate([a, b], axis=0)
    pieces = []
    first = 0
    for part in parts:
        w_high, w_low = halves(part[f])
        depth, width = w_high.shape
        here = slice(first, first + depth)
        after = slice(first + depth, first + width)
        high, low = bdot(stacked[:, here], w_high), bdot(a[:, here], w_low)
        value = high[:rows] + (high[rows:] + low)
        pieces.append((first, value))
        if width > depth:
            high = turned_dot(stacked[:, after], w_high[:, depth:])
            low = turned_dot(a[:, after], w_low[:, depth:])
            pieces.append((first, high[:rows] + (high[rows:] + low)))
        first += depth
    bands = []
    edges = [0]
    for part in parts:
        edges.append(edges[-1] + part.shape[1])
    for start, stop in zip(edges[:-1], edges[1:], strict=True):
        total = 0.0
        for begin, value in pieces:
            if begin <= start and stop <= begin + value.shape[1]:
                total = total + value[:, start - begin : stop - begin]
        bands.append(total)
    return jnp.concatenate(bands, axis=1)


def smooth(inner, near, smoothed, f):
    smoothed[f] = times_symmetric(inner[f], near, f)


def subtract_modes(field, columns, basis, f):
    value = field
    for m, column in enumerate(columns):
        value = value - column * basis[m, f : f + 1, :]
    return value


def start_contact(
    organs, arrived, sent, start, right, a_high, a_low, unit, modes_ref, new_right, base, added
):
    sent, start, maps = sent(), start(), (a_high(), a_low(), unit())
    devices = sent.shape[0] // 4
    subs = devices // organs
    blocks, directions = start.shape[0], start.shape[1]
    base[...] = start[...]
    base[0] += contact(sent, arrived, 4, 4, *maps)
    modes_ref, right = modes_ref(), right()
    organ = lax.axis_index("organ")
    block = arrived[pl.ds(pl.multiple_of(organ * subs * 4, 8), subs * 4), :]
    here = lax.rem(iota(block.shape, 0), 4) == 3
    row = jnp.sum(jnp.where(here, block, 0.0), axis=0, keepdims=True)
    columns = [to_column(row, m * directions, directions) for m in range(modes_ref.shape[0])]
    for f in range(blocks):
        new_right.ref[f] = subtract_modes(right[f], columns, modes_ref, f)
    new_right.flush()
    half = LANES // 2
    mine, other = get(sent, 4, 2), get(arrived, 4, 2)
    own_rows = unpack(mine[:, :half], mine[:, half:], 8)
    other_rows = unpack(other[:, half:], other[:, :half], 8)
    source = lax.rem(iota(own_rows[0].shape, 1), devices) // subs
    stacks = []
    for own_half, other_half in zip(own_rows, other_rows, strict=True):
        stack = []
        for o in range(organs):
            owns = jnp.where(organ == o, 1.0, 0.0)
            stack.append(jnp.where(source == o, other_half, 0.0) + owns * own_half)
        stacks.append(jnp.concatenate(stack, axis=0))
    added[...] = times(stacks[0], maps[0][...], maps[1][...]) + exact(stacks[1], maps[2][...])


def start_kernel(
    organs, bands, matches, f0, f1, f2, f3, f4, base, added, a_high, a_low, unit, modes_ref, *refs
):
    near, rest = refs[:bands], refs[bands:]
    message, smoothed_out, jump_out, s0, s1, s2, s3, s4, inner = rest
    faces = (f0, f1, f2, f3, f4)
    smoothed = smoothed_out.ref
    blocks, directions = base.shape[0], base.shape[1]
    for r, face in zip(ORDER, faces, strict=True):
        inner[matches[r]] = base[matches[r]] - face[0:directions, :]
    for f in range(blocks):
        smooth(inner, near, smoothed, f)
        if f == 0:
            send_contact(message.ref, 2, smoothed[0], a_high, a_low, unit)
            message.flush()
    for r, send in enumerate((s0, s1, s2, s3, s4)):
        send(smoothed.at[matches[r]])
    smoothed_out.flush()
    modes = modes_ref.shape[0]
    jump_modes = jump_out.ref
    organ = lax.axis_index("organ")
    jump_modes[...] = jnp.zeros(jump_modes.shape, F32)
    for r, values in zip(ORDER, faces, strict=True):
        face = matches[r]
        for m in range(modes):
            own = modes_ref[m, pl.ds(face, 1), :]
            other = values[directions + m : directions + m + 1, :]
            if r < SUB_ROUNDS:
                own = own - other
            else:
                partner = organ ^ (1 << (r - SUB_ROUNDS))
                jump_modes[face, pl.ds(m * organs + partner, 1), :] = -other
            jump_modes[face, pl.ds(m * organs + organ, 1), :] = own
    for o in range(organs):
        for m in range(modes):
            row = pl.ds(m * organs + o, 1)
            jump_modes[0, row, :] = jump_modes[0, row, :] + added[8 * o + m : 8 * o + m + 1, :]


def residual_contact(arrived, sent, smoothed, right, a_high, a_low, unit, part):
    sent, smoothed, right = sent(), smoothed(), right()
    part[...] = right[...] - smoothed[...]
    part[0] -= contact(sent, arrived, 2, 2, a_high(), a_low(), unit())


def residual_kernel(
    matches, f0, f1, f2, f3, f4, part, a_high, a_low, unit, modes_ref, message, resid, *sends
):
    for r, face in zip(ORDER, (f0, f1, f2, f3, f4), strict=True):
        resid.ref[matches[r]] = part[matches[r]] + face[...]
    send_residual(matches, resid, modes_ref, (a_high, a_low, unit), message, sends)


def send_residual(matches, resid, modes_ref, maps, message, sends):
    for r, send in enumerate(sends):
        send(resid.ref.at[matches[r]])
    resid.flush()
    send_contact(message.ref, 4, resid.ref[0], *maps)
    spread_rows(message.ref, 4, 2, coefficients_row(resid.ref, modes_ref))
    message.flush()


def inner_contact(
    organs, steps, arrived, sent, resid, modes_ref, jump_modes, *refs
):
    rest = list(refs)
    a_high, a_low, unit = (rest.pop(0) for _ in range(3))
    if steps:
        start, behind, jumps, sizes = (
            rest[0],
            *(rest[1 + i * steps : 1 + (i + 1) * steps] for i in range(3)),
        )
        projected, total, direction, jumped, last_size, base, norms = rest[1 + 3 * steps :]
    else:
        projected_out, base, norms = rest
        projected = projected_out.ref
    sent, resid, maps = sent(), resid(), (a_high(), a_low(), unit())
    modes_ref, jump_modes = modes_ref(), jump_modes()
    devices = sent.shape[0] // 4
    subs = devices // organs
    blocks, directions = resid.shape[0], resid.shape[1]
    parts = get(arrived, 4, 2)
    sums = [
        jnp.sum(parts[o * subs : (o + 1) * subs], axis=0, keepdims=True) for o in range(organs)
    ]
    added = contact(sent, arrived, 4, 4, *maps)
    turned = square(jnp.concatenate(sums, axis=0))
    left = jnp.concatenate(
        [turned[m * directions : (m + 1) * directions, :organs] for m in range(8)], axis=1
    )
    organ = lax.axis_index("organ")
    own = sum(jnp.where(organ == o, 1.0, 0.0) * sums[o] for o in range(organs))
    columns = [to_column(own, m * directions, directions) for m in range(modes_ref.shape[0])]
    for f in range(blocks):
        projected[f] = subtract_modes(resid[f], columns, modes_ref, f)
    if not steps:
        projected_out.flush()
    for f in range(blocks):
        value = resid[f] - times_split(left, jump_modes[f])
        base[f] = value + added if f == 0 else value
    norms[...] = jnp.broadcast_to(dots_row([(projected, projected)]), norms.shape)
    if steps:
        start = start()
        behind, jumps, sizes = ([late() for late in group] for group in (behind, jumps, sizes))
        last_size[...] = sizes[-1][...]
        for f in range(blocks):
            value = behind[0][f]
            sum_up = start[f] + sizes[0][2, :, 0:1] * value
            for field, size in zip(behind[1:], sizes[1:], strict=True):
                value = field[f] + size[3, :, 0:1] * value
                sum_up = sum_up + size[2, :, 0:1] * value
            total[f] = sum_up
            direction[f] = value
            value = jumps[0][f]
            for field, size in zip(jumps[1:], sizes[1:], strict=True):
                value = field[f] + size[3, :, 0:1] * value
            jumped[f] = value


def inner_kernel(bands, last, older, matches, f0, f1, f2, f3, f4, base, norms, *refs):
    maps, rest = (None, refs) if last else (refs[:3], refs[3:])
    near, rest = rest[:bands], list(rest[bands:])
    previous = rest.pop(0) if older else None
    message = rest.pop(0)
    if last:
        inner, smoothed = rest
    else:
        inner_out, smoothed_out = rest[:2]
        inner, smoothed = inner_out.ref, smoothed_out.ref
    for r, face in zip(ORDER, (f0, f1, f2, f3, f4), strict=True):
        inner[matches[r]] = base[matches[r]] - face[...]
    if not last:
        inner_out.flush()
    for f in range(inner.shape[0]):
        smooth(inner, near, smoothed, f)
        if f == 0 and not last:
            send_contact(message.ref, 4, smoothed[0], *maps)
    if not last:
        for r, send in enumerate(rest[2:]):
            send(smoothed.at[matches[r]])
        smoothed_out.flush()
    directions = inner.shape[1]
    pairs = [(inner, smoothed)]
    if older:
        pairs.append((previous, smoothed))
    row = dots_row(pairs, directions) + norms[0:1, :]
    if last:
        message.ref[...] = jnp.broadcast_to(row, message.ref.shape)
    else:
        spread_rows(message.ref, 4, 2, row)


def step_sizes(row, older, scalars, directions):
    rho = to_column(row, 0, directions)
    curvature = to_column(row, directions, directions)
    if not older:
        return rho, None, curvature, rho / curvature
    cross = to_column(row, 2 * directions, directions)
    beta = rho / scalars[0, :, 0:1]
    curvature = curvature + beta * (2.0 * cross + beta * scalars[1, :, 0:1])
    return rho, beta, curvature, rho / curvature


def outer_contact(older, arrived, sent, smoothed, projected, *refs):
    rest = list(refs)
    old_image = scalars = None
    if older:
        old_image, scalars = rest[0](), rest[1]()
        rest = rest[2:]
    a_high, a_low, unit, new_scalars, part, steps, image = rest
    sent, smoothed, projected = sent(), smoothed(), projected()
    blocks, directions = smoothed.shape[0], smoothed.shape[1]
    row = jnp.sum(get(arrived, 4, 2), axis=0, keepdims=True)
    rho, beta, curvature, step = step_sizes(row, older, scalars, directions)
    wide = (directions, LANES)
    for place, column in enumerate((rho, curvature, step) + ((beta,) if older else ())):
        new_scalars.ref[place] = jnp.broadcast_to(column, wide)
    new_scalars.flush()
    steps[...] = jnp.broadcast_to(step, wide)
    added = contact(sent, arrived, 4, 4, a_high(), a_low(), unit())
    for f in range(blocks):
        value = smoothed[f]
        if f == 0:
            value = value + added
        if older:
            value = value + beta * old_image[f]
        image[f] = value
        part[f] = projected[f] - step * value


def outer_kernel(older, matches, f0, f1, f2, f3, f4, part, steps, image, *refs):
    a_high, a_low, unit, modes_ref = refs[:4]
    rest = list(refs[4:])
    if older:
        message, resid = rest[:2]
        sends = rest[2:]
    else:
        message, resid, new_image = rest[:3]
        sends = rest[3:]
    step = steps[:, 0:1]
    for r, face in zip(ORDER, (f0, f1, f2, f3, f4), strict=True):
        resid.ref[matches[r]] = part[matches[r]] + step * face[...]
        if not older:
            new_image.ref[matches[r]] = image[matches[r]] - face[...]
    send_residual(matches, resid, modes_ref, (a_high, a_low, unit), message, sends)


def last_kernel(arrived, projected, old_direction, total, scalars, out):
    blocks, directions = projected.shape[0], projected.shape[1]
    row = jnp.sum(arrived[...], axis=0, keepdims=True)
    _, beta, _, step = step_sizes(row, True, scalars, directions)
    for f in range(blocks):
        value = total[f] + step * (projected[f] + beta * old_direction[f])
        for c in range(directions):
            out.ref[c * blocks + f] = value[c : c + 1]


class Late:
    def __init__(self, source, target, sem, priority=0):
        self.target, self.waiting, self.priority = target, True, priority
        self.copy = pltpu.make_async_copy(source, target, sem)

    def start(self):
        self.copy.start(priority=self.priority)

    def __call__(self):
        if self.waiting:
            self.copy.wait()
            self.waiting = False
        return self.target


class Send:
    def __init__(self, target, sem):
        self.target, self.sem, self.copy = target, sem, None

    def __call__(self, source):
        self.copy = pltpu.make_async_copy(source, self.target, self.sem)
        self.copy.start()


class Out:
    def __init__(self, ref, target, sem):
        self.ref = ref
        self.copy = pltpu.make_async_copy(ref, target, sem)
        self.started = False

    def flush(self):
        if not self.started:
            self.copy.start()
            self.started = True


def call(kernel, outs, args, late=(), smem=0, near=(), sends=(), scratch=(), bring=(), held=0, shared=0):
    n_late, n_out, n_arg, n_near = len(late), len(outs), len(args), len(near)
    bring = [item if isinstance(item, tuple) else (item, item.shape, None) for item in bring]
    brought = [(shape, a.dtype) for a, shape, _ in bring]

    def body(*refs):
        refs = list(refs)

        def take(n):
            taken = refs[:n]
            del refs[:n]
            return taken

        given, sources, origins = take(n_arg), take(n_late), take(len(bring))
        targets, ports, close = take(n_out), take(len(sends)), take(n_near)
        goals = take(len(bring))
        buffers, results = take(n_late), take(n_out)
        extra = take(len(scratch))
        in_sem, bring_sem, out_sem = refs
        copies = []
        for i, (origin, goal) in enumerate(zip(origins, goals, strict=True)):
            first = bring[i][2]
            if first is not None:
                rows, columns = goal.shape[1], goal.shape[2]
                origin = origin.at[:, pl.ds(first, rows), pl.ds(first, columns)]
            copies.append(Late(origin, goal, bring_sem.at[i], 0 if i < shared else 1))
        lates = [Late(s, b, in_sem.at[i]) for i, (s, b) in enumerate(zip(sources, buffers))]
        for item in copies[:shared] + lates + copies[shared:]:
            item.start()
        written = [Out(r, t, out_sem.at[i]) for i, (r, t) in enumerate(zip(results, targets))]
        posts = [Send(t, out_sem.at[n_out + i]) for i, t in enumerate(ports)]
        kernel(*given, *lates, *copies[:shared], *written, *posts, *close, *extra)
        for item in lates + copies:
            item()
        for item in written:
            item.flush()
        for item in written + posts:
            item.copy.wait()

    in_specs = [pl.BlockSpec(memory_space=pltpu.SMEM)] * smem
    in_specs += [pl.BlockSpec(memory_space=pltpu.VMEM)] * (n_arg - smem)
    remote = tuple(late) + tuple(a for a, _, _ in bring)
    in_specs += [pl.BlockSpec(memory_space=pltpu.HBM)] * len(remote)
    out_specs = [pl.BlockSpec(memory_space=pltpu.HBM)] * (n_out + len(sends))
    out_specs += [pl.BlockSpec(memory_space=pltpu.VMEM)] * (n_near + len(bring))
    scratch_shapes = [pltpu.SMEM(a.shape, a.dtype) for a in late[:held]]
    scratch_shapes += [pltpu.VMEM(a.shape, a.dtype) for a in late[held:]]
    scratch_shapes += [pltpu.VMEM(shape, kind) for shape, kind in outs]
    scratch_shapes += list(scratch)
    counts = (n_late, len(bring), n_out + len(sends))
    scratch_shapes += [pltpu.SemaphoreType.DMA((max(n, 1),)) for n in counts]
    return pl.pallas_call(
        body,
        out_shape=[pltpu.HBM(shape, kind) for shape, kind in tuple(outs) + tuple(sends)]
        + [pltpu.VMEM(shape, kind) for shape, kind in list(near) + brought],
        in_specs=in_specs,
        out_specs=out_specs,
        scratch_shapes=scratch_shapes,
        compiler_params=pltpu.CompilerParams(vmem_limit_bytes=VMEM_LIMIT),
        cost_estimate=pl.CostEstimate(flops=COST, bytes_accessed=COST, transcendentals=0),
    )(*args, *(pltpu.with_memory_space_constraint(a, pltpu.HBM) for a in remote))


def from_partner(value, axis, apart):
    mask = 2**apart
    pairs = [(source, source ^ mask) for source in range(lax.axis_size(axis))]
    return lax.ppermute(value, axis, pairs)


def exchange(message):
    return lax.all_to_all(message, AXES, split_axis=0, concat_axis=0, tiled=True)


def swap_faces(faces):
    swapped = []
    for r in ORDER:
        axis, apart = ("sub", r) if r < SUB_ROUNDS else ("organ", r - SUB_ROUNDS)
        swapped.append(from_partner(faces[r], axis, apart))
    return swapped


def local(
    dual_rhs, warm_start, inverse_blocks, coarse_basis, mortar_rows, match_rounds, slave_owner,
    slave_dofs, active_set, row_counts,
):
    directions, blocks, length = dual_rhs.shape[0], dual_rhs.shape[3], dual_rhs.shape[4]
    rows = mortar_rows.shape[2]
    modes = coarse_basis.shape[0]
    organs, subs = lax.axis_size("organ"), lax.axis_size("sub")
    devices = organs * subs
    width = CAP * devices
    field = (blocks, directions, length)
    right_rows = dual_rhs.reshape(directions * blocks, 1, length)
    start_rows = warm_start.reshape(directions * blocks, 1, length)
    matrices = inverse_blocks.reshape(blocks, length, length)
    basis = coarse_basis.reshape(modes * blocks, 1, length)
    mortar = mortar_rows.reshape(rows, length)
    matches = match_rounds.reshape(-1)
    owner = slave_owner.reshape(1, rows)
    dofs = slave_dofs.reshape(1, rows)
    active = active_set.reshape(1, rows)
    count = row_counts.reshape(1)
    face = ((directions, length), F32)
    whole = (field, F32)
    message_line = ((4 * devices, LANES), F32)

    sends = [face] * blocks
    near_matrices, first = [], 0
    while first < length:
        rows = min(BAND, length - first)
        near_matrices.append((matrices, (blocks, rows, length - first), first))
        first += rows
    near_matrices = tuple(near_matrices)
    bands = len(near_matrices)

    (setup,) = call(
        functools.partial(setup_kernel, blocks),
        [((devices, LANES), F32)],
        (count,),
        (owner, dofs, active, basis),
        smem=1,
    )
    arrived = exchange(setup)
    a_high, a_low, start, right, products = call(
        functools.partial(slots_kernel, devices),
        [((width, length), BF16)] * 2 + [whole] * 2 + [((32, width), F32)],
        (count,),
        (owner, active, mortar, start_rows, right_rows, basis),
        smem=1,
    )
    sent, unit, modes_ref, *faces = call(
        functools.partial(first_kernel, organs),
        [
            message_line,
            ((width, length), BF16),
            ((modes, blocks, length), F32),
        ]
        + [((directions + 8, length), F32)] * blocks,
        (arrived,),
        (matches, basis, start, products, right),
        held=1,
    )
    maps = (a_high, a_low, unit)
    arrived = exchange(sent)
    faces = swap_faces(faces)
    right, base, added, *more = call(
        functools.partial(start_contact, organs),
        [whole],
        (arrived,),
        (sent, start, right),
        near=[whole, ((8 * organs, length), F32)],
        bring=maps + (modes_ref,) + near_matrices,
        shared=4,
    )
    message, smoothed, jump_modes, *posts = call(
        functools.partial(start_kernel, organs, bands),
        [((2 * devices, LANES), F32), whole, ((blocks, 8 * organs, length), F32)],
        (matches, *faces, base, added, *more),
        smem=1,
        sends=sends,
        scratch=[pltpu.VMEM(field, F32)],
    )
    arrived = exchange(message)
    faces = swap_faces(posts)
    part, *more = call(
        residual_contact,
        [],
        (arrived,),
        (message, smoothed, right),
        near=[whole],
        bring=maps + (modes_ref,),
        shared=3,
    )
    sent, resid, *posts = call(
        residual_kernel,
        [message_line, whole],
        (matches, *faces, part, *more),
        smem=1,
        sends=sends,
    )
    image = None
    size = (4, directions, LANES)
    fields, jumps, scalars = [], [], []
    for step in range(ITERS):
        older, last = step > 0, step == ITERS - 1
        arrived = exchange(sent)
        faces = swap_faces(posts)
        history = (start, *fields, *jumps, *scalars) if last else ()
        more_near = [whole] * 3 + [(size, F32)] if last else []
        ahead = (jumps[-1],) if older and not last else ()
        projected, *more = call(
            functools.partial(inner_contact, organs, step if last else 0),
            [] if last else [whole],
            (arrived,),
            (sent, resid, modes_ref, jump_modes) + (maps if last else ()) + history,
            near=([whole] + more_near if last else []) + [whole, ((8, LANES), F32)],
            bring=(() if last else maps) + near_matrices + ahead,
            shared=0 if last else 3,
        )
        if last:
            total, direction, jumped, last_size, base, norms, *near = more
            (message,) = call(
                functools.partial(inner_kernel, bands, last, older),
                [((devices, LANES), F32)],
                (matches, *faces, base, norms, *near, jumped),
                smem=1,
                scratch=[pltpu.VMEM(field, F32)] * 2,
            )
            arrived = exchange(message)
            break
        message, inner, smoothed, *posts = call(
            functools.partial(inner_kernel, bands, last, older),
            [message_line, whole, whole],
            (matches, *faces, *more),
            smem=1,
            sends=sends,
        )
        arrived = exchange(message)
        faces = swap_faces(posts)
        old = (image, scalars[-1]) if older else ()
        new_scalars, *more = call(
            functools.partial(outer_contact, older),
            [(size, F32)],
            (arrived,),
            (message, smoothed, projected) + old,
            near=[whole, ((directions, LANES), F32), whole],
            bring=maps + (modes_ref,),
            shared=3,
        )
        sent, resid, *posts = call(
            functools.partial(outer_kernel, older),
            [message_line, whole] + ([] if older else [whole]),
            (matches, *faces, *more),
            smem=1,
            sends=sends,
        )
        if not older:
            image, *posts = posts
        fields.append(projected)
        jumps.append(inner)
        scalars.append(new_scalars)
    (result,) = call(
        last_kernel,
        [((directions * blocks, 1, length), F32)],
        (arrived, projected, direction, total, last_size),
    )
    return result.reshape(dual_rhs.shape)


def solution(mesh):
    in_specs = (
        P(None, "organ", "sub", None, None),
        P(None, "organ", "sub", None, None),
        P("organ", "sub", None, None, None),
        P(None, "organ", "sub", None, None),
        P("organ", "sub", None, None),
        P("organ", "sub", None),
        P("organ", "sub", None, None),
        P("organ", "sub", None),
        P("organ", "sub", None),
        P("organ", "sub", None),
    )
    out_specs = P(None, "organ", "sub", None, None)
    return jax.shard_map(local, mesh=mesh, in_specs=in_specs, out_specs=out_specs, check_vma=False)
```

```python
import functools

import jax
import jax.numpy as jnp
from jax import lax
from jax.experimental import pallas as pl
from jax.experimental.pallas import tpu as pltpu
from jax.sharding import PartitionSpec as P

ITERS = 3
CAP = 8
SUB_ROUNDS = 3
ORDER = (2, 0, 1, 4, 3)
AXES = ("organ", "sub")
LANES = 128
F32 = jnp.float32
BF16 = jnp.bfloat16
VMEM_LIMIT = 24 * 2**20
COST = 2_000_000
BAND = 256


def iota(shape, dim):
    return lax.broadcasted_iota(jnp.int32, shape, dim)


def halves(x):
    high = x.astype(BF16)
    return high, (x - high.astype(F32)).astype(BF16)


def thirds(x):
    high = x.astype(BF16)
    rest = x - high.astype(F32)
    middle = rest.astype(BF16)
    return high, middle, (rest - middle.astype(F32)).astype(BF16)


def bdot(a, b):
    return jnp.dot(a, b, preferred_element_type=F32)


def turned_dot(a, b):
    return lax.dot_general(a, b, (((1,), (1,)), ((), ())), preferred_element_type=F32)


def times(x, w_high, w_low, dot=bdot):
    rows = x.shape[0]
    a, b, c = thirds(x)
    full = dot(jnp.concatenate([a, b, c], axis=0), w_high)
    part = dot(jnp.concatenate([a, b], axis=0), w_low)
    low = full[2 * rows :] + part[rows:]
    return full[:rows] + (full[rows : 2 * rows] + part[:rows] + low)


def times_split(x, w):
    rows = x.shape[0]
    a, b = halves(x)
    w_high, w_low = halves(w)
    full = bdot(jnp.concatenate([a, b], axis=0), w_high)
    return full[:rows] + (full[rows:] + bdot(a, w_low))


def square(x):
    rows, cols = x.shape
    if rows < LANES:
        x = jnp.concatenate([x, jnp.zeros((LANES - rows, cols), F32)], axis=0)
    if cols < LANES:
        x = jnp.concatenate([x, jnp.zeros((x.shape[0], LANES - cols), F32)], axis=1)
    return x.T


def pack(master, slave, devices):
    def stacked(x):
        pieces = [x[:, k * devices : (k + 1) * devices] for k in range(CAP)]
        return jnp.concatenate(pieces, axis=0)

    turned = square(jnp.concatenate([stacked(master), stacked(slave)], axis=1))
    return turned[:devices], turned[devices : 2 * devices]


def unpack(master, slave, rows):
    devices = master.shape[0]
    turned = square(jnp.concatenate([master, slave], axis=0))

    def laid(first):
        pieces = [
            turned[k * rows : (k + 1) * rows, first : first + devices] for k in range(CAP)
        ]
        return jnp.concatenate(pieces, axis=1)

    return laid(0), laid(devices)


def put(ref, per, line, value):
    ref[pl.ds(line, value.shape[0], stride=per), :] = value


def get(ref, per, line):
    return ref[pl.ds(line, ref.shape[0] // per, stride=per), :]


def to_column(row, base, rows):
    spread = jnp.broadcast_to(row, (rows, LANES))
    here = iota((rows, LANES), 1) == iota((rows, LANES), 0) + base
    return jnp.sum(jnp.where(here, spread, 0.0), axis=1, keepdims=True)


def at_lanes(column, base):
    rows = column.shape[0]
    here = iota((rows, LANES), 1) == iota((rows, LANES), 0) + base
    return jnp.where(here, column, 0.0)


def fold(x):
    return sum(x[:, i : i + LANES] for i in range(0, x.shape[1], LANES))


def dots_row(pairs, base=0):
    total = 0.0
    for place, (left, right) in enumerate(pairs):
        acc = sum(fold(left[f] * right[f]) for f in range(left.shape[0]))
        column = jnp.sum(acc, axis=1, keepdims=True)
        total = total + at_lanes(column, base + place * column.shape[0])
    return jnp.sum(total, axis=0, keepdims=True)


def coefficients_row(field, basis):
    total = 0.0
    blocks, directions = field.shape[0], field.shape[1]
    for m in range(basis.shape[0]):
        acc = sum(fold(field[f] * basis[m, f : f + 1, :]) for f in range(blocks))
        total = total + at_lanes(jnp.sum(acc, axis=1, keepdims=True), m * directions)
    return jnp.sum(total, axis=0, keepdims=True)


def exact(x, unit, dot=bdot):
    rows = x.shape[0]
    full = dot(jnp.concatenate(thirds(x), axis=0), unit)
    return full[:rows] + (full[rows : 2 * rows] + full[2 * rows :])


def contact(mine, theirs, per_mine, per_theirs, a_high, a_low, unit):
    own = [get(mine, per_mine, i) for i in range(2)]
    other = [get(theirs, per_theirs, i) for i in range(2)]
    master, slave = unpack(own[0] + other[1], own[1] + other[0], LANES // CAP)
    return times(master, a_high[...], a_low[...]) + exact(slave, unit[...])


def send_contact(message, per, surface, a_high, a_low, unit):
    devices = message.shape[0] // per
    master = times(surface, a_high[...], a_low[...], turned_dot)
    slave = exact(surface, unit[...], turned_dot)
    for line, value in enumerate(pack(master, slave, devices)):
        put(message, per, line, value)


def spread_rows(message, per, line, row):
    put(message, per, line, jnp.broadcast_to(row, (message.shape[0] // per, LANES)))


def ranks(owner_row, active_row, count):
    rows = owner_row.shape[1]
    up, across = iota((rows, rows), 0), iota((rows, rows), 1)
    diagonal = up == across

    def column(row):
        return jnp.sum(jnp.where(diagonal, row, 0), axis=1, keepdims=True)

    live_row = jnp.where(iota((1, rows), 1) < count, active_row, 0)
    owner_col, live_col = column(owner_row), column(live_row)
    same = owner_col == owner_row
    rank_col = jnp.sum(jnp.where(same & (across < up), live_row, 0), axis=1, keepdims=True)
    rank_row = jnp.sum(jnp.where(same & (up < across), live_col, 0), axis=0, keepdims=True)
    return column, live_row, rank_row, rank_col


def load_modes(basis, modes, blocks):
    return [
        jnp.concatenate([basis[m * blocks + f] for f in range(blocks)], axis=0)
        for m in range(modes)
    ]


def setup_kernel(blocks, count, owner, dofs, active, basis, message):
    devices = message.ref.shape[0]
    owner, dofs, active, basis = owner(), dofs(), active(), basis()
    rows = owner.shape[1]
    column, live_row, _, rank_col = ranks(owner[...], active[...], count[0])
    named = (iota((devices, rows), 0) == owner[...]) & (live_row > 0)
    slots = jnp.where(iota((rows, LANES), 1) == rank_col, column(dofs[...]) + 1, 0)
    lines = jnp.dot(
        jnp.where(named, 1.0, 0.0),
        slots.astype(F32),
        precision=lax.Precision.HIGHEST,
        preferred_element_type=F32,
    )
    modes = basis.shape[0] // blocks
    slabs = load_modes(basis, modes, blocks)
    lane = iota((1, LANES), 1)
    gram = jnp.zeros((1, LANES), F32)
    for i in range(modes):
        for j in range(i + 1):
            value = jnp.sum(fold(slabs[i] * slabs[j]), axis=0, keepdims=True)
            value = jnp.sum(value, axis=1, keepdims=True)
            gram = jnp.where(lane == LANES // 2 + 8 * i + j, value, gram)
    message.ref[...] = jnp.where(iota((devices, LANES), 1) < CAP, lines, gram)


def slots_kernel(
    devices, count, owner, active, mortar, start_rows, right_rows, basis, a_high, a_low, start,
    right, products, raw_out,
):
    owner, active = owner(), active()
    rows = owner.shape[1]
    width = CAP * devices
    _, live_row, rank_row, _ = ranks(owner[...], active[...], count[0])
    slot_row = jnp.where(live_row > 0, rank_row * devices + owner[...], -1)
    pick = jnp.where(iota((width, rows), 0) == slot_row, 1.0, 0.0).astype(BF16)
    blocks, directions = start.ref.shape[0], start.ref.shape[1]
    for source, target in ((start_rows(), start), (right_rows(), right)):
        for f in range(blocks):
            for c in range(directions):
                target.ref[f, c : c + 1, :] = source[c * blocks + f]
        target.flush()
    for part, target in zip(halves(mortar()[...]), (a_high, a_low), strict=True):
        target.ref[...] = bdot(pick, part).astype(BF16)
        target.flush()
    basis = basis()
    modes, length = basis.shape[0] // blocks, basis.shape[2]
    first = [basis[m * blocks] for m in range(modes)]
    extra = jnp.zeros((2 * 16 - directions - modes, length), F32)
    both = jnp.concatenate([start.ref[0]] + first + [extra], axis=0)
    products.ref[...] = times(both, a_high.ref[...], a_low.ref[...], turned_dot)
    products.flush()
    here = lax.rem(iota((directions, LANES), 1), directions) == iota((directions, LANES), 0)
    raw_out.ref[...] = jnp.zeros(raw_out.ref.shape, F32)
    for m in range(modes):
        acc = sum(fold(right.ref[f] * basis[m * blocks + f]) for f in range(blocks))
        column = jnp.sum(acc, axis=1, keepdims=True)
        row = jnp.sum(jnp.where(here, column, 0.0), axis=0, keepdims=True)
        raw_out.ref[m : m + 1, :] = row


def first_kernel(
    organs, arrived, matches, basis, start, products, raw, message, unit, modes_out, *sends
):
    devices = arrived.shape[0]
    subs = devices // organs
    blocks = len(sends)
    basis = basis()
    modes = basis.shape[0] // blocks
    length = basis.shape[2]
    dofs = arrived[...]
    place = iota((devices, length), 1).astype(F32) + 1.0
    for k in range(CAP):
        block = jnp.where(place == dofs[:, k : k + 1], -1.0, 0.0).astype(BF16)
        unit.ref[k * devices : (k + 1) * devices, :] = block
    unit.flush()
    mine = lax.axis_index("organ") * subs
    total = jnp.sum(arrived[pl.ds(pl.multiple_of(mine, 8), subs), :], axis=0, keepdims=True)
    lane = iota((1, LANES), 1)

    def entry(i, j):
        here = lane == LANES // 2 + 8 * i + j
        return jnp.sum(jnp.where(here, total, 0.0), axis=1, keepdims=True)

    low, inverse = {}, {}
    for j in range(modes):
        pivot = entry(j, j) - sum(low[j, k] * low[j, k] for k in range(j))
        inverse[j, j] = 1.0 / jnp.sqrt(pivot)
        for i in range(j + 1, modes):
            value = entry(i, j) - sum(low[i, k] * low[j, k] for k in range(j))
            low[i, j] = value * inverse[j, j]
    for j in range(modes):
        for i in range(j + 1, modes):
            value = sum(low[i, k] * inverse[k, j] for k in range(j, i))
            inverse[i, j] = -inverse[i, i] * value
    slabs = load_modes(basis, modes, blocks)
    modes_ref = modes_out.ref
    for i in range(modes):
        modes_ref[i] = sum(inverse[i, j] * slabs[j] for j in range(i + 1))
    modes_out.flush()
    start, matches = start(), matches()
    directions = start.shape[1]
    for r in range(blocks):
        face = matches[r]
        send = sends[r].ref
        send[0:directions, :] = start[face]
        for m in range(modes):
            send[directions + m : directions + m + 1, :] = modes_ref[m, pl.ds(face, 1), :]
        for m in range(modes, 8):
            send[directions + m : directions + m + 1, :] = jnp.zeros((1, length), F32)
        sends[r].flush()
    first = [modes_ref[m, 0:1, :] for m in range(modes)]
    extra = jnp.zeros((2 * 16 - directions - modes, length), F32)
    both = jnp.concatenate([start[0]] + first + [extra], axis=0)
    products = products()
    turned_modes = [
        sum(inverse[i, j] * products[directions + j : directions + j + 1, :] for j in range(i + 1))
        for i in range(modes)
    ]
    none = jnp.zeros((8 - modes, products.shape[1]), F32)
    turned_modes = jnp.concatenate(turned_modes + [none], axis=0)
    slave = exact(both, unit.ref[...], turned_dot)
    for line, value in enumerate(pack(products[0:directions, :], slave[:directions], devices)):
        put(message.ref, 4, line, value)
    rows = slice(directions, directions + 8)
    lines = pack(turned_modes, slave[rows], devices)
    half = LANES // 2
    put(message.ref, 4, 2, jnp.concatenate([line[:, :half] for line in lines], axis=1))
    raw = raw()
    row = jnp.zeros((1, LANES), F32)
    for i in range(modes):
        value = sum(inverse[i, j] * raw[j : j + 1, :] for j in range(i + 1))
        row = jnp.where(lane // directions == i, value, row)
    spread_rows(message.ref, 4, 3, row)
    message.flush()


def times_symmetric(x, parts, f):
    rows = x.shape[0]
    a, b = halves(x)
    stacked = jnp.concatenate([a, b], axis=0)
    pieces = []
    first = 0
    for part in parts:
        w_high, w_low = halves(part[f])
        depth, width = w_high.shape
        here = slice(first, first + depth)
        after = slice(first + depth, first + width)
        high, low = bdot(stacked[:, here], w_high), bdot(a[:, here], w_low)
        value = high[:rows] + (high[rows:] + low)
        pieces.append((first, value))
        if width > depth:
            high = turned_dot(stacked[:, after], w_high[:, depth:])
            low = turned_dot(a[:, after], w_low[:, depth:])
            pieces.append((first, high[:rows] + (high[rows:] + low)))
        first += depth
    bands = []
    edges = [0]
    for part in parts:
        edges.append(edges[-1] + part.shape[1])
    for start, stop in zip(edges[:-1], edges[1:], strict=True):
        total = 0.0
        for begin, value in pieces:
            if begin <= start and stop <= begin + value.shape[1]:
                total = total + value[:, start - begin : stop - begin]
        bands.append(total)
    return jnp.concatenate(bands, axis=1)


def smooth(inner, near, smoothed, f):
    smoothed[f] = times_symmetric(inner[f], near, f)


def subtract_modes(field, columns, basis, f):
    value = field
    for m, column in enumerate(columns):
        value = value - column * basis[m, f : f + 1, :]
    return value


def start_contact(
    organs, arrived, sent, start, right, a_high, a_low, unit, modes_ref, new_right, base, added
):
    sent, start, maps = sent(), start(), (a_high(), a_low(), unit())
    devices = sent.shape[0] // 4
    subs = devices // organs
    blocks, directions = start.shape[0], start.shape[1]
    base[...] = start[...]
    base[0] += contact(sent, arrived, 4, 4, *maps)
    modes_ref, right = modes_ref(), right()
    organ = lax.axis_index("organ")
    block = arrived[pl.ds(pl.multiple_of(organ * subs * 4, 8), subs * 4), :]
    here = lax.rem(iota(block.shape, 0), 4) == 3
    row = jnp.sum(jnp.where(here, block, 0.0), axis=0, keepdims=True)
    columns = [to_column(row, m * directions, directions) for m in range(modes_ref.shape[0])]
    for f in range(blocks):
        new_right.ref[f] = subtract_modes(right[f], columns, modes_ref, f)
    new_right.flush()
    half = LANES // 2
    mine, other = get(sent, 4, 2), get(arrived, 4, 2)
    own_rows = unpack(mine[:, :half], mine[:, half:], 8)
    other_rows = unpack(other[:, half:], other[:, :half], 8)
    source = lax.rem(iota(own_rows[0].shape, 1), devices) // subs
    stacks = []
    for own_half, other_half in zip(own_rows, other_rows, strict=True):
        stack = []
        for o in range(organs):
            owns = jnp.where(organ == o, 1.0, 0.0)
            stack.append(jnp.where(source == o, other_half, 0.0) + owns * own_half)
        stacks.append(jnp.concatenate(stack, axis=0))
    added[...] = times(stacks[0], maps[0][...], maps[1][...]) + exact(stacks[1], maps[2][...])


def start_kernel(
    organs, bands, matches, f0, f1, f2, f3, f4, base, added, a_high, a_low, unit, modes_ref, *refs
):
    near, rest = refs[:bands], refs[bands:]
    message, smoothed_out, jump_out, s0, s1, s2, s3, s4, inner = rest
    faces = (f0, f1, f2, f3, f4)
    smoothed = smoothed_out.ref
    blocks, directions = base.shape[0], base.shape[1]
    for r, face in zip(ORDER, faces, strict=True):
        inner[matches[r]] = base[matches[r]] - face[0:directions, :]
    for f in range(blocks):
        smooth(inner, near, smoothed, f)
        if f == 0:
            send_contact(message.ref, 2, smoothed[0], a_high, a_low, unit)
            message.flush()
    for r, send in enumerate((s0, s1, s2, s3, s4)):
        send(smoothed.at[matches[r]])
    smoothed_out.flush()
    modes = modes_ref.shape[0]
    jump_modes = jump_out.ref
    organ = lax.axis_index("organ")
    jump_modes[...] = jnp.zeros(jump_modes.shape, F32)
    for r, values in zip(ORDER, faces, strict=True):
        face = matches[r]
        for m in range(modes):
            own = modes_ref[m, pl.ds(face, 1), :]
            other = values[directions + m : directions + m + 1, :]
            if r < SUB_ROUNDS:
                own = own - other
            else:
                partner = organ ^ (1 << (r - SUB_ROUNDS))
                jump_modes[face, pl.ds(m * organs + partner, 1), :] = -other
            jump_modes[face, pl.ds(m * organs + organ, 1), :] = own
    for o in range(organs):
        for m in range(modes):
            row = pl.ds(m * organs + o, 1)
            jump_modes[0, row, :] = jump_modes[0, row, :] + added[8 * o + m : 8 * o + m + 1, :]


def residual_contact(arrived, sent, smoothed, right, a_high, a_low, unit, part):
    sent, smoothed, right = sent(), smoothed(), right()
    part[...] = right[...] - smoothed[...]
    part[0] -= contact(sent, arrived, 2, 2, a_high(), a_low(), unit())


def residual_kernel(
    matches, f0, f1, f2, f3, f4, part, a_high, a_low, unit, modes_ref, message, resid, *sends
):
    for r, face in zip(ORDER, (f0, f1, f2, f3, f4), strict=True):
        resid.ref[matches[r]] = part[matches[r]] + face[...]
    send_residual(matches, resid, modes_ref, (a_high, a_low, unit), message, sends)


def send_residual(matches, resid, modes_ref, maps, message, sends):
    for r, send in enumerate(sends):
        send(resid.ref.at[matches[r]])
    resid.flush()
    send_contact(message.ref, 4, resid.ref[0], *maps)
    spread_rows(message.ref, 4, 2, coefficients_row(resid.ref, modes_ref))
    message.flush()


def inner_contact(
    organs, steps, arrived, sent, resid, modes_ref, jump_modes, *refs
):
    rest = list(refs)
    a_high, a_low, unit = (rest.pop(0) for _ in range(3))
    if steps:
        start, behind, jumps, sizes = (
            rest[0],
            *(rest[1 + i * steps : 1 + (i + 1) * steps] for i in range(3)),
        )
        projected, total, direction, jumped, last_size, base, norms = rest[1 + 3 * steps :]
    else:
        projected_out, base, norms = rest
        projected = projected_out.ref
    sent, resid, maps = sent(), resid(), (a_high(), a_low(), unit())
    modes_ref, jump_modes = modes_ref(), jump_modes()
    devices = sent.shape[0] // 4
    subs = devices // organs
    blocks, directions = resid.shape[0], resid.shape[1]
    parts = get(arrived, 4, 2)
    sums = [
        jnp.sum(parts[o * subs : (o + 1) * subs], axis=0, keepdims=True) for o in range(organs)
    ]
    added = contact(sent, arrived, 4, 4, *maps)
    turned = square(jnp.concatenate(sums, axis=0))
    left = jnp.concatenate(
        [turned[m * directions : (m + 1) * directions, :organs] for m in range(8)], axis=1
    )
    organ = lax.axis_index("organ")
    own = sum(jnp.where(organ == o, 1.0, 0.0) * sums[o] for o in range(organs))
    columns = [to_column(own, m * directions, directions) for m in range(modes_ref.shape[0])]
    for f in range(blocks):
        projected[f] = subtract_modes(resid[f], columns, modes_ref, f)
    if not steps:
        projected_out.flush()
    for f in range(blocks):
        value = resid[f] - times_split(left, jump_modes[f])
        base[f] = value + added if f == 0 else value
    norms[...] = jnp.broadcast_to(dots_row([(projected, projected)]), norms.shape)
    if steps:
        start = start()
        behind, jumps, sizes = ([late() for late in group] for group in (behind, jumps, sizes))
        last_size[...] = sizes[-1][...]
        for f in range(blocks):
            value = behind[0][f]
            sum_up = start[f] + sizes[0][2, :, 0:1] * value
            for field, size in zip(behind[1:], sizes[1:], strict=True):
                value = field[f] + size[3, :, 0:1] * value
                sum_up = sum_up + size[2, :, 0:1] * value
            total[f] = sum_up
            direction[f] = value
            value = jumps[0][f]
            for field, size in zip(jumps[1:], sizes[1:], strict=True):
                value = field[f] + size[3, :, 0:1] * value
            jumped[f] = value


def inner_kernel(bands, last, older, matches, f0, f1, f2, f3, f4, base, norms, *refs):
    maps, rest = (None, refs) if last else (refs[:3], refs[3:])
    near, rest = rest[:bands], list(rest[bands:])
    previous = rest.pop(0) if older else None
    message = rest.pop(0)
    if last:
        inner, smoothed = rest
    else:
        inner_out, smoothed_out = rest[:2]
        inner, smoothed = inner_out.ref, smoothed_out.ref
    for r, face in zip(ORDER, (f0, f1, f2, f3, f4), strict=True):
        inner[matches[r]] = base[matches[r]] - face[...]
    if not last:
        inner_out.flush()
    for f in range(inner.shape[0]):
        smooth(inner, near, smoothed, f)
        if f == 0 and not last:
            send_contact(message.ref, 4, smoothed[0], *maps)
    if not last:
        for r, send in enumerate(rest[2:]):
            send(smoothed.at[matches[r]])
        smoothed_out.flush()
    directions = inner.shape[1]
    pairs = [(inner, smoothed)]
    if older:
        pairs.append((previous, smoothed))
    row = dots_row(pairs, directions) + norms[0:1, :]
    if last:
        message.ref[...] = jnp.broadcast_to(row, message.ref.shape)
    else:
        spread_rows(message.ref, 4, 2, row)


def step_sizes(row, older, scalars, directions):
    rho = to_column(row, 0, directions)
    curvature = to_column(row, directions, directions)
    if not older:
        return rho, None, curvature, rho / curvature
    cross = to_column(row, 2 * directions, directions)
    beta = rho / scalars[0, :, 0:1]
    curvature = curvature + beta * (2.0 * cross + beta * scalars[1, :, 0:1])
    return rho, beta, curvature, rho / curvature


def outer_contact(older, arrived, sent, smoothed, projected, *refs):
    rest = list(refs)
    old_image = scalars = None
    if older:
        old_image, scalars = rest[0](), rest[1]()
        rest = rest[2:]
    a_high, a_low, unit, new_scalars, part, steps, image = rest
    sent, smoothed, projected = sent(), smoothed(), projected()
    blocks, directions = smoothed.shape[0], smoothed.shape[1]
    row = jnp.sum(get(arrived, 4, 2), axis=0, keepdims=True)
    rho, beta, curvature, step = step_sizes(row, older, scalars, directions)
    wide = (directions, LANES)
    for place, column in enumerate((rho, curvature, step) + ((beta,) if older else ())):
        new_scalars.ref[place] = jnp.broadcast_to(column, wide)
    new_scalars.flush()
    steps[...] = jnp.broadcast_to(step, wide)
    added = contact(sent, arrived, 4, 4, a_high(), a_low(), unit())
    for f in range(blocks):
        value = smoothed[f]
        if f == 0:
            value = value + added
        if older:
            value = value + beta * old_image[f]
        image[f] = value
        part[f] = projected[f] - step * value


def outer_kernel(older, matches, f0, f1, f2, f3, f4, part, steps, image, *refs):
    a_high, a_low, unit, modes_ref = refs[:4]
    rest = list(refs[4:])
    if older:
        message, resid = rest[:2]
        sends = rest[2:]
    else:
        message, resid, new_image = rest[:3]
        sends = rest[3:]
    step = steps[:, 0:1]
    for r, face in zip(ORDER, (f0, f1, f2, f3, f4), strict=True):
        resid.ref[matches[r]] = part[matches[r]] + step * face[...]
        if not older:
            new_image.ref[matches[r]] = image[matches[r]] - face[...]
    send_residual(matches, resid, modes_ref, (a_high, a_low, unit), message, sends)


def last_kernel(arrived, projected, old_direction, total, scalars, out):
    blocks, directions = projected.shape[0], projected.shape[1]
    row = jnp.sum(arrived[...], axis=0, keepdims=True)
    _, beta, _, step = step_sizes(row, True, scalars, directions)
    for f in range(blocks):
        value = total[f] + step * (projected[f] + beta * old_direction[f])
        for c in range(directions):
            out.ref[c * blocks + f] = value[c : c + 1]


class Late:
    def __init__(self, source, target, sem, priority=0):
        self.target, self.waiting, self.priority = target, True, priority
        self.copy = pltpu.make_async_copy(source, target, sem)

    def start(self):
        self.copy.start(priority=self.priority)

    def __call__(self):
        if self.waiting:
            self.copy.wait()
            self.waiting = False
        return self.target


class Send:
    def __init__(self, target, sem):
        self.target, self.sem, self.copy = target, sem, None

    def __call__(self, source):
        self.copy = pltpu.make_async_copy(source, self.target, self.sem)
        self.copy.start()


class Out:
    def __init__(self, ref, target, sem):
        self.ref = ref
        self.copy = pltpu.make_async_copy(ref, target, sem)
        self.started = False

    def flush(self):
        if not self.started:
            self.copy.start()
            self.started = True


def call(kernel, outs, args, late=(), smem=0, near=(), sends=(), scratch=(), bring=(), held=0, shared=0):
    n_late, n_out, n_arg, n_near = len(late), len(outs), len(args), len(near)
    bring = [item if isinstance(item, tuple) else (item, item.shape, None) for item in bring]
    brought = [(shape, a.dtype) for a, shape, _ in bring]

    def body(*refs):
        refs = list(refs)

        def take(n):
            taken = refs[:n]
            del refs[:n]
            return taken

        given, sources, origins = take(n_arg), take(n_late), take(len(bring))
        targets, ports, close = take(n_out), take(len(sends)), take(n_near)
        goals = take(len(bring))
        buffers, results = take(n_late), take(n_out)
        extra = take(len(scratch))
        in_sem, bring_sem, out_sem = refs
        copies = []
        for i, (origin, goal) in enumerate(zip(origins, goals, strict=True)):
            first = bring[i][2]
            if first is not None:
                rows, columns = goal.shape[1], goal.shape[2]
                origin = origin.at[:, pl.ds(first, rows), pl.ds(first, columns)]
            copies.append(Late(origin, goal, bring_sem.at[i], 0 if i < shared else 1))
        lates = [Late(s, b, in_sem.at[i]) for i, (s, b) in enumerate(zip(sources, buffers))]
        for item in copies[:shared] + lates + copies[shared:]:
            item.start()
        written = [Out(r, t, out_sem.at[i]) for i, (r, t) in enumerate(zip(results, targets))]
        posts = [Send(t, out_sem.at[n_out + i]) for i, t in enumerate(ports)]
        kernel(*given, *lates, *copies[:shared], *written, *posts, *close, *extra)
        for item in lates + copies:
            item()
        for item in written:
            item.flush()
        for item in written + posts:
            item.copy.wait()

    in_specs = [pl.BlockSpec(memory_space=pltpu.SMEM)] * smem
    in_specs += [pl.BlockSpec(memory_space=pltpu.VMEM)] * (n_arg - smem)
    remote = tuple(late) + tuple(a for a, _, _ in bring)
    in_specs += [pl.BlockSpec(memory_space=pltpu.HBM)] * len(remote)
    out_specs = [pl.BlockSpec(memory_space=pltpu.HBM)] * (n_out + len(sends))
    out_specs += [pl.BlockSpec(memory_space=pltpu.VMEM)] * (n_near + len(bring))
    scratch_shapes = [pltpu.SMEM(a.shape, a.dtype) for a in late[:held]]
    scratch_shapes += [pltpu.VMEM(a.shape, a.dtype) for a in late[held:]]
    scratch_shapes += [pltpu.VMEM(shape, kind) for shape, kind in outs]
    scratch_shapes += list(scratch)
    counts = (n_late, len(bring), n_out + len(sends))
    scratch_shapes += [pltpu.SemaphoreType.DMA((max(n, 1),)) for n in counts]
    return pl.pallas_call(
        body,
        out_shape=[pltpu.HBM(shape, kind) for shape, kind in tuple(outs) + tuple(sends)]
        + [pltpu.VMEM(shape, kind) for shape, kind in list(near) + brought],
        in_specs=in_specs,
        out_specs=out_specs,
        scratch_shapes=scratch_shapes,
        compiler_params=pltpu.CompilerParams(vmem_limit_bytes=VMEM_LIMIT),
        cost_estimate=pl.CostEstimate(flops=COST, bytes_accessed=COST, transcendentals=0),
    )(*args, *(pltpu.with_memory_space_constraint(a, pltpu.HBM) for a in remote))


def from_partner(value, axis, apart):
    mask = 2**apart
    pairs = [(source, source ^ mask) for source in range(lax.axis_size(axis))]
    return lax.ppermute(value, axis, pairs)


def exchange(message):
    return lax.all_to_all(message, AXES, split_axis=0, concat_axis=0, tiled=True)


def swap_faces(faces):
    swapped = []
    for r in ORDER:
        axis, apart = ("sub", r) if r < SUB_ROUNDS else ("organ", r - SUB_ROUNDS)
        swapped.append(from_partner(faces[r], axis, apart))
    return swapped


def local(
    dual_rhs, warm_start, inverse_blocks, coarse_basis, mortar_rows, match_rounds, slave_owner,
    slave_dofs, active_set, row_counts,
):
    directions, blocks, length = dual_rhs.shape[0], dual_rhs.shape[3], dual_rhs.shape[4]
    rows = mortar_rows.shape[2]
    modes = coarse_basis.shape[0]
    organs, subs = lax.axis_size("organ"), lax.axis_size("sub")
    devices = organs * subs
    width = CAP * devices
    field = (blocks, directions, length)
    right_rows = dual_rhs.reshape(directions * blocks, 1, length)
    start_rows = warm_start.reshape(directions * blocks, 1, length)
    matrices = inverse_blocks.reshape(blocks, length, length)
    basis = coarse_basis.reshape(modes * blocks, 1, length)
    mortar = mortar_rows.reshape(rows, length)
    matches = match_rounds.reshape(-1)
    owner = slave_owner.reshape(1, rows)
    dofs = slave_dofs.reshape(1, rows)
    active = active_set.reshape(1, rows)
    count = row_counts.reshape(1)
    face = ((directions, length), F32)
    whole = (field, F32)
    message_line = ((4 * devices, LANES), F32)

    sends = [face] * blocks
    near_matrices, first = [], 0
    while first < length:
        rows = min(BAND, length - first)
        near_matrices.append((matrices, (blocks, rows, length - first), first))
        first += rows
    near_matrices = tuple(near_matrices)
    bands = len(near_matrices)

    (setup,) = call(
        functools.partial(setup_kernel, blocks),
        [((devices, LANES), F32)],
        (count,),
        (owner, dofs, active, basis),
        smem=1,
    )
    arrived = exchange(setup)
    a_high, a_low, start, right, products, raw = call(
        functools.partial(slots_kernel, devices),
        [((width, length), BF16)] * 2 + [whole] * 2 + [((32, width), F32), ((8, LANES), F32)],
        (count,),
        (owner, active, mortar, start_rows, right_rows, basis),
        smem=1,
    )
    sent, unit, modes_ref, *faces = call(
        functools.partial(first_kernel, organs),
        [
            message_line,
            ((width, length), BF16),
            ((modes, blocks, length), F32),
        ]
        + [((directions + 8, length), F32)] * blocks,
        (arrived,),
        (matches, basis, start, products, raw),
        held=1,
    )
    maps = (a_high, a_low, unit)
    arrived = exchange(sent)
    faces = swap_faces(faces)
    right, base, added, *more = call(
        functools.partial(start_contact, organs),
        [whole],
        (arrived,),
        (sent, start, right),
        near=[whole, ((8 * organs, length), F32)],
        bring=maps + (modes_ref,) + near_matrices,
        shared=4,
    )
    message, smoothed, jump_modes, *posts = call(
        functools.partial(start_kernel, organs, bands),
        [((2 * devices, LANES), F32), whole, ((blocks, 8 * organs, length), F32)],
        (matches, *faces, base, added, *more),
        smem=1,
        sends=sends,
        scratch=[pltpu.VMEM(field, F32)],
    )
    arrived = exchange(message)
    faces = swap_faces(posts)
    part, *more = call(
        residual_contact,
        [],
        (arrived,),
        (message, smoothed, right),
        near=[whole],
        bring=maps + (modes_ref,),
        shared=3,
    )
    sent, resid, *posts = call(
        residual_kernel,
        [message_line, whole],
        (matches, *faces, part, *more),
        smem=1,
        sends=sends,
    )
    image = None
    size = (4, directions, LANES)
    fields, jumps, scalars = [], [], []
    for step in range(ITERS):
        older, last = step > 0, step == ITERS - 1
        arrived = exchange(sent)
        faces = swap_faces(posts)
        history = (start, *fields, *jumps, *scalars) if last else ()
        more_near = [whole] * 3 + [(size, F32)] if last else []
        ahead = (jumps[-1],) if older and not last else ()
        projected, *more = call(
            functools.partial(inner_contact, organs, step if last else 0),
            [] if last else [whole],
            (arrived,),
            (sent, resid, modes_ref, jump_modes) + (maps if last else ()) + history,
            near=([whole] + more_near if last else []) + [whole, ((8, LANES), F32)],
            bring=(() if last else maps) + near_matrices + ahead,
            shared=0 if last else 3,
        )
        if last:
            total, direction, jumped, last_size, base, norms, *near = more
            (message,) = call(
                functools.partial(inner_kernel, bands, last, older),
                [((devices, LANES), F32)],
                (matches, *faces, base, norms, *near, jumped),
                smem=1,
                scratch=[pltpu.VMEM(field, F32)] * 2,
            )
            arrived = exchange(message)
            break
        message, inner, smoothed, *posts = call(
            functools.partial(inner_kernel, bands, last, older),
            [message_line, whole, whole],
            (matches, *faces, *more),
            smem=1,
            sends=sends,
        )
        arrived = exchange(message)
        faces = swap_faces(posts)
        old = (image, scalars[-1]) if older else ()
        new_scalars, *more = call(
            functools.partial(outer_contact, older),
            [(size, F32)],
            (arrived,),
            (message, smoothed, projected) + old,
            near=[whole, ((directions, LANES), F32), whole],
            bring=maps + (modes_ref,),
            shared=3,
        )
        sent, resid, *posts = call(
            functools.partial(outer_kernel, older),
            [message_line, whole] + ([] if older else [whole]),
            (matches, *faces, *more),
            smem=1,
            sends=sends,
        )
        if not older:
            image, *posts = posts
        fields.append(projected)
        jumps.append(inner)
        scalars.append(new_scalars)
    (result,) = call(
        last_kernel,
        [((directions * blocks, 1, length), F32)],
        (arrived, projected, direction, total, last_size),
    )
    return result.reshape(dual_rhs.shape)


def solution(mesh):
    in_specs = (
        P(None, "organ", "sub", None, None),
        P(None, "organ", "sub", None, None),
        P("organ", "sub", None, None, None),
        P(None, "organ", "sub", None, None),
        P("organ", "sub", None, None),
        P("organ", "sub", None),
        P("organ", "sub", None, None),
        P("organ", "sub", None),
        P("organ", "sub", None),
        P("organ", "sub", None),
    )
    out_specs = P(None, "organ", "sub", None, None)
    return jax.shard_map(local, mesh=mesh, in_specs=in_specs, out_specs=out_specs, check_vma=False)
```
